32 devices in a mesh: group: 4 (over y, x), replica: 8 (over z, core).
Axes of the slice: x: 2, y: 2, z: 4, core: 2. Of those that a mesh axis runs over, the one named last changes fastest.
Arguments:
- latents: bfloat16 [64, 256, 384], P(('group', 'replica')), may hold values from -6 to 6
- condition: float32 [64, 384], P(('group', 'replica')), may hold values from -6 to 6
- cotangent: bfloat16 [64, 256, 384], P(('group', 'replica')), may hold values from -6 to 6
- live_counts: int32 [32], P(('group', 'replica')), may hold values from 1 to 2, 41 in all
- modulation: bfloat16 [384, 2304], P('group'), may hold values from -0.3125 to 0.3125
- attending: bfloat16 [384, 1152], P('group'), may hold values from -0.3125 to 0.3125
- projection: bfloat16 [384, 384], P('group'), may hold values from -1.25 to 1.25
- expand: bfloat16 [384, 1536], P(None, 'group'), may hold values from -0.3125 to 0.3125
- contract: bfloat16 [1536, 384], P('group'), may hold values from -0.15625 to 0.15625
- biases: bfloat16 [14, 384], P(None, 'group'), may hold values from -1.1953125 to 1.1953125
- modulation_mean: bfloat16 [384, 2304], P('group'), may hold values from -20 to 20
- attending_mean: bfloat16 [384, 1152], P('group'), may hold values from -20 to 20
- projection_mean: bfloat16 [384, 384], P('group'), may hold values from -10 to 10
- expand_mean: bfloat16 [384, 1536], P(None, 'group'), may hold values from -12 to 12
- contract_mean: bfloat16 [1536, 384], P('group'), may hold values from -32 to 32
- biases_mean: bfloat16 [14, 384], P(None, 'group'), may hold values from -20 to 20
- modulation_square: bfloat16 [384, 2304], P('group'), may hold values from 0.47070312 to 7.53125
- attending_square: bfloat16 [384, 1152], P('group'), may hold values from 0.47070312 to 7.53125
- projection_square: bfloat16 [384, 384], P('group'), may hold values from 0.11767578 to 1.8828125
- expand_square: bfloat16 [384, 1536], P(None, 'group'), may hold values from 0.16992188 to 2.71875
- contract_square: bfloat16 [1536, 384], P('group'), may hold values from 1.0625 to 17
- biases_square: bfloat16 [14, 384], P(None, 'group'), may hold values from 0.47070312 to 7.53125
Outputs:
- out_latents: bfloat16 [64, 256, 384], P(('group', 'replica'))
- grad_latents: bfloat16 [64, 256, 384], P(('group', 'replica'))
- grad_condition: float32 [64, 384], P(('group', 'replica'))
- modulation_updated: float32 [384, 2304], P('group')
- attending_updated: float32 [384, 1152], P('group')
- projection_updated: float32 [384, 384], P('group')
- expand_updated: float32 [384, 1536], P(None, 'group')
- contract_updated: float32 [1536, 384], P('group')
- biases_updated: float32 [14, 384], P(None, 'group')
- modulation_momentum: float32 [384, 2304], P('group')
- attending_momentum: float32 [384, 1152], P('group')
- projection_momentum: float32 [384, 384], P('group')
- expand_momentum: float32 [384, 1536], P(None, 'group')
- contract_momentum: float32 [1536, 384], P('group')
- biases_momentum: float32 [14, 384], P(None, 'group')
- modulation_variance: float32 [384, 2304], P('group')
- attending_variance: float32 [384, 1152], P('group')
- projection_variance: float32 [384, 384], P('group')
- expand_variance: float32 [384, 1536], P(None, 'group')
- contract_variance: float32 [1536, 384], P('group')
- biases_variance: float32 [14, 384], P(None, 'group')
The draws below stay inside these ranges and needn't reach their ends.
Inputs may be any that keep to these rules, and one draw needn't show every extreme that they name: A device's first live_counts slots are live, the rest are not; the entries add up to 41 and some device has all 2 slots live.
All inputs are finite; a program needn't handle non-finite values.
Results may differ from the reference program's by a relative error of at most 0.019.
Values may be sent and summed in bfloat16 or wider, within the bound.
No kernel may reach another device: no remote copies, remote signals or barrier semaphores. Data moves between devices by JAX's collectives and lax.ppermute only.
A program may use at most 128 MiB of HBM per device.

```python
import math
import jax
import jax.numpy as jnp
import numpy as np
from jax import lax

D = 384
HEADS = 6
HEAD_DIM = 64
FF = 1536
SEQ = 256
SLOTS = 2
STEP = 10
SLOT_ROWS = 64
LATENTS = 41
BIAS_ROWS = 14
N_GROUP = 4
N_REPLICA = 8


def steps_of(stream_key, extent, cuts, least, high):
    def one(axis_at, blocks):
        draws = jax.random.uniform(jax.random.fold_in(jax.random.fold_in(stream_key, 6), axis_at), (blocks,), jnp.float32, least / len(cuts), high / len(cuts))
        return jnp.repeat(jnp.exp(draws), extent[axis_at] // blocks).reshape((-1,) + (1,) * (len(extent) - axis_at - 1))

    level = one(*cuts[0])
    for cut in cuts[1:]:
        level = level * one(*cut)
    return level


def length_profile(number_of, total, limit, skew):
    loads = [(1 << 20) // math.isqrt(grade ** skew) + 1 for grade in range(2, number_of + 1)]
    spare, counts = total - limit - (number_of - 1), [1] * (number_of - 1)
    while spare > 0:
        movable = [i for i in range(number_of - 1) if counts[i] < limit]
        pool, budget = sum([loads[i] for i in movable]), spare
        for i in movable:
            addition = min(limit - counts[i], max(1, budget * loads[i] // pool), spare)
            counts[i] = counts[i] + addition
            spare = spare - addition
    return np.array([limit] + counts)


def ragged(stream_key, count, total, limit, slope):
    if count == 2:
        one = jax.random.randint(stream_key, (), max(1, total - limit), min(limit, total - 1) + 1)
        return jnp.stack([one, total - one])
    lengths = jnp.asarray(length_profile(count, total, limit, slope), jnp.int32)
    couples = (count - 1) // 2
    giver, sink = lengths[1:1 + 2 * couples:2], lengths[2:2 + 2 * couples:2]
    margin = jnp.minimum(giver - 1, limit - sink)
    shifted = jax.random.randint(jax.random.fold_in(stream_key, 1), (couples,), 0, 1 << 20) % (margin + 1)
    lengths = lengths.at[1:1 + 2 * couples:2].set(giver - shifted).at[2:2 + 2 * couples:2].set(sink + shifted)
    return lengths[jax.random.permutation(jax.random.fold_in(stream_key, 2), count)]


def normal_values(rng, shape, width, reach, cuts=(), held_as=jnp.bfloat16):
    array = width * jax.random.normal(rng, shape, jnp.float32)
    if cuts:
        array = array * steps_of(rng, shape, cuts, -0.22, 0.18)
    return jnp.clip(array, -reach, reach).astype(held_as)


def setup_inputs(seed: int = 0) -> dict:
    seeds = jax.random.split(jax.random.key(seed), 23)
    return {
        "latents": normal_values(seeds[0], (SLOT_ROWS, SEQ, D), 1.0, 6.0, ((0, 32),)),
        "condition": normal_values(seeds[1], (SLOT_ROWS, D), 1.0, 6.0, ((0, 32),), jnp.float32),
        "cotangent": normal_values(seeds[2], (SLOT_ROWS, SEQ, D), 1.0, 6.0, ((0, 32),)),
        "live_counts": ragged(seeds[3], N_GROUP * N_REPLICA, LATENTS, SLOTS, 2).astype(jnp.int32),
        "modulation": normal_values(seeds[4], (D, 6 * D), D ** -0.5, 0.3125, ((0, 4),)),
        "attending": normal_values(seeds[5], (D, 3 * D), D ** -0.5, 0.3125, ((0, 4),)),
        "projection": normal_values(seeds[6], (D, D), (D * 16 // SEQ) ** -0.5, 1.25, ((0, 4),)),
        "expand": normal_values(seeds[7], (D, FF), D ** -0.5, 0.3125, ((1, 4),)),
        "contract": normal_values(seeds[8], (FF, D), FF ** -0.5, 0.15625, ((0, 4),)),
        "biases": normal_values(seeds[9], (BIAS_ROWS, D), 0.2, 1.1953125, ((1, 4),)),
        "modulation_mean": normal_values(seeds[10], (D, 6 * D), (0.0333 * (LATENTS * SEQ) ** 0.5), 20.0, ((0, 4),)),
        "attending_mean": normal_values(seeds[11], (D, 3 * D), (0.0333 * (LATENTS * SEQ) ** 0.5), 20.0, ((0, 4),)),
        "projection_mean": normal_values(seeds[12], (D, D), (0.01665 * (LATENTS * SEQ) ** 0.5), 10.0, ((0, 4),)),
        "expand_mean": normal_values(seeds[13], (D, FF), (0.02 * (LATENTS * SEQ) ** 0.5), 12.0, ((1, 4),)),
        "contract_mean": normal_values(seeds[14], (FF, D), (0.05 * (LATENTS * SEQ) ** 0.5), 32.0, ((0, 4),)),
        "biases_mean": normal_values(seeds[15], (BIAS_ROWS, D), (0.0333 * (LATENTS * SEQ) ** 0.5), 20.0, ((1, 4),)),
        "modulation_square": jnp.clip(jnp.exp(math.log(7.53125) - 2.7725887 * jax.random.uniform(seeds[16], (D, 6 * D), jnp.float32) ** steps_of(seeds[16], (D, 6 * D), ((0, 4),), -0.2, 0.2)), 0.47070312, 7.53125).astype(jnp.bfloat16),
        "attending_square": jnp.clip(jnp.exp(math.log(7.53125) - 2.7725887 * jax.random.uniform(seeds[17], (D, 3 * D), jnp.float32) ** steps_of(seeds[17], (D, 3 * D), ((0, 4),), -0.2, 0.2)), 0.47070312, 7.53125).astype(jnp.bfloat16),
        "projection_square": jnp.clip(jnp.exp(math.log(1.8828125) - 2.7725887 * jax.random.uniform(seeds[18], (D, D), jnp.float32) ** steps_of(seeds[18], (D, D), ((0, 4),), -0.2, 0.2)), 0.11767578, 1.8828125).astype(jnp.bfloat16),
        "expand_square": jnp.clip(jnp.exp(math.log(2.71875) - 2.7725887 * jax.random.uniform(seeds[19], (D, FF), jnp.float32) ** steps_of(seeds[19], (D, FF), ((1, 4),), -0.2, 0.2)), 0.16992188, 2.71875).astype(jnp.bfloat16),
        "contract_square": jnp.clip(jnp.exp(math.log(17.0) - 2.7725887 * jax.random.uniform(seeds[20], (FF, D), jnp.float32) ** steps_of(seeds[20], (FF, D), ((0, 4),), -0.2, 0.2)), 1.0625, 17.0).astype(jnp.bfloat16),
        "biases_square": jnp.clip(jnp.exp(math.log(7.53125) - 2.7725887 * jax.random.uniform(seeds[21], (BIAS_ROWS, D), jnp.float32) ** steps_of(seeds[21], (BIAS_ROWS, D), ((1, 4),), -0.2, 0.2)), 0.47070312, 7.53125).astype(jnp.bfloat16),
    }


@jax.custom_vjp
def low(v):
    return lax.optimization_barrier(v.astype(jnp.bfloat16)).astype(jnp.float32)

@jax.custom_vjp
def low_back(v):
    return v

def low_keep(v):
    return (low(v), None)

def low_pass(kept, grad):
    return (grad,)

def back_keep(v):
    return (v, None)

def back_low(kept, grad):
    return (low(grad),)
low.defvjp(low_keep, low_pass)
low_back.defvjp(back_keep, back_low)
NORM_EPS = 1e-06
ADAM_EPS = 1e-08
BETA_FIRST = 0.9
BETA_SECOND = 0.999
DECAY_RATE = 0.1
LEARN_RATES = (0.05, 0.05, 0.2, 0.05, 0.025, 0.1)
DECAY_FLAGS = (1.0, 1.0, 1.0, 1.0, 1.0, 0.0)
HIGH = lax.Precision.HIGHEST

def layer_norm(values):
    centred = values - lax.optimization_barrier(jnp.mean(values, axis=-1, keepdims=True))
    return centred * lax.rsqrt(lax.optimization_barrier(jnp.mean(centred * centred, axis=-1, keepdims=True)) + NORM_EPS)

def block_forward(params, tokens, condition):
    modulation, attending, projection, expand, contract, biases = params
    batch_size, length, model_width = tokens.shape
    hidden_rows = FF // model_width
    head_scale = HEAD_DIM ** (-0.5)
    mod_bias = biases[0:6].reshape(6 * model_width)
    joined_bias = jnp.concatenate([biases[6], jnp.zeros_like(biases[6]), biases[7]])
    proj_bias = biases[8]
    expand_bias = biases[9:9 + hidden_rows].reshape(FF)
    contract_bias = biases[9 + hidden_rows]
    cond_low = low(jax.nn.silu(condition))
    modulated = low_back(jnp.dot(cond_low, modulation, precision=HIGH) + mod_bias)
    pieces = modulated.reshape(batch_size, 6, 1, model_width)
    first_in = low(layer_norm(tokens) * (1.0 + pieces[:, 1]) + pieces[:, 0])
    joined = jnp.einsum('bld,de->ble', first_in, attending, precision=HIGH) + joined_bias
    joined = low(low_back(joined)).reshape(batch_size, length, 3, HEADS, HEAD_DIM)
    query_vectors = joined[:, :, 0]
    key_vectors = joined[:, :, 1]
    value_vectors = joined[:, :, 2]
    scores = jnp.einsum('bqhe,bkhe->bhqk', query_vectors, key_vectors, precision=HIGH) * head_scale
    scores = low_back(scores)
    attention_weights = low(jax.nn.softmax(scores, axis=-1))
    mixed_heads = jnp.einsum('bhqk,bkhe->bqhe', attention_weights, value_vectors, precision=HIGH)
    mixed_heads = low(low_back(mixed_heads.reshape(batch_size, length, model_width)))
    branch = low_back(jnp.einsum('bld,de->ble', mixed_heads, projection, precision=HIGH) + proj_bias)
    middle = tokens + pieces[:, 2] * branch
    second_in = low(layer_norm(middle) * (1.0 + pieces[:, 4]) + pieces[:, 3])
    before = low_back(jnp.einsum('bld,df->blf', second_in, expand, precision=HIGH) + expand_bias)
    activated = low(jax.nn.gelu(before, approximate=True))
    feed_out = low_back(jnp.einsum('blf,fd->bld', activated, contract, precision=HIGH) + contract_bias)
    return middle + pieces[:, 5] * feed_out

def adam_update(weight, gradient, mean_old, square_old, step_rate, decay_flag):
    momentum = BETA_FIRST * mean_old + (1.0 - BETA_FIRST) * gradient
    variance = BETA_SECOND * square_old + (1.0 - BETA_SECOND) * gradient * gradient
    mean_hat = momentum / (1.0 - BETA_FIRST ** STEP)
    square_hat = variance / (1.0 - BETA_SECOND ** STEP)
    updated = weight - step_rate * (mean_hat / (jnp.sqrt(square_hat) + ADAM_EPS) + decay_flag * DECAY_RATE * weight)
    return (updated, momentum, variance)

def reference(latents, condition, cotangent, live_counts, modulation, attending, projection, expand, contract, biases, modulation_mean, attending_mean, projection_mean, expand_mean, contract_mean, biases_mean, modulation_square, attending_square, projection_square, expand_square, contract_square, biases_square):
    total_slots = latents.shape[0]
    slot_number = jnp.arange(total_slots, dtype=jnp.int32) % SLOTS
    live_mask = (slot_number < jnp.repeat(live_counts, SLOTS)).astype(jnp.float32)
    stored = (modulation, attending, projection, expand, contract, biases)
    params = tuple((weight_item.astype(jnp.float32) for weight_item in stored))
    grad_out = cotangent.astype(jnp.float32) * live_mask[:, None, None]
    block_size = math.gcd(total_slots, max(1, 4096 // SEQ))
    block_count = total_slots // block_size

    def one_block(summed, inputs):
        tokens, cond_block, back_block = inputs
        outputs, pullback = jax.vjp(block_forward, params, tokens, cond_block)
        param_grads, token_grads, cond_grads = pullback(back_block)
        summed = tuple((running + addend for running, addend in zip(summed, param_grads)))
        return (summed, (outputs, token_grads, cond_grads))
    initial = tuple((jnp.zeros_like(weight_item) for weight_item in params))
    blocked = (latents.astype(jnp.float32).reshape(block_count, block_size, SEQ, D), condition.reshape(block_count, block_size, D), grad_out.reshape(block_count, block_size, SEQ, D))
    summed, (outputs, token_grads, cond_grads) = lax.scan(one_block, initial, blocked)
    out_latents = (outputs.reshape(total_slots, SEQ, D) * live_mask[:, None, None]).astype(jnp.bfloat16)
    grad_latents = token_grads.reshape(total_slots, SEQ, D).astype(jnp.bfloat16)
    grad_condition = cond_grads.reshape(total_slots, D)
    means = (modulation_mean, attending_mean, projection_mean, expand_mean, contract_mean, biases_mean)
    squares = (modulation_square, attending_square, projection_square, expand_square, contract_square, biases_square)
    results = [adam_update(params[kind], summed[kind], means[kind].astype(jnp.float32), squares[kind].astype(jnp.float32), LEARN_RATES[kind], DECAY_FLAGS[kind]) for kind in range(6)]
    return (out_latents, grad_latents, grad_condition, results[0][0], results[1][0], results[2][0], results[3][0], results[4][0], results[5][0], results[0][1], results[1][1], results[2][1], results[3][1], results[4][1], results[5][1], results[0][2], results[1][2], results[2][2], results[3][2], results[4][2], results[5][2])
```

```python
import functools

import jax
import jax.numpy as jnp
from jax import lax
from jax.experimental import pallas as pl
from jax.experimental.pallas import tpu as pltpu
from jax.sharding import PartitionSpec as P

HEADS = 6
HEAD_DIM = 64
FF = 1536
STEP = 10


NORM_EPS = 1e-06
ADAM_EPS = 1e-08
BETA_FIRST = 0.9
BETA_SECOND = 0.999
DECAY_RATE = 0.1
LEARN_RATES = (0.05, 0.05, 0.2, 0.05, 0.025, 0.1)
DECAY_FLAGS = (1.0, 1.0, 1.0, 1.0, 1.0, 0.0)
GELU_COEF = 0.7978845608028654
BIAS_ROWS = 14
D = 384
SEQ = 256
QUARTER = D // 4
VMEM_BYTES = 48 * 1024 * 1024
LOW = jnp.bfloat16
SMALL = 32
WIDE = jnp.float32


def dot_plain(left_side, right_side):
    return jnp.dot(left_side, right_side, preferred_element_type=WIDE)


def dot_first(left_side, right_side):
    return lax.dot_general(
        left_side, right_side, (((0,), (0,)), ((), ())), preferred_element_type=WIDE
    )


def dot_last(left_side, right_side):
    return lax.dot_general(
        left_side, right_side, (((1,), (1,)), ((), ())), preferred_element_type=WIDE
    )


def adam_update(weight, gradient, mean_old, square_old, step_rate, decay_flag):
    momentum = BETA_FIRST * mean_old + (1.0 - BETA_FIRST) * gradient
    variance = BETA_SECOND * square_old + (1.0 - BETA_SECOND) * gradient * gradient
    mean_hat = momentum / (1.0 - BETA_FIRST**STEP)
    square_hat = variance / (1.0 - BETA_SECOND**STEP)
    updated = weight - step_rate * (
        mean_hat / (jnp.sqrt(square_hat) + ADAM_EPS) + decay_flag * DECAY_RATE * weight
    )
    return (updated, momentum, variance)


def replica_stages(count):
    stages, low_bit = [(0, 2)], 1
    while (1 << low_bit) < count:
        radix = min(4, count >> low_bit)
        stages.append((low_bit, radix))
        low_bit += radix.bit_length() - 1
    return stages


def swap_group(value, k):
    if k == 0:
        return value
    return lax.ppermute(value, "group", [(i, i ^ k) for i in range(lax.axis_size("group"))])


def swap_replica(value, k):
    if k == 0:
        return value
    return lax.ppermute(value, "replica", [(i, i ^ k) for i in range(lax.axis_size("replica"))])


def pick(blocks, index):
    return lax.dynamic_index_in_dim(blocks, index, axis=0, keepdims=False)


def in_order(blocks, digit):
    ordered = []
    for place in range(len(blocks)):
        chosen = blocks[0]
        for k in range(1, len(blocks)):
            chosen = jnp.where((digit ^ k) == place, blocks[k], chosen)
        ordered.append(chosen)
    return jnp.stack(ordered)


def wide_sum(blocks):
    total = blocks[0].astype(jnp.float32)
    for block in blocks[1:]:
        total = total + block.astype(jnp.float32)
    return total


def scatter_stage(value, digit, low_bit, radix):
    rows = value.shape[-2] // radix
    parts = [
        lax.dynamic_slice_in_dim(value, (digit ^ k) * rows, rows, value.ndim - 2)
        for k in range(radix)
    ]
    received = [swap_replica(parts[k], k << low_bit) for k in range(radix)]
    return wide_sum(received).astype(jnp.bfloat16)


def reduce_replicas(value, copy, stages):
    core = copy % 2
    for low_bit, radix in stages[1:]:
        value = scatter_stage(value, (copy >> low_bit) % radix, low_bit, radix)
    for low_bit, radix in reversed(stages[1:]):
        blocks = [swap_replica(value, k << low_bit) for k in range(radix)]
        value = in_order(blocks, (copy >> low_bit) % radix)
        value = value.reshape(-1, value.shape[-1])
    other = swap_replica(value, 1)
    return (
        jnp.where(core == 0, value, other).astype(jnp.float32),
        jnp.where(core == 0, other, value).astype(jnp.float32),
    )


def layer_norm_parts(values):
    centred = values - jnp.mean(values, axis=-1, keepdims=True)
    inverse = lax.rsqrt(jnp.mean(centred * centred, axis=-1, keepdims=True) + NORM_EPS)
    return (centred * inverse, inverse)


def norm_backward(grad_normed, normed, inverse):
    mean_grad = jnp.mean(grad_normed, axis=-1, keepdims=True)
    mean_cross = jnp.mean(grad_normed * normed, axis=-1, keepdims=True)
    return inverse * (grad_normed - mean_grad - normed * mean_cross)


def column_sum(values):
    return jnp.sum(values, axis=0, keepdims=True)


def head_mask(shape, which):
    lane = lax.broadcasted_iota(jnp.int32, shape, 1)
    return (lane < HEAD_DIM) if which == 0 else (lane >= HEAD_DIM)


def place_rows(target, lanes, block, owner):
    start = pl.multiple_of(owner * QUARTER, 32)
    target[pl.ds(start, QUARTER), lanes] = block


def neighbours(where):
    rank, core = where[0], where[1]
    return (rank ^ (1 + core), rank ^ (2 - core), rank ^ 3)


def payload_kernel(where, condition, attending, projection, biases, out):
    @pl.when(where[1] == 0)
    def _():
        out[0:QUARTER, :] = attending[:, 0:D]
        out[QUARTER : 2 * QUARTER, :] = attending[:, D : 2 * D]

    @pl.when(where[1] != 0)
    def _():
        out[0:QUARTER, :] = attending[:, 2 * D : 3 * D]
        out[QUARTER : 2 * QUARTER, :] = projection[...]

    cond = condition[...]
    active = cond / (1.0 + jnp.exp(-cond))
    padded = jnp.concatenate(
        [biases[...].astype(WIDE), jnp.zeros((BIAS_ROWS, D - QUARTER), WIDE)], axis=1
    )
    out[2 * QUARTER :, :] = jnp.concatenate([active, padded], axis=0).astype(LOW)


def modulation_kernel(
    where, own, first, second, last, weight, expand, contract, stay, go, bias_out, feed_part
):
    rank = where[0]
    owners = (rank,) + neighbours(where)
    rows = [block[...].astype(WIDE) for block in (own, first, second, last)]
    conds = jnp.concatenate([rows[0][0:2], rows[2][0:2], rows[1][0:2], rows[3][0:2]], axis=0)
    columns = conds[:, :QUARTER]
    for place in range(1, 4):
        lanes = slice(place * QUARTER, (place + 1) * QUARTER)
        columns = jnp.where(rank == place, conds[:, lanes], columns)
    partial = dot_plain(columns.astype(LOW), weight[...])
    stay[...] = partial[:4]
    go[...] = partial[4:]
    lanes = []
    for place in range(4):
        chosen = rows[0][:, :QUARTER]
        for k in range(1, 4):
            chosen = jnp.where(owners[k] == place, rows[k][:, :QUARTER], chosen)
        lanes.append(chosen)
    bias_out[...] = jnp.concatenate(lanes, axis=1)

    @pl.when(where[1] == 0)
    def _():
        feed_part[...] = expand[...]

    @pl.when(where[1] != 0)
    def _():
        feed_part[...] = contract[...]


def attention_forward_kernel(
    where, tokens, stay, arrived, bias, own_att, own_proj, n1, n2, n3, f1, f2, f3,
    joined_out, soft_out, mixed_out, mod_out, att, proj,
):
    slot = pl.program_id(0)
    rank = where[0]

    core = where[1]

    def assemble(lows, highs):
        for k, block in zip((1, 2, 3), lows):
            place_rows(att, slice(0, D), block[0:QUARTER, :], rank ^ k)
            place_rows(att, slice(D, 2 * D), block[QUARTER : 2 * QUARTER, :], rank ^ k)
        for k, block in zip((2, 1, 3), highs):
            place_rows(att, slice(2 * D, 3 * D), block[0:QUARTER, :], rank ^ k)
            place_rows(proj, slice(0, D), block[QUARTER : 2 * QUARTER, :], rank ^ k)

    @pl.when(slot == 0)
    def _():
        place_rows(att, slice(0, 3 * D), own_att[...], rank)
        place_rows(proj, slice(0, D), own_proj[...], rank)

        @pl.when(core == 0)
        def _():
            assemble((n1, n2, n3), (f1, f2, f3))

        @pl.when(core != 0)
        def _():
            assemble((f1, f2, f3), (n1, n2, n3))

    summed = stay[0:2, :] + arrived[...]
    row = jnp.where(slot == 0, summed[0:1], summed[1:2])
    pieces = [row[:, j * D : (j + 1) * D] + bias[2 + j : 3 + j, :] for j in range(6)]
    mod_out[0] = jnp.concatenate(pieces, axis=0)
    normed, _ = layer_norm_parts(tokens[0].astype(WIDE))
    first_in = (normed * (1.0 + pieces[1]) + pieces[0]).astype(LOW)
    thirds = []
    for third in range(3):
        part = dot_plain(first_in, att[:, third * D : (third + 1) * D])
        if third == 0:
            part = part + bias[8:9, :]
        if third == 2:
            part = part + bias[9:10, :]
        part = part.astype(LOW)
        joined_out[0, :, third * D : (third + 1) * D] = part
        thirds.append(part)
    first_half = head_mask((SEQ, 128), 0)
    scale = jnp.asarray(HEAD_DIM ** (-0.5), LOW)
    zero = jnp.zeros((SEQ, 128), LOW)
    for pair in range(HEADS // 2):
        lanes = slice(pair * 128, (pair + 1) * 128)
        query, key, value = (part[:, lanes] for part in thirds)
        query = query * scale
        outs = []
        for half in range(2):
            masked = (
                jnp.where(first_half, query, zero)
                if half == 0
                else jnp.where(first_half, zero, query)
            )
            scores = dot_last(masked, key)
            weights = jnp.exp(scores - jnp.max(scores, axis=-1, keepdims=True))
            total = jnp.sum(weights, axis=-1, keepdims=True)
            soft = (weights * (1.0 / total)).astype(LOW)
            soft_out[0, 2 * pair + half] = soft
            outs.append(dot_plain(soft, value))
        mixed_out[0, :, lanes] = jnp.where(first_half, outs[0], outs[1]).astype(LOW)


def feed_kernel(
    where, mixed, tokens, cotangent, mod, bias, proj, own_expand, own_contract, n1, n2, n3, f1, f2, f3,
    out, grad_middle_out, send_out, keep_out, rows_out,
    expands, contracts, branch, middle, second, normed, inverse, grad_feed, feed, grad_second,
):
    step = pl.program_id(0)
    rank, core, live = where[0], where[1], where[3]

    def assemble(lows, highs):
        for k, block in zip((1, 2, 3), lows):
            expands[k] = block[...]
        for k, block in zip((2, 1, 3), highs):
            contracts[k] = block[...]

    slots = [slice(s * SEQ, (s + 1) * SEQ) for s in range(2)]

    @pl.when(step == 0)
    def _():
        expands[0] = own_expand[...]
        contracts[0] = own_contract[...]

        @pl.when(core == 0)
        def _():
            assemble((n1, n2, n3), (f1, f2, f3))

        @pl.when(core != 0)
        def _():
            assemble((f1, f2, f3), (n1, n2, n3))

        for s, rows in enumerate(slots):
            pieces = mod[s]
            value = dot_plain(mixed[s], proj[...]) + bias[10:11, :]
            branch[rows, :] = value
            centre = tokens[s].astype(WIDE) + pieces[2:3] * value
            middle[rows, :] = centre
            unit, spread = layer_norm_parts(centre)
            normed[rows, :] = unit
            inverse[rows, :] = jnp.broadcast_to(spread, (SEQ, 128))
            second[rows, :] = (unit * (1.0 + pieces[4:5]) + pieces[3:4]).astype(LOW)
            alive = jnp.where(s < live, 1.0, 0.0)
            grad_feed[rows, :] = (
                pieces[5:6] * (cotangent[s].astype(WIDE) * alive)
            ).astype(LOW)
        rows_out[...] = jnp.zeros_like(rows_out)
        rows_out[12:13, :] = column_sum(grad_feed[...].astype(WIDE))

    hidden_bias = bias[pl.ds(11 + (rank ^ step), 1), :]
    expand, contract = expands[step], contracts[step]
    before = dot_plain(second[...], expand) + hidden_bias
    square = before * before
    tangent = jnp.tanh(before * (GELU_COEF + (GELU_COEF * 0.044715) * square))
    half_up = 0.5 + 0.5 * tangent
    activated = (before * half_up).astype(LOW)
    slope = half_up + (0.5 * before) * (1.0 - tangent * tangent) * (
        GELU_COEF + (GELU_COEF * 3.0 * 0.044715) * square
    )
    grad_before_wide = dot_last(grad_feed[...], contract) * slope
    grad_before = grad_before_wide.astype(LOW)
    feed_term = dot_plain(activated, contract)
    second_term = dot_last(grad_before, expand)
    grad_expand = dot_first(second[...], grad_before).astype(LOW)
    grad_contract = dot_first(activated, grad_feed[...]).astype(LOW)
    rows_out[pl.ds(8 + (rank ^ step), 1), :] = column_sum(grad_before.astype(WIDE))

    @pl.when(core == 0)
    def _():
        send_out[0] = grad_contract
        keep_out[0] = grad_expand

    @pl.when(core != 0)
    def _():
        send_out[0] = grad_expand
        keep_out[0] = grad_contract

    @pl.when(step == 0)
    def _():
        feed[...] = feed_term
        grad_second[...] = second_term

    @pl.when(step > 0)
    def _():
        feed[...] += feed_term
        grad_second[...] += second_term

    @pl.when(step == 3)
    def _():
        for s, rows in enumerate(slots):
            pieces = mod[s]
            alive = jnp.where(s < live, 1.0, 0.0)
            feed_out = feed[rows, :] + bias[15:16, :]
            grad_out = cotangent[s].astype(WIDE) * alive
            out[s] = ((middle[rows, :] + pieces[5:6] * feed_out) * alive).astype(LOW)
            grad = grad_second[rows, :]
            unit = normed[rows, :]
            grad_middle = grad_out + norm_backward(
                grad * (1.0 + pieces[4:5]), unit, inverse[rows, 0:1]
            )
            grad_middle_out[s] = grad_middle
            rows_out[4 * s : 4 * s + 1, :] = column_sum(grad_middle * branch[rows, :])
            rows_out[4 * s + 1 : 4 * s + 2, :] = column_sum(grad)
            rows_out[4 * s + 2 : 4 * s + 3, :] = column_sum(grad * unit)
            rows_out[4 * s + 3 : 4 * s + 4, :] = column_sum(grad_out * feed_out)


def attention_backward_kernel(
    slot, where, tokens, grad_middle_in, joined, soft_in, mixed, mod, feed_rows, cond, att, proj, *refs
):
    rank, core = where[0], where[1]
    if slot == 0:
        grad_tokens_out, grad_att, grad_proj, rows, grad_joined = refs
    else:
        before_att, before_proj, before_rows, _, _ = refs[:5]
        grad_tokens_out, send_out, keep_out, rows_out = refs[5:9]
        grad_joined, grad_att, grad_proj, rows = refs[9:]

    if slot == 0:
        rows[...] = jnp.zeros_like(rows)
        rows[12:14, :] = cond[...]
        rows[17:22, :] = feed_rows[8:13, :]
    else:
        rows[...] = before_rows[...]

    pieces = mod[0]
    grad_middle = grad_middle_in[0]
    grad_branch = (pieces[2:3] * grad_middle).astype(LOW)
    rows[16:17, :] += column_sum(grad_branch.astype(WIDE))
    proj_term = dot_first(mixed[0], grad_branch)
    grad_proj[...] = proj_term if slot == 0 else before_proj[...] + proj_term
    grad_mixed = dot_last(grad_branch, proj[...]).astype(LOW)
    first_half = head_mask((SEQ, 128), 0)
    zero = jnp.zeros((SEQ, 128), LOW)
    scale = HEAD_DIM ** (-0.5)
    for pair in range(HEADS // 2):
        lanes = slice(pair * 128, (pair + 1) * 128)
        query = joined[0, :, pair * 128 : (pair + 1) * 128]
        key = joined[0, :, D + pair * 128 : D + (pair + 1) * 128]
        value = joined[0, :, 2 * D + pair * 128 : 2 * D + (pair + 1) * 128]
        grads = grad_mixed[:, lanes]
        results = []
        for half in range(2):
            soft = soft_in[0, 2 * pair + half]
            masked = (
                jnp.where(first_half, grads, zero)
                if half == 0
                else jnp.where(first_half, zero, grads)
            )
            grad_soft = dot_last(masked, value)
            grad_values = dot_first(soft, grads)
            soft_wide = soft.astype(WIDE)
            weighted = soft_wide * grad_soft
            inner = jnp.sum(weighted, axis=-1, keepdims=True)
            grad_scores = (weighted - soft_wide * inner).astype(LOW)
            results.append(
                (dot_plain(grad_scores, key), dot_first(grad_scores, query), grad_values)
            )
        for third in range(3):
            merged = jnp.where(first_half, results[0][third], results[1][third])
            if third < 2:
                merged = merged * scale
            grad_joined[:, third * D + pair * 128 : third * D + (pair + 1) * 128] = merged.astype(LOW)
    grads = grad_joined[...]
    sums = column_sum(grads.astype(WIDE))
    rows[14:15, :] += sums[:, :D]
    rows[15:16, :] += sums[:, 2 * D :]
    normed, inverse = layer_norm_parts(tokens[0].astype(WIDE))
    first_in = (normed * (1.0 + pieces[1:2]) + pieces[0:1]).astype(LOW)
    att_term = dot_first(first_in, grads)
    grad_att[...] = att_term if slot == 0 else before_att[...] + att_term
    grad_first = dot_last(grads, att[...])
    grad_tokens_out[0] = (
        grad_middle + norm_backward(grad_first * (1.0 + pieces[1:2]), normed, inverse)
    ).astype(LOW)
    own_rows = jnp.concatenate(
        [
            column_sum(grad_first),
            column_sum(grad_first * normed),
        ],
        axis=0,
    )

    rows[6 * slot : 6 * slot + 2, :] = own_rows
    rows[6 * slot + 2 : 6 * slot + 6, :] = feed_rows[4 * slot : 4 * slot + 4, :]
    if slot == 0:
        return
    rows_out[...] = rows[...].astype(LOW)
    for k in range(4):
        start = pl.multiple_of((rank ^ k) * QUARTER, 32)
        block = grad_att[pl.ds(start, QUARTER), :].astype(LOW)
        low_part = (block[:, :D], block[:, D : 2 * D])
        high_part = (block[:, 2 * D :], grad_proj[pl.ds(start, QUARTER), :].astype(LOW))
        turned = (0, 2, 1, 3)[k]

        @pl.when(core == 0)
        def _():
            for j in range(2):
                keep_out[turned, j * QUARTER : (j + 1) * QUARTER, :] = low_part[j]
                send_out[k, j * QUARTER : (j + 1) * QUARTER, :] = high_part[j]

        @pl.when(core != 0)
        def _():
            for j in range(2):
                keep_out[k, j * QUARTER : (j + 1) * QUARTER, :] = high_part[j]
                send_out[turned, j * QUARTER : (j + 1) * QUARTER, :] = low_part[j]


def half_of(where):
    return (where[2] >> where[1]) & 1


def rows_at(index, count):
    return pl.ds(pl.multiple_of(index * count, 32), count)


def step0_kernel(
    where, att_keep, att_in, feed_keep, feed_in, small, att_stay, att_go, feed_stay, message, total
):
    half = half_of(where)
    att_stay[...] = att_keep[0:2].astype(WIDE) + att_in[0:2].astype(WIDE)
    att_go[...] = (att_keep[2:4].astype(WIDE) + att_in[2:4].astype(WIDE)).astype(LOW)
    total[...] = feed_keep[0] + feed_in[0].astype(WIDE)
    count = D // 2
    feed_stay[...] = total[rows_at(half, count), :]
    message[0:count, :] = total[rows_at(1 - half, count), :].astype(LOW)
    message[count:, :] = small[...]


def step1_kernel(
    where, att_keep, att_in, feed_keep, own, feed_in, att_stay, att_go, message
):
    count = D // 2
    att_stay[...] = att_keep[0] + att_in[0].astype(WIDE)
    att_go[...] = (att_keep[1] + att_in[1].astype(WIDE)).astype(LOW)
    message[0:count, :] = (feed_keep[...] + feed_in[0:count, :].astype(WIDE)).astype(LOW)
    message[count : count + SMALL, :] = own[count:, :]
    message[count + SMALL :, :] = feed_in[count:, :]


def step2_kernel(
    where, att_keep, att_in, own, feed_in, att_stay, att_go, feed_half, small, total
):
    half = half_of(where)
    count = D // 2
    total[...] = att_keep[...] + att_in[...].astype(WIDE)
    att_stay[...] = total[rows_at(half, QUARTER), :]
    att_go[...] = total[rows_at(1 - half, QUARTER), :].astype(LOW)
    feed_half[...] = (own[0:count, :].astype(WIDE) + feed_in[0:count, :].astype(WIDE)).astype(LOW)
    small[0 : 2 * SMALL, :] = own[count:, :]
    small[2 * SMALL :, :] = feed_in[count:, :]


def step3_kernel(
    where, att_keep, att_in, feed_half, feed_in, small, small_in, att_half, feed_part, small_out
):
    half = half_of(where)
    count = D // 2
    att_half[...] = (att_keep[...] + att_in[...].astype(WIDE)).astype(LOW)
    feed_part[rows_at(half, count), :] = feed_half[...]
    feed_part[rows_at(1 - half, count), :] = feed_in[...]
    small_out[0 : 4 * SMALL, :] = small[...]
    small_out[4 * SMALL :, :] = small_in[...]


def step4_kernel(
    where, att_half, att_in, small, small_in, weight, att_sum, small_out, cond_keep, cond_go
):
    att_sum[...] = (att_half[...].astype(WIDE) + att_in[...].astype(WIDE)).astype(LOW)
    small_out[0 : 8 * SMALL, :] = small[...]
    small_out[8 * SMALL :, :] = small_in[...]
    rows = [
        block[start : start + SMALL, :].astype(WIDE)
        for block in (small, small_in)
        for start in (0, 4 * SMALL)
    ]
    total = None
    for j in range(6):
        lines = [row[6 * slot + j : 6 * slot + j + 1] for row in rows for slot in range(2)]
        term = dot_last(
            jnp.concatenate(lines, axis=0).astype(LOW), weight[:, j * D : (j + 1) * D]
        )
        total = term if total is None else total + term
    padded = jnp.concatenate([total, jnp.zeros((8, 128 - QUARTER), WIDE)], axis=1)
    blank = jnp.zeros((4, 128), WIDE)
    cond_keep[...] = jnp.concatenate([padded[0:4], blank], axis=0)
    cond_go[...] = jnp.concatenate([padded[4:8], blank], axis=0)


def step5_kernel(where, att_sum, att_in, cond_keep, cond_in, _, __, att_part, cond_go):
    half = half_of(where)
    att_part[rows_at(half, QUARTER), :] = att_sum[...]
    att_part[rows_at(1 - half, QUARTER), :] = att_in[...]
    blank = jnp.zeros((4, 128), WIDE)
    cond_go[...] = jnp.concatenate([cond_keep[2:4], cond_in[2:4], blank], axis=0)


def modulation_update_kernel(
    where, near, far, weight, mean, square, bias, bias_mean, bias_square,
    weight_out, mean_out, square_out, bias_out, bias_mean_out, bias_square_out, everyone,
):
    rank, core, plane = where[0], where[1], where[2]
    for side, source in enumerate((near, far)):
        here = core ^ side
        first, second = 1 + here, 2 - here
        for index in range(16):
            a, b, c, d = (index & 1, (index >> 1) & 1, (index >> 2) & 1, index >> 3)
            z_at = plane ^ (a * first) ^ (b * second)
            g_at = rank ^ (c * second) ^ (d * first)
            place = (g_at * 4 + z_at) * 2 + here
            block = source[index * SMALL : (index + 1) * SMALL, :].astype(WIDE)
            for third in range(3):
                everyone[third, rows_at(place, SMALL), :] = block[
                    :, third * 128 : (third + 1) * 128
                ]

    def line(at):
        parts = [everyone[third, pl.ds(at, 32, stride=SMALL), :] for third in range(3)]
        return jnp.concatenate(parts, axis=1)

    def both(at, other):
        return jnp.concatenate([line(at), line(other)], axis=0)

    def own_lanes(values):
        chosen = values[:, :QUARTER]
        for place in range(1, 4):
            lanes = slice(place * QUARTER, (place + 1) * QUARTER)
            chosen = jnp.where(rank == place, values[:, lanes], chosen)
        return chosen

    cond = own_lanes(both(12, 13)).astype(LOW)
    sums = []
    for j in range(6):
        lanes = slice(j * D, (j + 1) * D)
        grads = both(j, 6 + j)
        sums.append(column_sum(grads))
        gradient = dot_first(cond, grads.astype(LOW))
        updated, momentum, variance = adam_update(
            weight[:, lanes].astype(WIDE),
            gradient,
            mean[:, lanes].astype(WIDE),
            square[:, lanes].astype(WIDE),
            LEARN_RATES[0],
            DECAY_FLAGS[0],
        )
        weight_out[:, lanes] = updated
        mean_out[:, lanes] = momentum
        square_out[:, lanes] = variance
    for at in range(14, 22):
        sums.append(column_sum(line(at)))
    gradient = own_lanes(jnp.concatenate(sums, axis=0))
    updated, momentum, variance = adam_update(
        bias[...].astype(WIDE),
        gradient,
        bias_mean[...].astype(WIDE),
        bias_square[...].astype(WIDE),
        LEARN_RATES[5],
        DECAY_FLAGS[5],
    )
    bias_out[...] = updated
    bias_mean_out[...] = momentum
    bias_square_out[...] = variance


def split_kernel(keep, arrived, stay, go):
    half = stay.shape[0]
    stay[...] = keep[:half].astype(WIDE) + arrived[:half].astype(WIDE)
    go[...] = (keep[half:].astype(WIDE) + arrived[half:].astype(WIDE)).astype(LOW)


def whole(shape):
    return pl.BlockSpec(shape, lambda *grid: (0,) * len(shape))


def by_slot(shape):
    return pl.BlockSpec((1,) + shape, lambda s: (s,) + (0,) * len(shape))


def shape_of(shape, dtype):
    return jax.ShapeDtypeStruct(shape, dtype)


SMEM_SPEC = pl.BlockSpec(memory_space=pltpu.SMEM)
PARAMS = pltpu.CompilerParams(vmem_limit_bytes=VMEM_BYTES)


ANY_SPEC = pl.BlockSpec(memory_space=pl.ANY)


def small_call(kernel, name, outs, where, *operands, scratch=(), after=()):
    return pl.pallas_call(
        kernel,
        grid=(1,),
        in_specs=[SMEM_SPEC]
        + [whole(item.shape) for item in operands]
        + [ANY_SPEC] * len(after),
        out_specs=[whole(shape) for shape, _ in outs],
        out_shape=[shape_of(*item) for item in outs],
        scratch_shapes=[pltpu.VMEM(*item) for item in scratch],
        compiler_params=PARAMS,
        name=name,
    )(where, *operands, *after)


def run_payload(where, condition, attending, projection, biases):
    return small_call(
        payload_kernel,
        "own_payload",
        [((2 * QUARTER + 16, D), LOW)],
        where,
        condition,
        attending,
        projection,
        biases,
    )[0]


def run_modulation(where, blocks, weight, expand, contract):
    message = pl.BlockSpec((16, D), lambda s: (2 * QUARTER // 16, 0))
    return pl.pallas_call(
        modulation_kernel,
        grid=(1,),
        in_specs=[SMEM_SPEC] + [message] * 4 + [whole((QUARTER, 6 * D))] + [whole((D, D))] * 2,
        out_specs=[whole((4, 6 * D))] * 2 + [whole((16, D)), whole((D, D))],
        out_shape=[shape_of((4, 6 * D), WIDE)] * 2
        + [shape_of((16, D), WIDE), shape_of((D, D), LOW)],
        compiler_params=PARAMS,
        cost_estimate=pl.CostEstimate(flops=10**7, bytes_accessed=10**6, transcendentals=0),
        name="modulation_partials",
    )(where, *blocks, weight, expand, contract)


def run_attention_forward(where, tokens, stay, arrived, bias, own_att, own_proj, nears, fars):
    part = whole((2 * QUARTER + 16, D))
    return pl.pallas_call(
        attention_forward_kernel,
        grid=(2,),
        in_specs=[
            SMEM_SPEC,
            by_slot((SEQ, D)),
            whole((4, 6 * D)),
            whole((2, 6 * D)),
            whole((16, D)),
            whole((QUARTER, 3 * D)),
            whole((QUARTER, D)),
        ]
        + [part] * 6,
        out_specs=[
            by_slot((SEQ, 3 * D)),
            by_slot((HEADS, SEQ, SEQ)),
            by_slot((SEQ, D)),
            by_slot((6, D)),
            whole((D, 3 * D)),
            whole((D, D)),
        ],
        out_shape=[
            shape_of((2, SEQ, 3 * D), LOW),
            shape_of((2, HEADS, SEQ, SEQ), LOW),
            shape_of((2, SEQ, D), LOW),
            shape_of((2, 6, D), WIDE),
            shape_of((D, 3 * D), LOW),
            shape_of((D, D), LOW),
        ],
        compiler_params=PARAMS,
        cost_estimate=pl.CostEstimate(
            flops=3 * 10**9, bytes_accessed=6 * 10**6, transcendentals=10**6
        ),
        name="attention_forward",
    )(where, tokens, stay, arrived, bias, own_att, own_proj, *nears, *fars)


def run_feed(where, mixed, tokens, cotangent, mod, bias, proj, own_expand, own_contract, nears, fars):
    rows = 2 * SEQ

    def turned(step):
        return jnp.where(step == 1, 2, jnp.where(step == 2, 1, step))

    def keep_place(step, where):
        return (jnp.where(where[1] == 0, turned(step), step), 0, 0)

    def send_place(step, where):
        return (jnp.where(where[1] == 0, step, turned(step)), 0, 0)

    return pl.pallas_call(
        feed_kernel,
        grid_spec=pltpu.PrefetchScalarGridSpec(
            num_scalar_prefetch=1,
            grid=(4,),
            in_specs=[whole((2, SEQ, D))] * 3
            + [whole((2, 6, D)), whole((16, D))]
            + [whole((D, D))] * 9,
            out_specs=[
                whole((2, SEQ, D)),
                whole((2, SEQ, D)),
                pl.BlockSpec((1, D, D), send_place),
                pl.BlockSpec((1, D, D), keep_place),
                whole((16, D)),
            ],
            scratch_shapes=[
                pltpu.VMEM((4, D, D), LOW),
                pltpu.VMEM((4, D, D), LOW),
                pltpu.VMEM((rows, D), WIDE),
                pltpu.VMEM((rows, D), WIDE),
                pltpu.VMEM((rows, D), LOW),
                pltpu.VMEM((rows, D), WIDE),
                pltpu.VMEM((rows, 128), WIDE),
                pltpu.VMEM((rows, D), LOW),
                pltpu.VMEM((rows, D), WIDE),
                pltpu.VMEM((rows, D), WIDE),
            ],
        ),
        out_shape=[
            shape_of((2, SEQ, D), LOW),
            shape_of((2, SEQ, D), WIDE),
            shape_of((4, D, D), LOW),
            shape_of((4, D, D), LOW),
            shape_of((16, D), WIDE),
        ],
        compiler_params=PARAMS,
        cost_estimate=pl.CostEstimate(
            flops=8 * 10**9, bytes_accessed=10**7, transcendentals=10**6
        ),
        name="feed_forward_and_back",
    )(where, mixed, tokens, cotangent, mod, bias, proj, own_expand, own_contract, *nears, *fars)


def run_attention_backward(
    slot, where, tokens, grad_middle, joined, soft, mixed, mod, feed_rows, cond, att, proj, earlier=()
):
    def at_slot(shape):
        return pl.BlockSpec((1,) + shape, lambda i: (slot,) + (0,) * len(shape))

    sums = [((D, 3 * D), WIDE), ((D, D), WIDE), ((SMALL, D), WIDE)]
    in_specs = [
        SMEM_SPEC,
        at_slot((SEQ, D)),
        at_slot((SEQ, D)),
        at_slot((SEQ, 3 * D)),
        at_slot((HEADS, SEQ, SEQ)),
        at_slot((SEQ, D)),
        at_slot((6, D)),
        whole((16, D)),
        whole((2, D)),
        whole((D, 3 * D)),
        whole((D, D)),
    ]
    out_specs = [at_slot((SEQ, D))]
    out_shape = [shape_of((2, SEQ, D), LOW)]
    scratch = [pltpu.VMEM((SEQ, 3 * D), LOW)]
    aliases = {}
    if slot == 0:
        out_specs += [whole(shape) for shape, _ in sums]
        out_shape += [shape_of(*item) for item in sums]
    else:
        in_specs += [whole(shape) for shape, _ in sums] + [ANY_SPEC, ANY_SPEC]
        aliases = {14: 0}
        out_specs += [whole((4, 2 * QUARTER, D))] * 2 + [whole((SMALL, D))]
        out_shape += [shape_of((4, 2 * QUARTER, D), LOW)] * 2 + [shape_of((SMALL, D), LOW)]
        scratch += [pltpu.VMEM(*item) for item in sums]
    return pl.pallas_call(
        functools.partial(attention_backward_kernel, slot),
        grid=(1,),
        in_specs=in_specs,
        out_specs=out_specs,
        out_shape=out_shape,
        scratch_shapes=scratch,
        input_output_aliases=aliases,
        compiler_params=PARAMS,
        cost_estimate=pl.CostEstimate(
            flops=4 * 10**9, bytes_accessed=8 * 10**6, transcendentals=0
        ),
        name="attention_backward",
    )(where, tokens, grad_middle, joined, soft, mixed, mod, feed_rows, cond, att, proj, *earlier)


def run_split(keep, arrived):
    count, rest = keep.shape[0], keep.shape[1:]
    half = (count // 2,) + rest
    return pl.pallas_call(
        split_kernel,
        grid=(1,),
        in_specs=[whole(keep.shape)] * 2,
        out_specs=[whole(half)] * 2,
        out_shape=[shape_of(half, WIDE), shape_of(half, LOW)],
        compiler_params=PARAMS,
        name="sum_and_split",
    )(keep, arrived)


def swap_plane(value, which):
    pairs = [(r, r ^ ((1 + ((r + which) & 1)) << 1)) for r in range(lax.axis_size("replica"))]
    return lax.ppermute(value, "replica", pairs)


def swap_pair(value, which):
    groups, copies = lax.axis_size("group"), lax.axis_size("replica")
    pairs = []
    for g in range(groups):
        for r in range(copies):
            other = g ^ (1 if (r + which) % 2 == 0 else 2)
            pairs.append((g * copies + r, other * copies + r))
    return lax.ppermute(value, ("group", "replica"), pairs)


def gather_pair(value):
    first = swap_pair(value, 0)
    second = swap_pair(value, 1)
    return (first, second, swap_pair(first, 1))


def update_all(stored, gradients, means, squares, kinds):
    return [
        adam_update(
            stored[kind].astype(jnp.float32),
            gradient,
            means[kind].astype(jnp.float32),
            squares[kind].astype(jnp.float32),
            LEARN_RATES[kind],
            DECAY_FLAGS[kind],
        )
        for kind, gradient in zip(kinds, gradients)
    ]


def by_core(core, own, other):
    return (
        jnp.where(core == 0, own, other).astype(jnp.float32),
        jnp.where(core == 0, other, own).astype(jnp.float32),
    )


def attention_shards(totals):
    joined = jnp.concatenate(
        [totals[0][:QUARTER], totals[0][QUARTER:], totals[1][:QUARTER]], axis=1
    )
    return (joined, totals[1][QUARTER:])


def tail_in_step(
    where, copy, stages, condition, ffn_halves, att_parts, small_rows, stored, means, squares
):
    core = where[1]
    (feed_stay, feed_go), (att_send, att_keep) = ffn_halves, att_parts
    half, third = (D // 2, D), (2 * QUARTER, D)
    att_stay, att_go, feed_stay, message = small_call(
        step0_kernel, "step_0",
        [((2,) + third, WIDE), ((2,) + third, LOW), (half, WIDE), ((D // 2 + SMALL, D), LOW)],
        where, att_keep, swap_replica(att_send, 1), feed_stay, swap_pair(feed_go, 1), small_rows,
        scratch=[((D, D), WIDE)],
    )
    att_stay, att_go, message = small_call(
        step1_kernel, "step_1",
        [(third, WIDE), (third, LOW), ((D // 2 + 2 * SMALL, D), LOW)],
        where, att_stay, swap_pair(att_go, 0), feed_stay, message, swap_plane(message, 0),
    )
    quarter = (QUARTER, D)
    att_stay, att_go, feed_half, small = small_call(
        step2_kernel, "step_2",
        [(quarter, WIDE), (quarter, LOW), (half, LOW), ((4 * SMALL, D), LOW)],
        where, att_stay, swap_pair(att_go, 1), message, swap_plane(message, 1),
        scratch=[(third, WIDE)],
    )
    att_half, feed_part, small = small_call(
        step3_kernel, "step_3",
        [(quarter, LOW), ((D, D), LOW), ((8 * SMALL, D), LOW)],
        where, att_stay, swap_plane(att_go, 0), feed_half, swap_plane(feed_half, 0),
        small, swap_pair(small, 1),
    )
    feed_totals = by_core(core, feed_part, swap_replica(feed_part, 1))
    att_sum, small, cond_keep, cond_go = small_call(
        step4_kernel, "step_4",
        [(quarter, LOW), ((16 * SMALL, D), LOW), ((8, 128), WIDE), ((8, 128), WIDE)],
        where, att_half, swap_plane(att_half, 1), small, swap_pair(small, 0), stored[0],
    )
    cond_in = swap_pair(cond_go, 0)
    feed_updates = update_all(stored, feed_totals, means, squares, (3, 4))
    att_part, cond_go = small_call(
        step5_kernel, "step_5",
        [(third, LOW), ((8, 128), WIDE)],
        where, att_sum, swap_plane(att_sum, 0), cond_keep, cond_in,
        after=(feed_updates[0][1], feed_updates[1][1]),
    )
    shard = [((QUARTER, 6 * D), WIDE)] * 3 + [((BIAS_ROWS, QUARTER), WIDE)] * 3
    updates = small_call(
        modulation_update_kernel, "modulation_update", shard,
        where, small, swap_replica(small, 1), stored[0], means[0], squares[0],
        stored[5], means[5], squares[5],
        scratch=[((3, 32 * SMALL, 128), WIDE)],
    )
    cond_last = swap_pair(cond_go, 1)
    att_totals = by_core(core, att_part, swap_replica(att_part, 1))
    blocks = [
        block[:, :QUARTER] for block in (cond_keep[:2], cond_in[:2], cond_last[:2], cond_last[2:4])
    ]
    owners = (where[0],) + neighbours(where)
    lanes = []
    for place in range(4):
        chosen = blocks[0]
        for k in range(1, 4):
            chosen = jnp.where(owners[k] == place, blocks[k], chosen)
        lanes.append(chosen)
    sigmoid_cond = jax.nn.sigmoid(condition)
    grad_condition = (
        jnp.concatenate(lanes, axis=1) * sigmoid_cond * (1.0 + condition * (1.0 - sigmoid_cond))
    )
    att_updates = update_all(stored, attention_shards(att_totals), means, squares, (1, 2))
    return grad_condition, [updates[:3]] + att_updates + feed_updates + [updates[3:]]


def tail_in_turn(
    where, copy, stages, condition, ffn_halves, att_parts, small_rows, stored, means, squares
):
    rank, core = where[0], where[1]
    slot_count, model_width = condition.shape
    modulation, cond_low = stored[0], jax.nn.silu(condition).astype(jnp.bfloat16)
    (ffn_stay, ffn_go), (att_send, att_keep) = ffn_halves, att_parts
    ffn_totals = reduce_replicas(
        wide_sum([ffn_stay[0], swap_pair(ffn_go[0], 1)]).astype(LOW), copy, stages
    )
    att_stay, att_go = run_split(att_keep, swap_replica(att_send, 1))
    att_stay, att_go = run_split(att_stay, swap_pair(att_go, 0))
    att_totals = reduce_replicas(
        wide_sum([att_stay[0], swap_pair(att_go[0], 1)]).astype(LOW), copy, stages
    )
    row_total = small_rows.shape[0]
    gathered = small_rows[None]
    for low_bit, radix in stages[1:]:
        digit = (copy >> low_bit) % radix
        gathered = in_order(
            [swap_replica(gathered, k << low_bit) for k in range(radix)], digit
        ).reshape(-1, row_total, model_width)
    gathered = in_order([swap_group(gathered, k) for k in range(4)], rank)
    own_plane = lax.dynamic_index_in_dim(gathered, copy >> 1, axis=1, keepdims=False)
    group_mod = own_plane[:, : 6 * slot_count].reshape(4 * slot_count, 6 * model_width)
    grad_cond_columns = dot_last(group_mod, modulation).reshape(4, slot_count, model_width // 4)
    cond_back = in_order(
        [swap_group(pick(grad_cond_columns, rank ^ k), k) for k in range(4)], rank
    )
    sigmoid_cond = jax.nn.sigmoid(condition)
    grad_condition = (
        jnp.swapaxes(cond_back, 0, 1).reshape(slot_count, model_width)
        * sigmoid_cond
        * (1.0 + condition * (1.0 - sigmoid_cond))
    )
    everyone = in_order([swap_replica(gathered, k) for k in range(2)], core).reshape(
        -1, row_total, model_width
    )
    all_mod = everyone[:, : 6 * slot_count].reshape(-1, 6 * model_width)
    all_cond = everyone[:, 6 * slot_count : 7 * slot_count].reshape(-1, model_width)
    cond_own = lax.dynamic_slice_in_dim(all_cond, rank * (model_width // 4), model_width // 4, 1)
    grad_mod = dot_first(cond_own, all_mod)
    mod_bias_grad = jnp.sum(all_mod, axis=0, dtype=jnp.float32).reshape(6, model_width)
    rest_bias_grad = jnp.sum(everyone[:, 7 * slot_count : 22], axis=0, dtype=jnp.float32)
    bias_grad = lax.dynamic_slice_in_dim(
        jnp.concatenate([mod_bias_grad, rest_bias_grad], axis=0),
        rank * (model_width // 4),
        model_width // 4,
        1,
    )
    grad_att_own = jnp.concatenate(
        [att_totals[0][:QUARTER], att_totals[0][QUARTER:], att_totals[1][:QUARTER]], axis=1
    )
    totals = (
        grad_mod,
        grad_att_own,
        att_totals[1][QUARTER:],
        ffn_totals[0],
        ffn_totals[1],
        bias_grad,
    )
    return grad_condition, update_all(stored, totals, means, squares, range(6))


def shards(
    latents,
    condition,
    cotangent,
    live_counts,
    modulation,
    attending,
    projection,
    expand,
    contract,
    biases,
    modulation_mean,
    attending_mean,
    projection_mean,
    expand_mean,
    contract_mean,
    biases_mean,
    modulation_square,
    attending_square,
    projection_square,
    expand_square,
    contract_square,
    biases_square,
):
    slot_count, length, model_width = latents.shape
    rank = lax.axis_index("group")
    copy = lax.axis_index("replica")
    core = copy % 2
    stages = replica_stages(lax.axis_size("replica"))
    where = jnp.stack([rank, core, copy >> 1, live_counts[0]]).astype(jnp.int32)

    cond_low = jax.nn.silu(condition).astype(LOW)
    payload = run_payload(where, condition, attending, projection, biases)
    nears = gather_pair(payload)
    fars = [swap_replica(item, 1) for item in nears]
    stay, go, bias, feed_part = run_modulation(
        where, (payload,) + nears, modulation, expand, contract
    )
    feed_nears = gather_pair(feed_part)
    feed_fars = [swap_replica(item, 1) for item in feed_nears]
    stay = stay + swap_pair(go, 0)
    arrived = swap_pair(stay[slot_count:], 1)

    joined, soft, mixed, mod, att, proj = run_attention_forward(
        where, latents, stay, arrived, bias, attending, projection, nears, fars
    )
    out_latents, grad_middle, ffn_send, ffn_keep, feed_rows = run_feed(
        where, mixed, latents, cotangent, mod, bias, proj, expand, contract, feed_nears, feed_fars
    )
    cond_wide = cond_low.astype(WIDE)
    ffn_stay, ffn_go = run_split(ffn_keep, swap_replica(ffn_send, 1))
    half_tokens, half_att, half_proj, half_rows = run_attention_backward(
        0, where, latents, grad_middle, joined, soft, mixed, mod, feed_rows, cond_wide, att, proj
    )
    ffn_stay, ffn_go = run_split(ffn_stay, swap_pair(ffn_go, 0))
    grad_latents, att_send, att_keep, small_rows = run_attention_backward(
        1, where, latents, grad_middle, joined, soft, mixed, mod, feed_rows, cond_wide, att, proj,
        (half_att, half_proj, half_rows, half_tokens, ffn_go),
    )
    tail = tail_in_step if lax.axis_size("replica") == 8 else tail_in_turn
    grad_condition, results = tail(
        where, copy, stages, condition, (ffn_stay, ffn_go), (att_send, att_keep), small_rows,
        (modulation, attending, projection, expand, contract, biases),
        (
            modulation_mean, attending_mean, projection_mean,
            expand_mean, contract_mean, biases_mean,
        ),
        (
            modulation_square, attending_square, projection_square,
            expand_square, contract_square, biases_square,
        ),
    )
    return (
        out_latents,
        grad_latents,
        grad_condition,
        results[0][0],
        results[1][0],
        results[2][0],
        results[3][0],
        results[4][0],
        results[5][0],
        results[0][1],
        results[1][1],
        results[2][1],
        results[3][1],
        results[4][1],
        results[5][1],
        results[0][2],
        results[1][2],
        results[2][2],
        results[3][2],
        results[4][2],
        results[5][2],
    )


def solution(mesh):
    return jax.shard_map(
        shards,
        mesh=mesh,
        in_specs=(
            P(("group", "replica"), None, None),
            P(("group", "replica"), None),
            P(("group", "replica"), None, None),
            P(("group", "replica")),
            P("group", None),
            P("group", None),
            P("group", None),
            P(None, "group"),
            P("group", None),
            P(None, "group"),
            P("group", None),
            P("group", None),
            P("group", None),
            P(None, "group"),
            P("group", None),
            P(None, "group"),
            P("group", None),
            P("group", None),
            P("group", None),
            P(None, "group"),
            P("group", None),
            P(None, "group"),
        ),
        out_specs=(
            P(("group", "replica"), None, None),
            P(("group", "replica"), None, None),
            P(("group", "replica"), None),
            P("group", None),
            P("group", None),
            P("group", None),
            P(None, "group"),
            P("group", None),
            P(None, "group"),
            P("group", None),
            P("group", None),
            P("group", None),
            P(None, "group"),
            P("group", None),
            P(None, "group"),
            P("group", None),
            P("group", None),
            P("group", None),
            P(None, "group"),
            P("group", None),
            P(None, "group"),
        ),
        check_vma=False,
    )
```

```python
import functools

import jax
import jax.numpy as jnp
from jax import lax
from jax.experimental import pallas as pl
from jax.experimental.pallas import tpu as pltpu
from jax.sharding import PartitionSpec as P

HEADS = 6
HEAD_DIM = 64
FF = 1536
STEP = 10


NORM_EPS = 1e-06
ADAM_EPS = 1e-08
BETA_FIRST = 0.9
BETA_SECOND = 0.999
DECAY_RATE = 0.1
LEARN_RATES = (0.05, 0.05, 0.2, 0.05, 0.025, 0.1)
DECAY_FLAGS = (1.0, 1.0, 1.0, 1.0, 1.0, 0.0)
GELU_COEF = 0.7978845608028654
BIAS_ROWS = 14
D = 384
SEQ = 256
QUARTER = D // 4
VMEM_BYTES = 48 * 1024 * 1024
LOW = jnp.bfloat16
SMALL = 32
WIDE = jnp.float32


def dot_plain(left_side, right_side):
    return jnp.dot(left_side, right_side, preferred_element_type=WIDE)


def dot_first(left_side, right_side):
    return lax.dot_general(
        left_side, right_side, (((0,), (0,)), ((), ())), preferred_element_type=WIDE
    )


def dot_last(left_side, right_side):
    return lax.dot_general(
        left_side, right_side, (((1,), (1,)), ((), ())), preferred_element_type=WIDE
    )


def adam_update(weight, gradient, mean_old, square_old, step_rate, decay_flag):
    momentum = BETA_FIRST * mean_old + (1.0 - BETA_FIRST) * gradient
    variance = BETA_SECOND * square_old + (1.0 - BETA_SECOND) * gradient * gradient
    mean_hat = momentum / (1.0 - BETA_FIRST**STEP)
    square_hat = variance / (1.0 - BETA_SECOND**STEP)
    updated = weight - step_rate * (
        mean_hat / (jnp.sqrt(square_hat) + ADAM_EPS) + decay_flag * DECAY_RATE * weight
    )
    return (updated, momentum, variance)


def replica_stages(count):
    stages, low_bit = [(0, 2)], 1
    while (1 << low_bit) < count:
        radix = min(4, count >> low_bit)
        stages.append((low_bit, radix))
        low_bit += radix.bit_length() - 1
    return stages


def swap_group(value, k):
    if k == 0:
        return value
    return lax.ppermute(value, "group", [(i, i ^ k) for i in range(lax.axis_size("group"))])


def swap_replica(value, k):
    if k == 0:
        return value
    return lax.ppermute(value, "replica", [(i, i ^ k) for i in range(lax.axis_size("replica"))])


def pick(blocks, index):
    return lax.dynamic_index_in_dim(blocks, index, axis=0, keepdims=False)


def in_order(blocks, digit):
    ordered = []
    for place in range(len(blocks)):
        chosen = blocks[0]
        for k in range(1, len(blocks)):
            chosen = jnp.where((digit ^ k) == place, blocks[k], chosen)
        ordered.append(chosen)
    return jnp.stack(ordered)


def wide_sum(blocks):
    total = blocks[0].astype(jnp.float32)
    for block in blocks[1:]:
        total = total + block.astype(jnp.float32)
    return total


def scatter_stage(value, digit, low_bit, radix):
    rows = value.shape[-2] // radix
    parts = [
        lax.dynamic_slice_in_dim(value, (digit ^ k) * rows, rows, value.ndim - 2)
        for k in range(radix)
    ]
    received = [swap_replica(parts[k], k << low_bit) for k in range(radix)]
    return wide_sum(received).astype(jnp.bfloat16)


def reduce_replicas(value, copy, stages):
    core = copy % 2
    for low_bit, radix in stages[1:]:
        value = scatter_stage(value, (copy >> low_bit) % radix, low_bit, radix)
    for low_bit, radix in reversed(stages[1:]):
        blocks = [swap_replica(value, k << low_bit) for k in range(radix)]
        value = in_order(blocks, (copy >> low_bit) % radix)
        value = value.reshape(-1, value.shape[-1])
    other = swap_replica(value, 1)
    return (
        jnp.where(core == 0, value, other).astype(jnp.float32),
        jnp.where(core == 0, other, value).astype(jnp.float32),
    )


def layer_norm_parts(values):
    centred = values - jnp.mean(values, axis=-1, keepdims=True)
    inverse = lax.rsqrt(jnp.mean(centred * centred, axis=-1, keepdims=True) + NORM_EPS)
    return (centred * inverse, inverse)


def norm_backward(grad_normed, normed, inverse):
    mean_grad = jnp.mean(grad_normed, axis=-1, keepdims=True)
    mean_cross = jnp.mean(grad_normed * normed, axis=-1, keepdims=True)
    return inverse * (grad_normed - mean_grad - normed * mean_cross)


def column_sum(values):
    return jnp.sum(values, axis=0, keepdims=True)


def head_mask(shape, which):
    lane = lax.broadcasted_iota(jnp.int32, shape, 1)
    return (lane < HEAD_DIM) if which == 0 else (lane >= HEAD_DIM)


def place_rows(target, lanes, block, owner):
    start = pl.multiple_of(owner * QUARTER, 32)
    target[pl.ds(start, QUARTER), lanes] = block


def neighbours(where):
    rank, core = where[0], where[1]
    return (rank ^ (1 + core), rank ^ (2 - core), rank ^ 3)


def payload_kernel(where, condition, attending, projection, biases, expand, contract, out, part):
    @pl.when(where[1] == 0)
    def _():
        part[...] = expand[...]
        out[0:QUARTER, :] = attending[:, 0:D]
        out[QUARTER : 2 * QUARTER, :] = attending[:, D : 2 * D]

    @pl.when(where[1] != 0)
    def _():
        part[...] = contract[...]
        out[0:QUARTER, :] = attending[:, 2 * D : 3 * D]
        out[QUARTER : 2 * QUARTER, :] = projection[...]

    cond = condition[...]
    active = cond / (1.0 + jnp.exp(-cond))
    padded = jnp.concatenate(
        [biases[...].astype(WIDE), jnp.zeros((BIAS_ROWS, D - QUARTER), WIDE)], axis=1
    )
    out[2 * QUARTER :, :] = jnp.concatenate([active, padded], axis=0).astype(LOW)


def modulation_kernel(
    where, own, first, second, last, weight, stay, go, bias_out
):
    rank = where[0]
    owners = (rank,) + neighbours(where)
    rows = [block[...].astype(WIDE) for block in (own, first, second, last)]
    conds = jnp.concatenate([rows[0][0:2], rows[2][0:2], rows[1][0:2], rows[3][0:2]], axis=0)
    columns = conds[:, :QUARTER]
    for place in range(1, 4):
        lanes = slice(place * QUARTER, (place + 1) * QUARTER)
        columns = jnp.where(rank == place, conds[:, lanes], columns)
    partial = dot_plain(columns.astype(LOW), weight[...])
    stay[...] = partial[:4]
    go[...] = partial[4:]
    lanes = []
    for place in range(4):
        chosen = rows[0][:, :QUARTER]
        for k in range(1, 4):
            chosen = jnp.where(owners[k] == place, rows[k][:, :QUARTER], chosen)
        lanes.append(chosen)
    bias_out[...] = jnp.concatenate(lanes, axis=1)


def relay_kernel(where, keep, arrived, _, stay, go, __):
    stay[...] = keep[0:2, :] + arrived[0:2, :]
    go[...] = keep[2:4, :] + arrived[2:4, :]


def gate_kernel(*refs):
    pass


def attention_forward_kernel(
    where, tokens, stay, arrived, bias, own_att, own_proj, n1, n2, n3, f1, f2, f3,
    joined_out, soft_out, mixed_out, mod_out, att, proj,
):
    slot = pl.program_id(0)
    rank = where[0]

    core = where[1]

    def assemble(lows, highs):
        for k, block in zip((1, 2, 3), lows):
            place_rows(att, slice(0, D), block[0:QUARTER, :], rank ^ k)
            place_rows(att, slice(D, 2 * D), block[QUARTER : 2 * QUARTER, :], rank ^ k)
        for k, block in zip((2, 1, 3), highs):
            place_rows(att, slice(2 * D, 3 * D), block[0:QUARTER, :], rank ^ k)
            place_rows(proj, slice(0, D), block[QUARTER : 2 * QUARTER, :], rank ^ k)

    @pl.when(slot == 0)
    def _():
        place_rows(att, slice(0, 3 * D), own_att[...], rank)
        place_rows(proj, slice(0, D), own_proj[...], rank)

        @pl.when(core == 0)
        def _():
            assemble((n1, n2, n3), (f1, f2, f3))

        @pl.when(core != 0)
        def _():
            assemble((f1, f2, f3), (n1, n2, n3))

    summed = stay[...] + arrived[...]
    row = jnp.where(slot == 0, summed[0:1], summed[1:2])
    pieces = [row[:, j * D : (j + 1) * D] + bias[2 + j : 3 + j, :] for j in range(6)]
    mod_out[0] = jnp.concatenate(pieces, axis=0)
    normed, _ = layer_norm_parts(tokens[0].astype(WIDE))
    first_in = (normed * (1.0 + pieces[1]) + pieces[0]).astype(LOW)
    thirds = []
    for third in range(3):
        part = dot_plain(first_in, att[:, third * D : (third + 1) * D])
        if third == 0:
            part = part + bias[8:9, :]
        if third == 2:
            part = part + bias[9:10, :]
        part = part.astype(LOW)
        joined_out[0, :, third * D : (third + 1) * D] = part
        thirds.append(part)
    first_half = head_mask((SEQ, 128), 0)
    scale = jnp.asarray(HEAD_DIM ** (-0.5), LOW)
    zero = jnp.zeros((SEQ, 128), LOW)
    for pair in range(HEADS // 2):
        lanes = slice(pair * 128, (pair + 1) * 128)
        query, key, value = (part[:, lanes] for part in thirds)
        query = query * scale
        outs = []
        for half in range(2):
            masked = (
                jnp.where(first_half, query, zero)
                if half == 0
                else jnp.where(first_half, zero, query)
            )
            scores = dot_last(masked, key)
            weights = jnp.exp(scores - jnp.max(scores, axis=-1, keepdims=True))
            total = jnp.sum(weights, axis=-1, keepdims=True)
            soft = (weights * (1.0 / total)).astype(LOW)
            soft_out[0, 2 * pair + half] = soft
            outs.append(dot_plain(soft, value))
        mixed_out[0, :, lanes] = jnp.where(first_half, outs[0], outs[1]).astype(LOW)


def feed_kernel(
    where, mixed, tokens, cotangent, mod, bias, proj, own_expand, own_contract, n1, n2, n3, f1, f2, f3,
    out, grad_middle_out, send_out, keep_out, rows_out,
    expands, contracts, branch, middle, second, normed, inverse, grad_feed, feed, grad_second,
):
    step = pl.program_id(0)
    rank, core, live = where[0], where[1], where[3]

    def assemble(lows, highs):
        for k, block in zip((1, 2, 3), lows):
            expands[k] = block[...]
        for k, block in zip((2, 1, 3), highs):
            contracts[k] = block[...]

    slots = [slice(s * SEQ, (s + 1) * SEQ) for s in range(2)]

    @pl.when(step == 0)
    def _():
        expands[0] = own_expand[...]
        contracts[0] = own_contract[...]

        @pl.when(core == 0)
        def _():
            assemble((n1, n2, n3), (f1, f2, f3))

        @pl.when(core != 0)
        def _():
            assemble((f1, f2, f3), (n1, n2, n3))

        for s, rows in enumerate(slots):
            pieces = mod[s]
            value = dot_plain(mixed[s], proj[...]) + bias[10:11, :]
            branch[rows, :] = value
            centre = tokens[s].astype(WIDE) + pieces[2:3] * value
            middle[rows, :] = centre
            unit, spread = layer_norm_parts(centre)
            normed[rows, :] = unit
            inverse[rows, :] = jnp.broadcast_to(spread, (SEQ, 128))
            second[rows, :] = (unit * (1.0 + pieces[4:5]) + pieces[3:4]).astype(LOW)
            alive = jnp.where(s < live, 1.0, 0.0)
            grad_feed[rows, :] = (
                pieces[5:6] * (cotangent[s].astype(WIDE) * alive)
            ).astype(LOW)
        rows_out[...] = jnp.zeros_like(rows_out)
        rows_out[12:13, :] = column_sum(grad_feed[...].astype(WIDE))

    hidden_bias = bias[pl.ds(11 + (rank ^ step), 1), :]
    expand, contract = expands[step], contracts[step]
    before = dot_plain(second[...], expand) + hidden_bias
    square = before * before
    tangent = jnp.tanh(before * (GELU_COEF + (GELU_COEF * 0.044715) * square))
    half_up = 0.5 + 0.5 * tangent
    activated = (before * half_up).astype(LOW)
    slope = half_up + (0.5 * before) * (1.0 - tangent * tangent) * (
        GELU_COEF + (GELU_COEF * 3.0 * 0.044715) * square
    )
    grad_before_wide = dot_last(grad_feed[...], contract) * slope
    grad_before = grad_before_wide.astype(LOW)
    feed_term = dot_plain(activated, contract)
    second_term = dot_last(grad_before, expand)
    grad_expand = dot_first(second[...], grad_before).astype(LOW)
    grad_contract = dot_first(activated, grad_feed[...]).astype(LOW)
    rows_out[pl.ds(8 + (rank ^ step), 1), :] = column_sum(grad_before.astype(WIDE))

    @pl.when(core == 0)
    def _():
        send_out[0] = grad_contract
        keep_out[0] = grad_expand

    @pl.when(core != 0)
    def _():
        send_out[0] = grad_expand
        keep_out[0] = grad_contract

    @pl.when(step == 0)
    def _():
        feed[...] = feed_term
        grad_second[...] = second_term

    @pl.when(step > 0)
    def _():
        feed[...] += feed_term
        grad_second[...] += second_term

    @pl.when(step == 3)
    def _():
        for s, rows in enumerate(slots):
            pieces = mod[s]
            alive = jnp.where(s < live, 1.0, 0.0)
            feed_out = feed[rows, :] + bias[15:16, :]
            grad_out = cotangent[s].astype(WIDE) * alive
            out[s] = ((middle[rows, :] + pieces[5:6] * feed_out) * alive).astype(LOW)
            grad = grad_second[rows, :]
            unit = normed[rows, :]
            grad_middle = grad_out + norm_backward(
                grad * (1.0 + pieces[4:5]), unit, inverse[rows, 0:1]
            )
            grad_middle_out[s] = grad_middle
            rows_out[4 * s : 4 * s + 1, :] = column_sum(grad_middle * branch[rows, :])
            rows_out[4 * s + 1 : 4 * s + 2, :] = column_sum(grad)
            rows_out[4 * s + 2 : 4 * s + 3, :] = column_sum(grad * unit)
            rows_out[4 * s + 3 : 4 * s + 4, :] = column_sum(grad_out * feed_out)


def attention_backward_kernel(
    slot, where, tokens, grad_middle_in, joined, soft_in, mixed, mod, feed_rows, cond, att, proj, *refs
):
    rank, core = where[0], where[1]
    if slot == 0:
        grad_tokens_out, grad_att, grad_proj, rows, grad_joined = refs
    else:
        before_att, before_proj, before_rows, _, _ = refs[:5]
        grad_tokens_out, send_out, keep_out, rows_out = refs[5:9]
        grad_joined, grad_att, grad_proj, rows = refs[9:]

    if slot == 0:
        rows[...] = jnp.zeros_like(rows)
        rows[12:14, :] = cond[...]
        rows[17:22, :] = feed_rows[8:13, :]
    else:
        rows[...] = before_rows[...]

    pieces = mod[0]
    grad_middle = grad_middle_in[0]
    grad_branch = (pieces[2:3] * grad_middle).astype(LOW)
    rows[16:17, :] += column_sum(grad_branch.astype(WIDE))
    proj_term = dot_first(mixed[0], grad_branch)
    grad_proj[...] = proj_term if slot == 0 else before_proj[...] + proj_term
    grad_mixed = dot_last(grad_branch, proj[...]).astype(LOW)
    first_half = head_mask((SEQ, 128), 0)
    zero = jnp.zeros((SEQ, 128), LOW)
    scale = HEAD_DIM ** (-0.5)
    for pair in range(HEADS // 2):
        lanes = slice(pair * 128, (pair + 1) * 128)
        query = joined[0, :, pair * 128 : (pair + 1) * 128]
        key = joined[0, :, D + pair * 128 : D + (pair + 1) * 128]
        value = joined[0, :, 2 * D + pair * 128 : 2 * D + (pair + 1) * 128]
        grads = grad_mixed[:, lanes]
        results = []
        for half in range(2):
            soft = soft_in[0, 2 * pair + half]
            masked = (
                jnp.where(first_half, grads, zero)
                if half == 0
                else jnp.where(first_half, zero, grads)
            )
            grad_soft = dot_last(masked, value)
            grad_values = dot_first(soft, grads)
            soft_wide = soft.astype(WIDE)
            weighted = soft_wide * grad_soft
            inner = jnp.sum(weighted, axis=-1, keepdims=True)
            grad_scores = (weighted - soft_wide * inner).astype(LOW)
            results.append(
                (dot_plain(grad_scores, key), dot_first(grad_scores, query), grad_values)
            )
        for third in range(3):
            merged = jnp.where(first_half, results[0][third], results[1][third])
            if third < 2:
                merged = merged * scale
            grad_joined[:, third * D + pair * 128 : third * D + (pair + 1) * 128] = merged.astype(LOW)
    grads = grad_joined[...]
    sums = column_sum(grads.astype(WIDE))
    rows[14:15, :] += sums[:, :D]
    rows[15:16, :] += sums[:, 2 * D :]
    normed, inverse = layer_norm_parts(tokens[0].astype(WIDE))
    first_in = (normed * (1.0 + pieces[1:2]) + pieces[0:1]).astype(LOW)
    att_term = dot_first(first_in, grads)
    grad_att[...] = att_term if slot == 0 else before_att[...] + att_term
    grad_first = dot_last(grads, att[...])
    grad_tokens_out[0] = (
        grad_middle + norm_backward(grad_first * (1.0 + pieces[1:2]), normed, inverse)
    ).astype(LOW)
    own_rows = jnp.concatenate(
        [
            column_sum(grad_first),
            column_sum(grad_first * normed),
        ],
        axis=0,
    )

    rows[6 * slot : 6 * slot + 2, :] = own_rows
    rows[6 * slot + 2 : 6 * slot + 6, :] = feed_rows[4 * slot : 4 * slot + 4, :]
    if slot == 0:
        return
    rows_out[...] = rows[...].astype(LOW)
    for k in range(4):
        start = pl.multiple_of((rank ^ k) * QUARTER, 32)
        block = grad_att[pl.ds(start, QUARTER), :].astype(LOW)
        low_part = (block[:, :D], block[:, D : 2 * D])
        high_part = (block[:, 2 * D :], grad_proj[pl.ds(start, QUARTER), :].astype(LOW))
        turned = (0, 2, 1, 3)[k]

        @pl.when(core == 0)
        def _():
            for j in range(2):
                keep_out[turned, j * QUARTER : (j + 1) * QUARTER, :] = low_part[j]
                send_out[k, j * QUARTER : (j + 1) * QUARTER, :] = high_part[j]

        @pl.when(core != 0)
        def _():
            for j in range(2):
                keep_out[k, j * QUARTER : (j + 1) * QUARTER, :] = high_part[j]
                send_out[turned, j * QUARTER : (j + 1) * QUARTER, :] = low_part[j]


def half_of(where):
    return (where[2] >> where[1]) & 1


def rows_at(index, count):
    return pl.ds(pl.multiple_of(index * count, 32), count)


def step1_kernel(
    where, att_keep, att_in, feed_keep, feed_in, small, small_in,
    att_stay, att_go, feed_stay, feed_go, small_out, total,
):
    half = half_of(where)
    count = D // 2
    att_stay[...] = att_keep[0] + att_in[0].astype(WIDE)
    att_go[...] = (att_keep[1] + att_in[1].astype(WIDE)).astype(LOW)
    total[...] = feed_keep[...] + feed_in[...].astype(WIDE)
    feed_stay[...] = total[rows_at(half, count), :]
    feed_go[...] = total[rows_at(1 - half, count), :].astype(LOW)
    small_out[0:SMALL, :] = small[...]
    small_out[SMALL:, :] = small_in[...]


def step2_kernel(
    where, att_keep, att_in, feed_keep, feed_in, small, small_in,
    att_stay, att_go, feed_half, small_out, total,
):
    half = half_of(where)
    total[...] = att_keep[...] + att_in[...].astype(WIDE)
    att_stay[...] = total[rows_at(half, QUARTER), :]
    att_go[...] = total[rows_at(1 - half, QUARTER), :].astype(LOW)
    feed_half[...] = (feed_keep[...] + feed_in[...].astype(WIDE)).astype(LOW)
    small_out[0 : 2 * SMALL, :] = small[...]
    small_out[2 * SMALL :, :] = small_in[...]


def step3_kernel(
    where, att_keep, att_in, feed_half, feed_in, small, small_in, att_half, feed_sum, small_out
):
    att_half[...] = (att_keep[...] + att_in[...].astype(WIDE)).astype(LOW)
    feed_sum[...] = (feed_half[...].astype(WIDE) + feed_in[...].astype(WIDE)).astype(LOW)
    small_out[0 : 4 * SMALL, :] = small[...]
    small_out[4 * SMALL :, :] = small_in[...]


def step4_kernel(
    where, att_half, att_in, feed_sum, feed_in, small, small_in, weight,
    att_sum, feed_part, small_out, cond_keep, cond_go,
):
    half = half_of(where)
    count = D // 2
    feed_part[rows_at(half, count), :] = feed_sum[...]
    feed_part[rows_at(1 - half, count), :] = feed_in[...]
    att_sum[...] = (att_half[...].astype(WIDE) + att_in[...].astype(WIDE)).astype(LOW)
    small_out[0 : 8 * SMALL, :] = small[...]
    small_out[8 * SMALL :, :] = small_in[...]
    rows = [
        block[start : start + SMALL, :].astype(WIDE)
        for block in (small, small_in)
        for start in (0, 4 * SMALL)
    ]
    total = None
    for j in range(6):
        lines = [row[6 * slot + j : 6 * slot + j + 1] for row in rows for slot in range(2)]
        term = dot_last(
            jnp.concatenate(lines, axis=0).astype(LOW), weight[:, j * D : (j + 1) * D]
        )
        total = term if total is None else total + term
    padded = jnp.concatenate([total, jnp.zeros((8, 128 - QUARTER), WIDE)], axis=1)
    blank = jnp.zeros((4, 128), WIDE)
    cond_keep[...] = jnp.concatenate([padded[0:4], blank], axis=0)
    cond_go[...] = jnp.concatenate([padded[4:8], blank], axis=0)


def step5_kernel(where, att_sum, att_in, cond_keep, cond_in, att_part, cond_go):
    half = half_of(where)
    att_part[rows_at(half, QUARTER), :] = att_sum[...]
    att_part[rows_at(1 - half, QUARTER), :] = att_in[...]
    blank = jnp.zeros((4, 128), WIDE)
    cond_go[...] = jnp.concatenate([cond_keep[2:4], cond_in[2:4], blank], axis=0)


def modulation_update_kernel(
    where, near, far, weight, mean, square, bias, bias_mean, bias_square,
    weight_out, mean_out, square_out, bias_out, bias_mean_out, bias_square_out, everyone,
):
    rank, core, plane = where[0], where[1], where[2]
    for side, source in enumerate((near, far)):
        here = core ^ side
        first, second = 1 + here, 2 - here
        for index in range(16):
            a, b, c, d = (index & 1, (index >> 1) & 1, (index >> 2) & 1, index >> 3)
            z_at = plane ^ (a * first) ^ (b * second)
            g_at = rank ^ (c * second) ^ (d * first)
            place = (g_at * 4 + z_at) * 2 + here
            block = source[index * SMALL : (index + 1) * SMALL, :].astype(WIDE)
            for third in range(3):
                everyone[third, rows_at(place, SMALL), :] = block[
                    :, third * 128 : (third + 1) * 128
                ]

    def line(at):
        parts = [everyone[third, pl.ds(at, 32, stride=SMALL), :] for third in range(3)]
        return jnp.concatenate(parts, axis=1)

    def both(at, other):
        return jnp.concatenate([line(at), line(other)], axis=0)

    def own_lanes(values):
        chosen = values[:, :QUARTER]
        for place in range(1, 4):
            lanes = slice(place * QUARTER, (place + 1) * QUARTER)
            chosen = jnp.where(rank == place, values[:, lanes], chosen)
        return chosen

    cond = own_lanes(both(12, 13)).astype(LOW)
    sums = []
    for j in range(6):
        lanes = slice(j * D, (j + 1) * D)
        grads = both(j, 6 + j)
        sums.append(column_sum(grads))
        gradient = dot_first(cond, grads.astype(LOW))
        updated, momentum, variance = adam_update(
            weight[:, lanes].astype(WIDE),
            gradient,
            mean[:, lanes].astype(WIDE),
            square[:, lanes].astype(WIDE),
            LEARN_RATES[0],
            DECAY_FLAGS[0],
        )
        weight_out[:, lanes] = updated
        mean_out[:, lanes] = momentum
        square_out[:, lanes] = variance
    for at in range(14, 22):
        sums.append(column_sum(line(at)))
    gradient = own_lanes(jnp.concatenate(sums, axis=0))
    updated, momentum, variance = adam_update(
        bias[...].astype(WIDE),
        gradient,
        bias_mean[...].astype(WIDE),
        bias_square[...].astype(WIDE),
        LEARN_RATES[5],
        DECAY_FLAGS[5],
    )
    bias_out[...] = updated
    bias_mean_out[...] = momentum
    bias_square_out[...] = variance


def split_kernel(keep, arrived, stay, go):
    half = stay.shape[0]
    stay[...] = keep[:half].astype(WIDE) + arrived[:half].astype(WIDE)
    go[...] = (keep[half:].astype(WIDE) + arrived[half:].astype(WIDE)).astype(LOW)


def whole(shape):
    return pl.BlockSpec(shape, lambda *grid: (0,) * len(shape))


def by_slot(shape):
    return pl.BlockSpec((1,) + shape, lambda s: (s,) + (0,) * len(shape))


def shape_of(shape, dtype):
    return jax.ShapeDtypeStruct(shape, dtype)


SMEM_SPEC = pl.BlockSpec(memory_space=pltpu.SMEM)
PARAMS = pltpu.CompilerParams(vmem_limit_bytes=VMEM_BYTES)


ANY_SPEC = pl.BlockSpec(memory_space=pl.ANY)


def small_call(kernel, name, outs, where, *operands, scratch=(), params=PARAMS):
    return pl.pallas_call(
        kernel,
        grid=(1,),
        in_specs=[SMEM_SPEC] + [whole(item.shape) for item in operands],
        out_specs=[whole(shape) for shape, _ in outs],
        out_shape=[shape_of(*item) for item in outs],
        scratch_shapes=[pltpu.VMEM(*item) for item in scratch],
        compiler_params=params,
        name=name,
    )(where, *operands)


def run_gate(value, *after):
    return pl.pallas_call(
        gate_kernel,
        in_specs=[ANY_SPEC] * (1 + len(after)),
        out_specs=ANY_SPEC,
        out_shape=shape_of(value.shape, value.dtype),
        input_output_aliases={0: 0},
        name="in_order",
    )(value, *after)


def run_relay(where, keep, arrived, passing):
    two = (2, keep.shape[1])
    return pl.pallas_call(
        relay_kernel,
        grid=(1,),
        in_specs=[SMEM_SPEC, whole(keep.shape), whole(arrived.shape), ANY_SPEC],
        out_specs=[whole(two), whole(two), ANY_SPEC],
        out_shape=[shape_of(two, WIDE)] * 2 + [shape_of(passing.shape, passing.dtype)],
        input_output_aliases={3: 2},
        compiler_params=PARAMS,
        name="relay",
    )(where, keep, arrived, passing)


def run_modulation(where, blocks, weight):
    message = pl.BlockSpec((16, D), lambda s: (2 * QUARTER // 16, 0))
    return pl.pallas_call(
        modulation_kernel,
        grid=(1,),
        in_specs=[SMEM_SPEC] + [message] * 4 + [whole((QUARTER, 6 * D))],
        out_specs=[whole((4, 6 * D))] * 2 + [whole((16, D))],
        out_shape=[shape_of((4, 6 * D), WIDE)] * 2 + [shape_of((16, D), WIDE)],
        compiler_params=PARAMS,
        cost_estimate=pl.CostEstimate(flops=10**7, bytes_accessed=10**6, transcendentals=0),
        name="modulation_partials",
    )(where, *blocks, weight)


def run_attention_forward(where, tokens, stay, arrived, bias, own_att, own_proj, nears, fars):
    part = whole((2 * QUARTER + 16, D))
    return pl.pallas_call(
        attention_forward_kernel,
        grid=(2,),
        in_specs=[
            SMEM_SPEC,
            by_slot((SEQ, D)),
            whole((2, 6 * D)),
            whole((2, 6 * D)),
            whole((16, D)),
            whole((QUARTER, 3 * D)),
            whole((QUARTER, D)),
        ]
        + [part] * 6,
        out_specs=[
            by_slot((SEQ, 3 * D)),
            by_slot((HEADS, SEQ, SEQ)),
            by_slot((SEQ, D)),
            by_slot((6, D)),
            whole((D, 3 * D)),
            whole((D, D)),
        ],
        out_shape=[
            shape_of((2, SEQ, 3 * D), LOW),
            shape_of((2, HEADS, SEQ, SEQ), LOW),
            shape_of((2, SEQ, D), LOW),
            shape_of((2, 6, D), WIDE),
            shape_of((D, 3 * D), LOW),
            shape_of((D, D), LOW),
        ],
        compiler_params=PARAMS,
        cost_estimate=pl.CostEstimate(
            flops=3 * 10**9, bytes_accessed=6 * 10**6, transcendentals=10**6
        ),
        name="attention_forward",
    )(where, tokens, stay, arrived, bias, own_att, own_proj, *nears, *fars)


def run_feed(where, mixed, tokens, cotangent, mod, bias, proj, own_expand, own_contract, nears, fars):
    rows = 2 * SEQ

    def turned(step):
        return jnp.where(step == 1, 2, jnp.where(step == 2, 1, step))

    def keep_place(step, where):
        return (jnp.where(where[1] == 0, turned(step), step), 0, 0)

    def send_place(step, where):
        return (jnp.where(where[1] == 0, step, turned(step)), 0, 0)

    return pl.pallas_call(
        feed_kernel,
        grid_spec=pltpu.PrefetchScalarGridSpec(
            num_scalar_prefetch=1,
            grid=(4,),
            in_specs=[whole((2, SEQ, D))] * 3
            + [whole((2, 6, D)), whole((16, D))]
            + [whole((D, D))] * 9,
            out_specs=[
                whole((2, SEQ, D)),
                whole((2, SEQ, D)),
                pl.BlockSpec((1, D, D), send_place),
                pl.BlockSpec((1, D, D), keep_place),
                whole((16, D)),
            ],
            scratch_shapes=[
                pltpu.VMEM((4, D, D), LOW),
                pltpu.VMEM((4, D, D), LOW),
                pltpu.VMEM((rows, D), WIDE),
                pltpu.VMEM((rows, D), WIDE),
                pltpu.VMEM((rows, D), LOW),
                pltpu.VMEM((rows, D), WIDE),
                pltpu.VMEM((rows, 128), WIDE),
                pltpu.VMEM((rows, D), LOW),
                pltpu.VMEM((rows, D), WIDE),
                pltpu.VMEM((rows, D), WIDE),
            ],
        ),
        out_shape=[
            shape_of((2, SEQ, D), LOW),
            shape_of((2, SEQ, D), WIDE),
            shape_of((4, D, D), LOW),
            shape_of((4, D, D), LOW),
            shape_of((16, D), WIDE),
        ],
        compiler_params=PARAMS,
        cost_estimate=pl.CostEstimate(
            flops=8 * 10**9, bytes_accessed=10**7, transcendentals=10**6
        ),
        name="feed_forward_and_back",
    )(where, mixed, tokens, cotangent, mod, bias, proj, own_expand, own_contract, *nears, *fars)


def run_attention_backward(
    slot, where, tokens, grad_middle, joined, soft, mixed, mod, feed_rows, cond, att, proj, earlier=()
):
    def at_slot(shape):
        return pl.BlockSpec((1,) + shape, lambda i: (slot,) + (0,) * len(shape))

    sums = [((D, 3 * D), WIDE), ((D, D), WIDE), ((SMALL, D), WIDE)]
    in_specs = [
        SMEM_SPEC,
        at_slot((SEQ, D)),
        at_slot((SEQ, D)),
        at_slot((SEQ, 3 * D)),
        at_slot((HEADS, SEQ, SEQ)),
        at_slot((SEQ, D)),
        at_slot((6, D)),
        whole((16, D)),
        whole((2, D)),
        whole((D, 3 * D)),
        whole((D, D)),
    ]
    out_specs = [at_slot((SEQ, D))]
    out_shape = [shape_of((2, SEQ, D), LOW)]
    scratch = [pltpu.VMEM((SEQ, 3 * D), LOW)]
    aliases = {}
    if slot == 0:
        out_specs += [whole(shape) for shape, _ in sums]
        out_shape += [shape_of(*item) for item in sums]
    else:
        in_specs += [whole(shape) for shape, _ in sums] + [ANY_SPEC, ANY_SPEC]
        aliases = {14: 0}
        out_specs += [whole((4, 2 * QUARTER, D))] * 2 + [whole((SMALL, D))]
        out_shape += [shape_of((4, 2 * QUARTER, D), LOW)] * 2 + [shape_of((SMALL, D), LOW)]
        scratch += [pltpu.VMEM(*item) for item in sums]
    return pl.pallas_call(
        functools.partial(attention_backward_kernel, slot),
        grid=(1,),
        in_specs=in_specs,
        out_specs=out_specs,
        out_shape=out_shape,
        scratch_shapes=scratch,
        input_output_aliases=aliases,
        compiler_params=PARAMS,
        cost_estimate=pl.CostEstimate(
            flops=4 * 10**9, bytes_accessed=8 * 10**6, transcendentals=0
        ),
        name="attention_backward",
    )(where, tokens, grad_middle, joined, soft, mixed, mod, feed_rows, cond, att, proj, *earlier)


def run_split(keep, arrived):
    count, rest = keep.shape[0], keep.shape[1:]
    half = (count // 2,) + rest
    return pl.pallas_call(
        split_kernel,
        grid=(1,),
        in_specs=[whole(keep.shape)] * 2,
        out_specs=[whole(half)] * 2,
        out_shape=[shape_of(half, WIDE), shape_of(half, LOW)],
        compiler_params=PARAMS,
        name="sum_and_split",
    )(keep, arrived)


def swap_plane(value, which):
    pairs = [(r, r ^ ((1 + ((r + which) & 1)) << 1)) for r in range(lax.axis_size("replica"))]
    return lax.ppermute(value, "replica", pairs)


def swap_pair(value, which):
    groups, copies = lax.axis_size("group"), lax.axis_size("replica")
    pairs = []
    for g in range(groups):
        for r in range(copies):
            other = g ^ (1 if (r + which) % 2 == 0 else 2)
            pairs.append((g * copies + r, other * copies + r))
    return lax.ppermute(value, ("group", "replica"), pairs)


def gather_pair(value):
    first = swap_pair(value, 0)
    second = swap_pair(value, 1)
    return (first, second, swap_pair(first, 1))


def update_all(stored, gradients, means, squares, kinds):
    return [
        adam_update(
            stored[kind].astype(jnp.float32),
            gradient,
            means[kind].astype(jnp.float32),
            squares[kind].astype(jnp.float32),
            LEARN_RATES[kind],
            DECAY_FLAGS[kind],
        )
        for kind, gradient in zip(kinds, gradients)
    ]


def by_core(core, own, other):
    return (
        jnp.where(core == 0, own, other).astype(jnp.float32),
        jnp.where(core == 0, other, own).astype(jnp.float32),
    )


def attention_shards(totals):
    joined = jnp.concatenate(
        [totals[0][:QUARTER], totals[0][QUARTER:], totals[1][:QUARTER]], axis=1
    )
    return (joined, totals[1][QUARTER:])


def tail_in_step(
    where, copy, stages, condition, ffn_halves, att_parts, small_rows, stored, means, squares
):
    core = where[1]
    (feed_stay, feed_in), (att_send, att_keep) = ffn_halves, att_parts
    half, third, quarter = (D // 2, D), (2 * QUARTER, D), (QUARTER, D)
    att_stay, att_go = run_split(att_keep, swap_replica(att_send, 1))
    feed_stay, feed_go = run_split(feed_stay, feed_in)
    feed_stay, feed_go = feed_stay[0], feed_go[0]
    att_stay, att_go, feed_stay, feed_go, small = small_call(
        step1_kernel, "step_1",
        [(third, WIDE), (third, LOW), (half, WIDE), (half, LOW), ((2 * SMALL, D), LOW)],
        where, att_stay, swap_pair(att_go, 0), feed_stay, swap_pair(feed_go, 1),
        small_rows, swap_plane(small_rows, 0),
        scratch=[((D, D), WIDE)],
    )
    att_stay, att_go, feed_half, small = small_call(
        step2_kernel, "step_2",
        [(quarter, WIDE), (quarter, LOW), (half, LOW), ((4 * SMALL, D), LOW)],
        where, att_stay, swap_pair(att_go, 1), feed_stay, swap_plane(feed_go, 0),
        small, swap_plane(small, 1),
        scratch=[(third, WIDE)],
    )
    att_half, feed_sum, small = small_call(
        step3_kernel, "step_3",
        [(quarter, LOW), (half, LOW), ((8 * SMALL, D), LOW)],
        where, att_stay, swap_plane(att_go, 0), feed_half, swap_plane(feed_half, 1),
        small, swap_pair(small, 1),
    )
    att_sum, feed_part, small, cond_keep, cond_go = small_call(
        step4_kernel, "step_4",
        [(quarter, LOW), ((D, D), LOW), ((16 * SMALL, D), LOW), ((8, 128), WIDE), ((8, 128), WIDE)],
        where, att_half, swap_plane(att_half, 1), feed_sum, swap_plane(feed_sum, 0),
        small, swap_pair(small, 0), stored[0],
    )
    feed_totals = by_core(core, feed_part, swap_replica(feed_part, 1))
    cond_in = swap_pair(cond_go, 0)
    feed_updates = update_all(stored, feed_totals, means, squares, (3, 4))
    att_part, cond_go = small_call(
        step5_kernel, "step_5",
        [(third, LOW), ((8, 128), WIDE)],
        where, att_sum, swap_plane(att_sum, 0), cond_keep, cond_in,
    )
    shard = [((QUARTER, 6 * D), WIDE)] * 3 + [((BIAS_ROWS, QUARTER), WIDE)] * 3
    updates = small_call(
        modulation_update_kernel, "modulation_update", shard,
        where, small, swap_replica(small, 1), stored[0], means[0], squares[0],
        stored[5], means[5], squares[5],
        scratch=[((3, 32 * SMALL, 128), WIDE)],
    )
    cond_last = swap_pair(cond_go, 1)
    att_totals = by_core(core, att_part, swap_replica(att_part, 1))
    blocks = [
        block[:, :QUARTER] for block in (cond_keep[:2], cond_in[:2], cond_last[:2], cond_last[2:4])
    ]
    owners = (where[0],) + neighbours(where)
    lanes = []
    for place in range(4):
        chosen = blocks[0]
        for k in range(1, 4):
            chosen = jnp.where(owners[k] == place, blocks[k], chosen)
        lanes.append(chosen)
    sigmoid_cond = jax.nn.sigmoid(condition)
    grad_condition = (
        jnp.concatenate(lanes, axis=1) * sigmoid_cond * (1.0 + condition * (1.0 - sigmoid_cond))
    )
    att_updates = update_all(stored, attention_shards(att_totals), means, squares, (1, 2))
    return grad_condition, [updates[:3]] + att_updates + feed_updates + [updates[3:]]


def tail_in_turn(
    where, copy, stages, condition, ffn_halves, att_parts, small_rows, stored, means, squares
):
    rank, core = where[0], where[1]
    slot_count, model_width = condition.shape
    modulation, cond_low = stored[0], jax.nn.silu(condition).astype(jnp.bfloat16)
    (ffn_stay, ffn_in), (att_send, att_keep) = ffn_halves, att_parts
    ffn_stay, ffn_go = run_split(ffn_stay, ffn_in)
    ffn_totals = reduce_replicas(
        wide_sum([ffn_stay[0], swap_pair(ffn_go[0], 1)]).astype(LOW), copy, stages
    )
    att_stay, att_go = run_split(att_keep, swap_replica(att_send, 1))
    att_stay, att_go = run_split(att_stay, swap_pair(att_go, 0))
    att_totals = reduce_replicas(
        wide_sum([att_stay[0], swap_pair(att_go[0], 1)]).astype(LOW), copy, stages
    )
    row_total = small_rows.shape[0]
    gathered = small_rows[None]
    for low_bit, radix in stages[1:]:
        digit = (copy >> low_bit) % radix
        gathered = in_order(
            [swap_replica(gathered, k << low_bit) for k in range(radix)], digit
        ).reshape(-1, row_total, model_width)
    gathered = in_order([swap_group(gathered, k) for k in range(4)], rank)
    own_plane = lax.dynamic_index_in_dim(gathered, copy >> 1, axis=1, keepdims=False)
    group_mod = own_plane[:, : 6 * slot_count].reshape(4 * slot_count, 6 * model_width)
    grad_cond_columns = dot_last(group_mod, modulation).reshape(4, slot_count, model_width // 4)
    cond_back = in_order(
        [swap_group(pick(grad_cond_columns, rank ^ k), k) for k in range(4)], rank
    )
    sigmoid_cond = jax.nn.sigmoid(condition)
    grad_condition = (
        jnp.swapaxes(cond_back, 0, 1).reshape(slot_count, model_width)
        * sigmoid_cond
        * (1.0 + condition * (1.0 - sigmoid_cond))
    )
    everyone = in_order([swap_replica(gathered, k) for k in range(2)], core).reshape(
        -1, row_total, model_width
    )
    all_mod = everyone[:, : 6 * slot_count].reshape(-1, 6 * model_width)
    all_cond = everyone[:, 6 * slot_count : 7 * slot_count].reshape(-1, model_width)
    cond_own = lax.dynamic_slice_in_dim(all_cond, rank * (model_width // 4), model_width // 4, 1)
    grad_mod = dot_first(cond_own, all_mod)
    mod_bias_grad = jnp.sum(all_mod, axis=0, dtype=jnp.float32).reshape(6, model_width)
    rest_bias_grad = jnp.sum(everyone[:, 7 * slot_count : 22], axis=0, dtype=jnp.float32)
    bias_grad = lax.dynamic_slice_in_dim(
        jnp.concatenate([mod_bias_grad, rest_bias_grad], axis=0),
        rank * (model_width // 4),
        model_width // 4,
        1,
    )
    grad_att_own = jnp.concatenate(
        [att_totals[0][:QUARTER], att_totals[0][QUARTER:], att_totals[1][:QUARTER]], axis=1
    )
    totals = (
        grad_mod,
        grad_att_own,
        att_totals[1][QUARTER:],
        ffn_totals[0],
        ffn_totals[1],
        bias_grad,
    )
    return grad_condition, update_all(stored, totals, means, squares, range(6))


def shards(
    latents,
    condition,
    cotangent,
    live_counts,
    modulation,
    attending,
    projection,
    expand,
    contract,
    biases,
    modulation_mean,
    attending_mean,
    projection_mean,
    expand_mean,
    contract_mean,
    biases_mean,
    modulation_square,
    attending_square,
    projection_square,
    expand_square,
    contract_square,
    biases_square,
):
    slot_count, length, model_width = latents.shape
    rank = lax.axis_index("group")
    copy = lax.axis_index("replica")
    core = copy % 2
    stages = replica_stages(lax.axis_size("replica"))
    where = jnp.stack([rank, core, copy >> 1, live_counts[0]]).astype(jnp.int32)

    cond_low = jax.nn.silu(condition).astype(LOW)
    payload, feed_part = small_call(
        payload_kernel, "own_payload",
        [((2 * QUARTER + 16, model_width), LOW), ((model_width, model_width), LOW)],
        where, condition, attending, projection, biases, expand, contract,
        params=pltpu.CompilerParams(vmem_limit_bytes=60 * 1024 * 1024),
    )
    first, second = swap_pair(payload, 0), swap_pair(payload, 1)
    feed_part = run_gate(feed_part, first, second)
    nears = (first, second, swap_pair(first, 1))
    fars = [swap_replica(item, 1) for item in nears]
    feed_first, feed_second = swap_pair(feed_part, 0), swap_pair(feed_part, 1)
    stay, go, bias = run_modulation(where, (payload,) + nears, modulation)
    stay, go, feed_first = run_relay(where, stay, swap_pair(go, 0), feed_first)
    arrived = swap_pair(go, 1)
    feed_nears = (feed_first, feed_second, swap_pair(feed_first, 1))
    feed_fars = [swap_replica(item, 1) for item in feed_nears]

    joined, soft, mixed, mod, att, proj = run_attention_forward(
        where, latents, stay, arrived, bias, attending, projection, nears, fars
    )
    out_latents, grad_middle, ffn_send, ffn_keep, feed_rows = run_feed(
        where, mixed, latents, cotangent, mod, bias, proj, expand, contract, feed_nears, feed_fars
    )
    cond_wide = cond_low.astype(WIDE)
    ffn_stay, ffn_go = run_split(ffn_keep, swap_replica(ffn_send, 1))
    half_tokens, half_att, half_proj, half_rows = run_attention_backward(
        0, where, latents, grad_middle, joined, soft, mixed, mod, feed_rows, cond_wide, att, proj
    )
    ffn_in = swap_pair(ffn_go, 0)
    grad_latents, att_send, att_keep, small_rows = run_attention_backward(
        1, where, latents, grad_middle, joined, soft, mixed, mod, feed_rows, cond_wide, att, proj,
        (half_att, half_proj, half_rows, half_tokens, ffn_go),
    )
    tail = tail_in_step if lax.axis_size("replica") == 8 else tail_in_turn
    grad_condition, results = tail(
        where, copy, stages, condition, (ffn_stay, ffn_in), (att_send, att_keep), small_rows,
        (modulation, attending, projection, expand, contract, biases),
        (
            modulation_mean, attending_mean, projection_mean,
            expand_mean, contract_mean, biases_mean,
        ),
        (
            modulation_square, attending_square, projection_square,
            expand_square, contract_square, biases_square,
        ),
    )
    return (
        out_latents,
        grad_latents,
        grad_condition,
        results[0][0],
        results[1][0],
        results[2][0],
        results[3][0],
        results[4][0],
        results[5][0],
        results[0][1],
        results[1][1],
        results[2][1],
        results[3][1],
        results[4][1],
        results[5][1],
        results[0][2],
        results[1][2],
        results[2][2],
        results[3][2],
        results[4][2],
        results[5][2],
    )


def solution(mesh):
    return jax.shard_map(
        shards,
        mesh=mesh,
        in_specs=(
            P(("group", "replica"), None, None),
            P(("group", "replica"), None),
            P(("group", "replica"), None, None),
            P(("group", "replica")),
            P("group", None),
            P("group", None),
            P("group", None),
            P(None, "group"),
            P("group", None),
            P(None, "group"),
            P("group", None),
            P("group", None),
            P("group", None),
            P(None, "group"),
            P("group", None),
            P(None, "group"),
            P("group", None),
            P("group", None),
            P("group", None),
            P(None, "group"),
            P("group", None),
            P(None, "group"),
        ),
        out_specs=(
            P(("group", "replica"), None, None),
            P(("group", "replica"), None, None),
            P(("group", "replica"), None),
            P("group", None),
            P("group", None),
            P("group", None),
            P(None, "group"),
            P("group", None),
            P(None, "group"),
            P("group", None),
            P("group", None),
            P("group", None),
            P(None, "group"),
            P("group", None),
            P(None, "group"),
            P("group", None),
            P("group", None),
            P("group", None),
            P(None, "group"),
            P("group", None),
            P(None, "group"),
        ),
        check_vma=False,
    )
```

```python
import functools

import jax
import jax.numpy as jnp
from jax import lax
from jax.experimental import pallas as pl
from jax.experimental.pallas import tpu as pltpu
from jax.sharding import PartitionSpec as P

HEADS = 6
HEAD_DIM = 64
FF = 1536
STEP = 10


NORM_EPS = 1e-06
ADAM_EPS = 1e-08
BETA_FIRST = 0.9
BETA_SECOND = 0.999
DECAY_RATE = 0.1
LEARN_RATES = (0.05, 0.05, 0.2, 0.05, 0.025, 0.1)
DECAY_FLAGS = (1.0, 1.0, 1.0, 1.0, 1.0, 0.0)
GELU_COEF = 0.7978845608028654
BIAS_ROWS = 14
D = 384
SEQ = 256
QUARTER = D // 4
VMEM_BYTES = 48 * 1024 * 1024
LOW = jnp.bfloat16
SMALL = 32
WIDE = jnp.float32


def dot_plain(left_side, right_side):
    return jnp.dot(left_side, right_side, preferred_element_type=WIDE)


def dot_first(left_side, right_side):
    return lax.dot_general(
        left_side, right_side, (((0,), (0,)), ((), ())), preferred_element_type=WIDE
    )


def dot_last(left_side, right_side):
    return lax.dot_general(
        left_side, right_side, (((1,), (1,)), ((), ())), preferred_element_type=WIDE
    )


def adam_update(weight, gradient, mean_old, square_old, step_rate, decay_flag):
    momentum = BETA_FIRST * mean_old + (1.0 - BETA_FIRST) * gradient
    variance = BETA_SECOND * square_old + ((1.0 - BETA_SECOND) * gradient) * gradient
    root = variance * lax.rsqrt(variance)
    bottom = root * (1.0 - BETA_SECOND**STEP) ** (-0.5) + ADAM_EPS
    change = momentum * (step_rate / (1.0 - BETA_FIRST**STEP)) / bottom
    updated = weight * (1.0 - step_rate * decay_flag * DECAY_RATE) - change
    return (updated, momentum, variance)


def replica_stages(count):
    stages, low_bit = [(0, 2)], 1
    while (1 << low_bit) < count:
        radix = min(4, count >> low_bit)
        stages.append((low_bit, radix))
        low_bit += radix.bit_length() - 1
    return stages


def swap_group(value, k):
    if k == 0:
        return value
    return lax.ppermute(value, "group", [(i, i ^ k) for i in range(lax.axis_size("group"))])


def swap_replica(value, k):
    if k == 0:
        return value
    return lax.ppermute(value, "replica", [(i, i ^ k) for i in range(lax.axis_size("replica"))])


def pick(blocks, index):
    return lax.dynamic_index_in_dim(blocks, index, axis=0, keepdims=False)


def in_order(blocks, digit):
    ordered = []
    for place in range(len(blocks)):
        chosen = blocks[0]
        for k in range(1, len(blocks)):
            chosen = jnp.where((digit ^ k) == place, blocks[k], chosen)
        ordered.append(chosen)
    return jnp.stack(ordered)


def wide_sum(blocks):
    total = blocks[0].astype(jnp.float32)
    for block in blocks[1:]:
        total = total + block.astype(jnp.float32)
    return total


def scatter_stage(value, digit, low_bit, radix):
    rows = value.shape[-2] // radix
    parts = [
        lax.dynamic_slice_in_dim(value, (digit ^ k) * rows, rows, value.ndim - 2)
        for k in range(radix)
    ]
    received = [swap_replica(parts[k], k << low_bit) for k in range(radix)]
    return wide_sum(received).astype(jnp.bfloat16)


def reduce_replicas(value, copy, stages):
    core = copy % 2
    for low_bit, radix in stages[1:]:
        value = scatter_stage(value, (copy >> low_bit) % radix, low_bit, radix)
    for low_bit, radix in reversed(stages[1:]):
        blocks = [swap_replica(value, k << low_bit) for k in range(radix)]
        value = in_order(blocks, (copy >> low_bit) % radix)
        value = value.reshape(-1, value.shape[-1])
    other = swap_replica(value, 1)
    return (
        jnp.where(core == 0, value, other).astype(jnp.float32),
        jnp.where(core == 0, other, value).astype(jnp.float32),
    )


def layer_norm_parts(values):
    centred = values - jnp.mean(values, axis=-1, keepdims=True)
    inverse = lax.rsqrt(jnp.mean(centred * centred, axis=-1, keepdims=True) + NORM_EPS)
    return (centred * inverse, inverse)


def norm_backward(grad_normed, normed, inverse):
    mean_grad = jnp.mean(grad_normed, axis=-1, keepdims=True)
    mean_cross = jnp.mean(grad_normed * normed, axis=-1, keepdims=True)
    return inverse * (grad_normed - mean_grad - normed * mean_cross)


def column_sum(values):
    return jnp.sum(values, axis=0, keepdims=True)


def head_mask(shape, which):
    lane = lax.broadcasted_iota(jnp.int32, shape, 1)
    return (lane < HEAD_DIM) if which == 0 else (lane >= HEAD_DIM)


def place_rows(target, lanes, block, owner):
    start = pl.multiple_of(owner * QUARTER, 32)
    target[pl.ds(start, QUARTER), lanes] = block


def neighbours(where):
    rank, core = where[0], where[1]
    return (rank ^ (1 + core), rank ^ (2 - core), rank ^ 3)


def own_message(condition, biases):
    cond = condition[...]
    active = cond / (1.0 + jnp.exp(-cond))
    padded = jnp.concatenate(
        [biases[...].astype(WIDE), jnp.zeros((BIAS_ROWS, D - QUARTER), WIDE)], axis=1
    )
    return jnp.concatenate([active, padded], axis=0)


def payload_kernel(where, condition, attending, projection, biases, expand, contract, out, part):
    @pl.when(where[1] == 0)
    def _():
        part[...] = expand[...]
        out[0:QUARTER, :] = attending[:, 0:D]
        out[QUARTER : 2 * QUARTER, :] = attending[:, D : 2 * D]

    @pl.when(where[1] != 0)
    def _():
        part[...] = contract[...]
        out[0:QUARTER, :] = attending[:, 2 * D : 3 * D]
        out[QUARTER : 2 * QUARTER, :] = projection[...]

    out[2 * QUARTER :, :] = own_message(condition, biases).astype(LOW)


def modulation_kernel(
    where, condition, biases, first, second, last, weight, stay, go, bias_out
):
    rank = where[0]
    owners = (rank,) + neighbours(where)
    rows = [own_message(condition, biases)]
    rows += [block[...].astype(WIDE) for block in (first, second, last)]
    conds = jnp.concatenate([rows[0][0:2], rows[2][0:2], rows[1][0:2], rows[3][0:2]], axis=0)
    columns = conds[:, :QUARTER]
    for place in range(1, 4):
        lanes = slice(place * QUARTER, (place + 1) * QUARTER)
        columns = jnp.where(rank == place, conds[:, lanes], columns)
    partial = dot_plain(columns.astype(LOW), weight[...])
    stay[...] = partial[:4]
    go[...] = partial[4:]
    lanes = []
    for place in range(4):
        chosen = rows[0][:, :QUARTER]
        for k in range(1, 4):
            chosen = jnp.where(owners[k] == place, rows[k][:, :QUARTER], chosen)
        lanes.append(chosen)
    bias_out[...] = jnp.concatenate(lanes, axis=1)


def relay_kernel(where, keep, arrived, _, stay, go, __):
    stay[...] = keep[0:2, :] + arrived[0:2, :]
    go[...] = keep[2:4, :] + arrived[2:4, :]


def gate_kernel(*refs):
    pass


def attention_forward_kernel(
    where, tokens, stay, arrived, bias, own_att, own_proj, n1, n2, n3, f1, f2, f3,
    joined_out, soft_out, mixed_out, mod_out, att, proj,
):
    slot = pl.program_id(0)
    rank = where[0]

    core = where[1]

    def assemble(lows, highs):
        for k, block in zip((1, 2, 3), lows):
            place_rows(att, slice(0, D), block[0:QUARTER, :], rank ^ k)
            place_rows(att, slice(D, 2 * D), block[QUARTER : 2 * QUARTER, :], rank ^ k)
        for k, block in zip((2, 1, 3), highs):
            place_rows(att, slice(2 * D, 3 * D), block[0:QUARTER, :], rank ^ k)
            place_rows(proj, slice(0, D), block[QUARTER : 2 * QUARTER, :], rank ^ k)

    @pl.when(slot == 0)
    def _():
        place_rows(att, slice(0, 3 * D), own_att[...], rank)
        place_rows(proj, slice(0, D), own_proj[...], rank)

        @pl.when(core == 0)
        def _():
            assemble((n1, n2, n3), (f1, f2, f3))

        @pl.when(core != 0)
        def _():
            assemble((f1, f2, f3), (n1, n2, n3))

    summed = stay[...] + arrived[...]
    row = jnp.where(slot == 0, summed[0:1], summed[1:2])
    pieces = [row[:, j * D : (j + 1) * D] + bias[2 + j : 3 + j, :] for j in range(6)]
    mod_out[0] = jnp.concatenate(pieces, axis=0)
    normed, _ = layer_norm_parts(tokens[0].astype(WIDE))
    first_in = (normed * (1.0 + pieces[1]) + pieces[0]).astype(LOW)
    thirds = []
    for third in range(3):
        part = dot_plain(first_in, att[:, third * D : (third + 1) * D])
        if third == 0:
            part = part + bias[8:9, :]
        if third == 2:
            part = part + bias[9:10, :]
        part = part.astype(LOW)
        joined_out[0, :, third * D : (third + 1) * D] = part
        thirds.append(part)
    first_half = head_mask((SEQ, 128), 0)
    scale = jnp.asarray(HEAD_DIM ** (-0.5), LOW)
    zero = jnp.zeros((SEQ, 128), LOW)
    for pair in range(HEADS // 2):
        lanes = slice(pair * 128, (pair + 1) * 128)
        query, key, value = (part[:, lanes] for part in thirds)
        query = query * scale
        outs = []
        for half in range(2):
            masked = (
                jnp.where(first_half, query, zero)
                if half == 0
                else jnp.where(first_half, zero, query)
            )
            scores = dot_last(masked, key)
            weights = jnp.exp(scores - jnp.max(scores, axis=-1, keepdims=True))
            total = jnp.sum(weights, axis=-1, keepdims=True)
            soft = (weights * (1.0 / total)).astype(LOW)
            soft_out[0, 2 * pair + half] = soft
            outs.append(dot_plain(soft, value))
        mixed_out[0, :, lanes] = jnp.where(first_half, outs[0], outs[1]).astype(LOW)


def feed_kernel(
    where, mixed, tokens, cotangent, mod, bias, proj, own_expand, own_contract, n1, n2, n3, f1, f2, f3,
    out, grad_middle_out, send_out, keep_out, rows_out,
    expands, contracts, branch, middle, second, normed, inverse, grad_feed, feed, grad_second,
):
    step = pl.program_id(0)
    rank, core, live = where[0], where[1], where[3]

    def assemble(lows, highs):
        for k, block in zip((1, 2, 3), lows):
            expands[k // 2, :, (k % 2) * D : (k % 2 + 1) * D] = block[...]
        for k, block in zip((2, 1, 3), highs):
            contracts[k // 2, (k % 2) * D : (k % 2 + 1) * D, :] = block[...]

    slots = [slice(s * SEQ, (s + 1) * SEQ) for s in range(2)]

    @pl.when(step == 0)
    def _():
        expands[0, :, 0:D] = own_expand[...]
        contracts[0, 0:D, :] = own_contract[...]

        @pl.when(core == 0)
        def _():
            assemble((n1, n2, n3), (f1, f2, f3))

        @pl.when(core != 0)
        def _():
            assemble((f1, f2, f3), (n1, n2, n3))

        for s, rows in enumerate(slots):
            pieces = mod[s]
            value = dot_plain(mixed[s], proj[...]) + bias[10:11, :]
            branch[rows, :] = value
            centre = tokens[s].astype(WIDE) + pieces[2:3] * value
            middle[rows, :] = centre
            unit, spread = layer_norm_parts(centre)
            normed[rows, :] = unit
            inverse[rows, :] = jnp.broadcast_to(spread, (SEQ, 128))
            second[rows, :] = (unit * (1.0 + pieces[4:5]) + pieces[3:4]).astype(LOW)
            alive = jnp.where(s < live, 1.0, 0.0)
            grad_feed[rows, :] = (
                pieces[5:6] * (cotangent[s].astype(WIDE) * alive)
            ).astype(LOW)
        rows_out[...] = jnp.zeros_like(rows_out)
        rows_out[12:13, :] = column_sum(grad_feed[...].astype(WIDE))

    owners = (rank ^ (2 * step), rank ^ (2 * step + 1))
    hidden_bias = jnp.concatenate([bias[pl.ds(11 + owner, 1), :] for owner in owners], axis=1)
    expand, contract = expands[step], contracts[step]
    before = dot_plain(second[...], expand) + hidden_bias
    square = before * before
    tangent = jnp.tanh(before * (GELU_COEF + (GELU_COEF * 0.044715) * square))
    half_up = 0.5 + 0.5 * tangent
    activated = (before * half_up).astype(LOW)
    slope = half_up + (0.5 * before) * (1.0 - tangent * tangent) * (
        GELU_COEF + (GELU_COEF * 3.0 * 0.044715) * square
    )
    grad_before_wide = dot_last(grad_feed[...], contract) * slope
    grad_before = grad_before_wide.astype(LOW)
    feed_term = dot_plain(activated, contract)
    second_term = dot_last(grad_before, expand)
    grad_expand = dot_first(second[...], grad_before).astype(LOW)
    grad_contract = dot_first(activated, grad_feed[...]).astype(LOW)
    sums = column_sum(grad_before.astype(WIDE))
    for k, owner in enumerate(owners):
        rows_out[pl.ds(8 + owner, 1), :] = sums[:, k * D : (k + 1) * D]

    @pl.when(core == 0)
    def _():
        for k in range(2):
            send_out[k] = grad_contract[k * D : (k + 1) * D, :]
            keep_out[k] = grad_expand[:, k * D : (k + 1) * D]

    @pl.when(core != 0)
    def _():
        for k in range(2):
            send_out[k] = grad_expand[:, k * D : (k + 1) * D]
            keep_out[k] = grad_contract[k * D : (k + 1) * D, :]

    @pl.when(step == 0)
    def _():
        feed[...] = feed_term
        grad_second[...] = second_term

    @pl.when(step > 0)
    def _():
        feed[...] += feed_term
        grad_second[...] += second_term

    @pl.when(step == 1)
    def _():
        for s, rows in enumerate(slots):
            pieces = mod[s]
            alive = jnp.where(s < live, 1.0, 0.0)
            feed_out = feed[rows, :] + bias[15:16, :]
            grad_out = cotangent[s].astype(WIDE) * alive
            out[s] = ((middle[rows, :] + pieces[5:6] * feed_out) * alive).astype(LOW)
            grad = grad_second[rows, :]
            unit = normed[rows, :]
            grad_middle = grad_out + norm_backward(
                grad * (1.0 + pieces[4:5]), unit, inverse[rows, 0:1]
            )
            grad_middle_out[s] = grad_middle
            rows_out[4 * s : 4 * s + 1, :] = column_sum(grad_middle * branch[rows, :])
            rows_out[4 * s + 1 : 4 * s + 2, :] = column_sum(grad)
            rows_out[4 * s + 2 : 4 * s + 3, :] = column_sum(grad * unit)
            rows_out[4 * s + 3 : 4 * s + 4, :] = column_sum(grad_out * feed_out)


def attention_backward_kernel(
    slot, where, tokens, grad_middle_in, joined, soft_in, mixed, mod, feed_rows, cond, att, proj, *refs
):
    rank, core = where[0], where[1]
    if slot == 0:
        grad_tokens_out, grad_joined, first_out, branch_out, rows = refs
    else:
        before_joined, before_first, before_branch, before_rows, _, _ = refs[:6]
        grad_tokens_out, send_out, keep_out, rows_out = refs[6:10]
        grad_joined, grad_att, grad_proj, rows = refs[10:]

    if slot == 0:
        rows[...] = jnp.zeros_like(rows)
        rows[12:14, :] = cond[...]
        rows[17:22, :] = feed_rows[8:13, :]
    else:
        rows[...] = before_rows[...]

    pieces = mod[0]
    grad_middle = grad_middle_in[0]
    grad_branch = (pieces[2:3] * grad_middle).astype(LOW)
    rows[16:17, :] += column_sum(grad_branch.astype(WIDE))
    if slot == 0:
        branch_out[...] = grad_branch
    else:
        grad_proj[...] = (
            dot_first(mixed[0], before_branch[...]) + dot_first(mixed[1], grad_branch)
        ).astype(LOW)
    grad_mixed = dot_last(grad_branch, proj[...]).astype(LOW)
    first_half = head_mask((SEQ, 128), 0)
    zero = jnp.zeros((SEQ, 128), LOW)
    scale = HEAD_DIM ** (-0.5)
    for pair in range(HEADS // 2):
        lanes = slice(pair * 128, (pair + 1) * 128)
        query = joined[0, :, pair * 128 : (pair + 1) * 128]
        key = joined[0, :, D + pair * 128 : D + (pair + 1) * 128]
        value = joined[0, :, 2 * D + pair * 128 : 2 * D + (pair + 1) * 128]
        grads = grad_mixed[:, lanes]
        results = []
        for half in range(2):
            soft = soft_in[0, 2 * pair + half]
            masked = (
                jnp.where(first_half, grads, zero)
                if half == 0
                else jnp.where(first_half, zero, grads)
            )
            grad_soft = dot_last(masked, value)
            grad_values = dot_first(soft, grads)
            soft_wide = soft.astype(WIDE)
            weighted = soft_wide * grad_soft
            inner = jnp.sum(weighted, axis=-1, keepdims=True)
            grad_scores = (weighted - soft_wide * inner).astype(LOW)
            results.append(
                (dot_plain(grad_scores, key), dot_first(grad_scores, query), grad_values)
            )
        for third in range(3):
            merged = jnp.where(first_half, results[0][third], results[1][third])
            if third < 2:
                merged = merged * scale
            grad_joined[:, third * D + pair * 128 : third * D + (pair + 1) * 128] = merged.astype(LOW)
    grads = grad_joined[...]
    sums = column_sum(grads.astype(WIDE))
    rows[14:15, :] += sums[:, :D]
    rows[15:16, :] += sums[:, 2 * D :]
    normed, inverse = layer_norm_parts(tokens[0].astype(WIDE))
    first_in = (normed * (1.0 + pieces[1:2]) + pieces[0:1]).astype(LOW)
    if slot == 0:
        first_out[...] = first_in
    else:
        for third in range(3):
            lanes = slice(third * D, (third + 1) * D)
            grad_att[:, lanes] = (
                dot_first(before_first[...], before_joined[:, lanes])
                + dot_first(first_in, grad_joined[:, lanes])
            ).astype(LOW)
    grad_first = dot_last(grads, att[...])
    grad_tokens_out[0] = (
        grad_middle + norm_backward(grad_first * (1.0 + pieces[1:2]), normed, inverse)
    ).astype(LOW)
    own_rows = jnp.concatenate(
        [
            column_sum(grad_first),
            column_sum(grad_first * normed),
        ],
        axis=0,
    )

    rows[6 * slot : 6 * slot + 2, :] = own_rows
    rows[6 * slot + 2 : 6 * slot + 6, :] = feed_rows[4 * slot : 4 * slot + 4, :]
    if slot == 0:
        return
    rows_out[...] = rows[...].astype(LOW)
    for k in range(4):
        start = pl.multiple_of((rank ^ k) * QUARTER, 32)
        block = grad_att[pl.ds(start, QUARTER), :]
        low_part = (block[:, :D], block[:, D : 2 * D])
        high_part = (block[:, 2 * D :], grad_proj[pl.ds(start, QUARTER), :])
        turned = (0, 2, 1, 3)[k]

        @pl.when(core == 0)
        def _():
            for j in range(2):
                keep_out[turned, j * QUARTER : (j + 1) * QUARTER, :] = low_part[j]
                send_out[k, j * QUARTER : (j + 1) * QUARTER, :] = high_part[j]

        @pl.when(core != 0)
        def _():
            for j in range(2):
                keep_out[k, j * QUARTER : (j + 1) * QUARTER, :] = high_part[j]
                send_out[turned, j * QUARTER : (j + 1) * QUARTER, :] = low_part[j]


def half_of(where, which):
    return (where[2] >> (where[1] ^ which)) & 1


def rows_at(index, count):
    return pl.ds(pl.multiple_of(index * count, 32), count)


def step1_kernel(
    where, att_keep, att_in, feed_keep, feed_in, small, small_in,
    att_stay, att_go, feed_stay, feed_go, small_out, total,
):
    half = half_of(where, 0)
    count = D // 2
    att_stay[...] = att_keep[0] + att_in[0].astype(WIDE)
    att_go[...] = (att_keep[1] + att_in[1].astype(WIDE)).astype(LOW)
    total[...] = feed_keep[...] + feed_in[...].astype(WIDE)
    feed_stay[...] = total[rows_at(half, count), :]
    feed_go[...] = total[rows_at(1 - half, count), :].astype(LOW)
    small_out[0:SMALL, :] = small[...]
    small_out[SMALL:, :] = small_in[...]


def step2_kernel(
    where, att_keep, att_in, feed_keep, feed_in, small, small_in, att_stay, message, small_out, total
):
    half = half_of(where, 1)
    count = D // 2
    total[...] = att_keep[...] + att_in[...].astype(WIDE)
    att_stay[...] = total[rows_at(half, QUARTER), :]
    message[0:count, :] = (feed_keep[...] + feed_in[...].astype(WIDE)).astype(LOW)
    message[count:, :] = total[rows_at(1 - half, QUARTER), :].astype(LOW)
    small_out[0 : 2 * SMALL, :] = small[...]
    small_out[2 * SMALL :, :] = small_in[...]


def step3_kernel(where, att_keep, own, arrived, small, small_in, message, small_out):
    count = D // 2
    message[0:count, :] = (
        own[0:count, :].astype(WIDE) + arrived[0:count, :].astype(WIDE)
    ).astype(LOW)
    message[count:, :] = (att_keep[...] + arrived[count:, :].astype(WIDE)).astype(LOW)
    small_out[0 : 4 * SMALL, :] = small[...]
    small_out[4 * SMALL :, :] = small_in[...]


def step4_kernel(
    where, own, arrived, small, small_in, weight, att_sum, feed_part, small_out, cond_keep, cond_go
):
    half = half_of(where, 0)
    count = D // 2
    feed_part[rows_at(half, count), :] = own[0:count, :]
    feed_part[rows_at(1 - half, count), :] = arrived[0:count, :]
    att_sum[...] = (own[count:, :].astype(WIDE) + arrived[count:, :].astype(WIDE)).astype(LOW)
    small_out[0 : 8 * SMALL, :] = small[...]
    small_out[8 * SMALL :, :] = small_in[...]
    rows = [
        block[start : start + SMALL, :].astype(WIDE)
        for block in (small, small_in)
        for start in (0, 4 * SMALL)
    ]
    total = None
    for j in range(6):
        lines = [row[6 * slot + j : 6 * slot + j + 1] for row in rows for slot in range(2)]
        term = dot_last(
            jnp.concatenate(lines, axis=0).astype(LOW), weight[:, j * D : (j + 1) * D]
        )
        total = term if total is None else total + term
    padded = jnp.concatenate([total, jnp.zeros((8, 128 - QUARTER), WIDE)], axis=1)
    blank = jnp.zeros((4, 128), WIDE)
    cond_keep[...] = jnp.concatenate([padded[0:4], blank], axis=0)
    cond_go[...] = jnp.concatenate([padded[4:8], blank], axis=0)


def step5_kernel(where, att_sum, att_in, cond_keep, cond_in, _, att_part, cond_go):
    half = half_of(where, 1)
    att_part[rows_at(half, QUARTER), :] = att_sum[...]
    att_part[rows_at(1 - half, QUARTER), :] = att_in[...]
    blank = jnp.zeros((4, 128), WIDE)
    cond_go[...] = jnp.concatenate([cond_keep[2:4], cond_in[2:4], blank], axis=0)


def modulation_update_kernel(
    where, near, far, weight, mean, square, bias, bias_mean, bias_square,
    weight_out, mean_out, square_out, bias_out, bias_mean_out, bias_square_out, mark, everyone,
):
    rank, core, plane = where[0], where[1], where[2]
    for side, source in enumerate((near, far)):
        here = core ^ side
        first, second = 1 + here, 2 - here
        for index in range(16):
            a, b, c, d = (index & 1, (index >> 1) & 1, (index >> 2) & 1, index >> 3)
            z_at = plane ^ (a * first) ^ (b * second)
            g_at = rank ^ (c * second) ^ (d * first)
            place = (g_at * 4 + z_at) * 2 + here
            block = source[index * SMALL : (index + 1) * SMALL, :].astype(WIDE)
            for third in range(3):
                everyone[third, rows_at(place, SMALL), :] = block[
                    :, third * 128 : (third + 1) * 128
                ]

    def line(at):
        parts = [everyone[third, pl.ds(at, 32, stride=SMALL), :] for third in range(3)]
        return jnp.concatenate(parts, axis=1)

    def both(at, other):
        return jnp.concatenate([line(at), line(other)], axis=0)

    def own_lanes(values):
        chosen = values[:, :QUARTER]
        for place in range(1, 4):
            lanes = slice(place * QUARTER, (place + 1) * QUARTER)
            chosen = jnp.where(rank == place, values[:, lanes], chosen)
        return chosen

    cond = own_lanes(both(12, 13)).astype(LOW)
    sums = []
    for j in range(6):
        lanes = slice(j * D, (j + 1) * D)
        grads = both(j, 6 + j)
        sums.append(column_sum(grads))
        gradient = dot_first(cond, grads.astype(LOW))
        updated, momentum, variance = adam_update(
            weight[:, lanes].astype(WIDE),
            gradient,
            mean[:, lanes].astype(WIDE),
            square[:, lanes].astype(WIDE),
            LEARN_RATES[0],
            DECAY_FLAGS[0],
        )
        weight_out[:, lanes] = updated
        mean_out[:, lanes] = momentum
        square_out[:, lanes] = variance
    for at in range(14, 22):
        sums.append(column_sum(line(at)))
    gradient = own_lanes(jnp.concatenate(sums, axis=0))
    updated, momentum, variance = adam_update(
        bias[...].astype(WIDE),
        gradient,
        bias_mean[...].astype(WIDE),
        bias_square[...].astype(WIDE),
        LEARN_RATES[5],
        DECAY_FLAGS[5],
    )
    bias_out[...] = updated
    bias_mean_out[...] = momentum
    bias_square_out[...] = variance
    mark[...] = jnp.zeros_like(mark)


def split_kernel(keep, arrived, stay, go):
    half = stay.shape[0]
    stay[...] = keep[:half].astype(WIDE) + arrived[:half].astype(WIDE)
    go[...] = (keep[half:].astype(WIDE) + arrived[half:].astype(WIDE)).astype(LOW)


def whole(shape):
    return pl.BlockSpec(shape, lambda *grid: (0,) * len(shape))


def by_slot(shape):
    return pl.BlockSpec((1,) + shape, lambda s: (s,) + (0,) * len(shape))


def shape_of(shape, dtype):
    return jax.ShapeDtypeStruct(shape, dtype)


SMEM_SPEC = pl.BlockSpec(memory_space=pltpu.SMEM)
PARAMS = pltpu.CompilerParams(vmem_limit_bytes=VMEM_BYTES)


ANY_SPEC = pl.BlockSpec(memory_space=pl.ANY)


def small_call(kernel, name, outs, where, *operands, scratch=(), after=(), params=PARAMS):
    return pl.pallas_call(
        kernel,
        grid=(1,),
        in_specs=[SMEM_SPEC]
        + [whole(item.shape) for item in operands]
        + [ANY_SPEC] * len(after),
        out_specs=[whole(shape) for shape, _ in outs],
        out_shape=[shape_of(*item) for item in outs],
        scratch_shapes=[pltpu.VMEM(*item) for item in scratch],
        compiler_params=params,
        name=name,
    )(where, *operands, *after)


def run_gate(value, *after, space=ANY_SPEC):
    return pl.pallas_call(
        gate_kernel,
        in_specs=[space] + [ANY_SPEC] * len(after),
        out_specs=space,
        out_shape=shape_of(value.shape, value.dtype),
        input_output_aliases={0: 0},
        compiler_params=pltpu.CompilerParams(vmem_limit_bytes=1024 * 1024),
        name="in_order",
    )(value, *after)


def run_relay(where, keep, arrived, passing):
    two = (2, keep.shape[1])
    return pl.pallas_call(
        relay_kernel,
        grid=(1,),
        in_specs=[SMEM_SPEC, whole(keep.shape), whole(arrived.shape), ANY_SPEC],
        out_specs=[whole(two), whole(two), ANY_SPEC],
        out_shape=[shape_of(two, WIDE)] * 2 + [shape_of(passing.shape, passing.dtype)],
        input_output_aliases={3: 2},
        compiler_params=PARAMS,
        name="relay",
    )(where, keep, arrived, passing)


def run_modulation(where, condition, biases, blocks, weight):
    message = pl.BlockSpec((16, D), lambda s: (2 * QUARTER // 16, 0))
    return pl.pallas_call(
        modulation_kernel,
        grid=(1,),
        in_specs=[SMEM_SPEC, whole((2, D)), whole((BIAS_ROWS, QUARTER))]
        + [message] * 3
        + [whole((QUARTER, 6 * D))],
        out_specs=[whole((4, 6 * D))] * 2 + [whole((16, D))],
        out_shape=[shape_of((4, 6 * D), WIDE)] * 2 + [shape_of((16, D), WIDE)],
        compiler_params=PARAMS,
        cost_estimate=pl.CostEstimate(flops=10**7, bytes_accessed=10**6, transcendentals=0),
        name="modulation_partials",
    )(where, condition, biases, *blocks, weight)


def run_attention_forward(where, tokens, stay, arrived, bias, own_att, own_proj, nears, fars):
    part = whole((2 * QUARTER + 16, D))
    return pl.pallas_call(
        attention_forward_kernel,
        grid=(2,),
        in_specs=[
            SMEM_SPEC,
            by_slot((SEQ, D)),
            whole((2, 6 * D)),
            whole((2, 6 * D)),
            whole((16, D)),
            whole((QUARTER, 3 * D)),
            whole((QUARTER, D)),
        ]
        + [part] * 6,
        out_specs=[
            by_slot((SEQ, 3 * D)),
            by_slot((HEADS, SEQ, SEQ)),
            by_slot((SEQ, D)),
            by_slot((6, D)),
            whole((D, 3 * D)),
            whole((D, D)),
        ],
        out_shape=[
            shape_of((2, SEQ, 3 * D), LOW),
            shape_of((2, HEADS, SEQ, SEQ), LOW),
            shape_of((2, SEQ, D), LOW),
            shape_of((2, 6, D), WIDE),
            shape_of((D, 3 * D), LOW),
            shape_of((D, D), LOW),
        ],
        compiler_params=PARAMS,
        cost_estimate=pl.CostEstimate(
            flops=3 * 10**9, bytes_accessed=6 * 10**6, transcendentals=10**6
        ),
        name="attention_forward",
    )(where, tokens, stay, arrived, bias, own_att, own_proj, *nears, *fars)


def run_feed(where, mixed, tokens, cotangent, mod, bias, proj, own_expand, own_contract, nears, fars):
    rows = 2 * SEQ

    return pl.pallas_call(
        feed_kernel,
        grid=(2,),
        in_specs=[SMEM_SPEC]
        + [whole((2, SEQ, D))] * 3
        + [whole((2, 6, D)), whole((16, D))]
        + [whole((D, D))] * 9,
        out_specs=[
            whole((2, SEQ, D)),
            whole((2, SEQ, D)),
            pl.BlockSpec((2, D, D), lambda i: (i, 0, 0)),
            pl.BlockSpec((2, D, D), lambda i: (i, 0, 0)),
            whole((16, D)),
        ],
        scratch_shapes=[
            pltpu.VMEM((2, D, 2 * D), LOW),
            pltpu.VMEM((2, 2 * D, D), LOW),
            pltpu.VMEM((rows, D), WIDE),
            pltpu.VMEM((rows, D), WIDE),
            pltpu.VMEM((rows, D), LOW),
            pltpu.VMEM((rows, D), WIDE),
            pltpu.VMEM((rows, 128), WIDE),
            pltpu.VMEM((rows, D), LOW),
            pltpu.VMEM((rows, D), WIDE),
            pltpu.VMEM((rows, D), WIDE),
        ],
        out_shape=[
            shape_of((2, SEQ, D), LOW),
            shape_of((2, SEQ, D), WIDE),
            shape_of((4, D, D), LOW),
            shape_of((4, D, D), LOW),
            shape_of((16, D), WIDE),
        ],
        compiler_params=PARAMS,
        cost_estimate=pl.CostEstimate(
            flops=8 * 10**9, bytes_accessed=10**7, transcendentals=10**6
        ),
        name="feed_forward_and_back",
    )(where, mixed, tokens, cotangent, mod, bias, proj, own_expand, own_contract, *nears, *fars)


def run_attention_backward(
    slot, where, tokens, grad_middle, joined, soft, mixed, mod, feed_rows, cond, att, proj, earlier=()
):
    def at_slot(shape):
        return pl.BlockSpec((1,) + shape, lambda i: (slot,) + (0,) * len(shape))

    passed = [((SEQ, 3 * D), LOW), ((SEQ, D), LOW), ((SEQ, D), LOW), ((SMALL, D), WIDE)]
    in_specs = [
        SMEM_SPEC,
        at_slot((SEQ, D)),
        at_slot((SEQ, D)),
        at_slot((SEQ, 3 * D)),
        at_slot((HEADS, SEQ, SEQ)),
        whole((2, SEQ, D)),
        at_slot((6, D)),
        whole((16, D)),
        whole((2, D)),
        whole((D, 3 * D)),
        whole((D, D)),
    ]
    out_specs = [at_slot((SEQ, D))]
    out_shape = [shape_of((2, SEQ, D), LOW)]
    scratch = []
    aliases = {}
    if slot == 0:
        out_specs += [whole(shape) for shape, _ in passed]
        out_shape += [shape_of(*item) for item in passed]
    else:
        in_specs += [whole(shape) for shape, _ in passed] + [ANY_SPEC, ANY_SPEC]
        aliases = {15: 0}
        out_specs += [whole((4, 2 * QUARTER, D))] * 2 + [whole((SMALL, D))]
        out_shape += [shape_of((4, 2 * QUARTER, D), LOW)] * 2 + [shape_of((SMALL, D), LOW)]
        sums = [((D, 3 * D), LOW), ((D, D), LOW)]
        scratch = [pltpu.VMEM(*item) for item in (passed[0], *sums, passed[3])]
    return pl.pallas_call(
        functools.partial(attention_backward_kernel, slot),
        grid=(1,),
        in_specs=in_specs,
        out_specs=out_specs,
        out_shape=out_shape,
        scratch_shapes=scratch,
        input_output_aliases=aliases,
        compiler_params=PARAMS,
        cost_estimate=pl.CostEstimate(
            flops=4 * 10**9, bytes_accessed=8 * 10**6, transcendentals=0
        ),
        name="attention_backward",
    )(where, tokens, grad_middle, joined, soft, mixed, mod, feed_rows, cond, att, proj, *earlier)


def turn_split_kernel(where, keep, arrived, stay, go):
    core = where[1]
    for place, block in enumerate((0, 2 - core)):
        stay[place] = keep[block].astype(WIDE) + arrived[block].astype(WIDE)
    for place, block in enumerate((1 + core, 3)):
        go[place] = (keep[block].astype(WIDE) + arrived[block].astype(WIDE)).astype(LOW)


def run_split(keep, arrived):
    count, rest = keep.shape[0], keep.shape[1:]
    half = (count // 2,) + rest
    return pl.pallas_call(
        split_kernel,
        grid=(1,),
        in_specs=[whole(keep.shape)] * 2,
        out_specs=[whole(half)] * 2,
        out_shape=[shape_of(half, WIDE), shape_of(half, LOW)],
        compiler_params=PARAMS,
        name="sum_and_split",
    )(keep, arrived)


def swap_plane(value, which):
    pairs = [(r, r ^ ((1 + ((r + which) & 1)) << 1)) for r in range(lax.axis_size("replica"))]
    return lax.ppermute(value, "replica", pairs)


def swap_pair(value, which):
    groups, copies = lax.axis_size("group"), lax.axis_size("replica")
    pairs = []
    for g in range(groups):
        for r in range(copies):
            other = g ^ (1 if (r + which) % 2 == 0 else 2)
            pairs.append((g * copies + r, other * copies + r))
    return lax.ppermute(value, ("group", "replica"), pairs)


def gather_pair(value):
    first = swap_pair(value, 0)
    second = swap_pair(value, 1)
    return (first, second, swap_pair(first, 1))


def update_all(stored, gradients, means, squares, kinds):
    return [
        adam_update(
            stored[kind].astype(jnp.float32),
            gradient,
            means[kind].astype(jnp.float32),
            squares[kind].astype(jnp.float32),
            LEARN_RATES[kind],
            DECAY_FLAGS[kind],
        )
        for kind, gradient in zip(kinds, gradients)
    ]


def by_core(core, own, other):
    return (
        jnp.where(core == 0, own, other).astype(jnp.float32),
        jnp.where(core == 0, other, own).astype(jnp.float32),
    )


def attention_shards(totals):
    joined = jnp.concatenate(
        [totals[0][:QUARTER], totals[0][QUARTER:], totals[1][:QUARTER]], axis=1
    )
    return (joined, totals[1][QUARTER:])


def tail_in_step(
    where, copy, stages, condition, ffn_halves, att_parts, small_rows, stored, means, squares
):
    core = where[1]
    (feed_stay, feed_in), (att_send, att_keep) = ffn_halves, att_parts
    half, third, quarter = (D // 2, D), (2 * QUARTER, D), (QUARTER, D)
    att_stay, att_go = run_split(att_keep, swap_replica(att_send, 1))
    feed_stay, feed_go = run_split(feed_stay, feed_in)
    feed_stay, feed_go = feed_stay[0], feed_go[0]
    att_stay, att_go, feed_stay, feed_go, small = small_call(
        step1_kernel, "step_1",
        [(third, WIDE), (third, LOW), (half, WIDE), (half, LOW), ((2 * SMALL, D), LOW)],
        where, att_stay, swap_pair(att_go, 0), feed_stay, swap_pair(feed_go, 1),
        small_rows, swap_plane(small_rows, 0),
        scratch=[((D, D), WIDE)],
    )
    att_stay, message, small = small_call(
        step2_kernel, "step_2",
        [(quarter, WIDE), ((3 * QUARTER, D), LOW), ((4 * SMALL, D), LOW)],
        where, att_stay, swap_pair(att_go, 1), feed_stay, swap_plane(feed_go, 0),
        small, swap_plane(small, 1),
        scratch=[(third, WIDE)],
    )
    message, small = small_call(
        step3_kernel, "step_3",
        [((3 * QUARTER, D), LOW), ((8 * SMALL, D), LOW)],
        where, att_stay, message, swap_plane(message, 1), small, swap_pair(small, 1),
    )
    att_sum, feed_part, small, cond_keep, cond_go = small_call(
        step4_kernel, "step_4",
        [(quarter, LOW), ((D, D), LOW), ((16 * SMALL, D), LOW), ((8, 128), WIDE), ((8, 128), WIDE)],
        where, message, swap_plane(message, 0), small, swap_pair(small, 0), stored[0],
    )
    shard = [((QUARTER, 6 * D), WIDE)] * 3 + [((BIAS_ROWS, QUARTER), WIDE)] * 3
    *updates, mark = small_call(
        modulation_update_kernel, "modulation_update", shard + [((8, 128), WIDE)],
        where, small, swap_replica(small, 1), stored[0], means[0], squares[0],
        stored[5], means[5], squares[5],
        scratch=[((3, 32 * SMALL, 128), WIDE)],
    )
    feed_totals = by_core(core, feed_part, swap_replica(feed_part, 1))
    feed_updates = update_all(stored, feed_totals, means, squares, (3, 4))
    cond_in = swap_pair(cond_go, 0)
    att_part, cond_go = small_call(
        step5_kernel, "step_5",
        [(third, LOW), ((8, 128), WIDE)],
        where, att_sum, swap_plane(att_sum, 1), cond_keep, cond_in,
        after=(mark,),
    )
    cond_last = swap_pair(cond_go, 1)
    att_totals = by_core(core, att_part, swap_replica(att_part, 1))
    blocks = [
        block[:, :QUARTER] for block in (cond_keep[:2], cond_in[:2], cond_last[:2], cond_last[2:4])
    ]
    owners = (where[0],) + neighbours(where)
    lanes = []
    for place in range(4):
        chosen = blocks[0]
        for k in range(1, 4):
            chosen = jnp.where(owners[k] == place, blocks[k], chosen)
        lanes.append(chosen)
    sigmoid_cond = jax.nn.sigmoid(condition)
    grad_condition = (
        jnp.concatenate(lanes, axis=1) * sigmoid_cond * (1.0 + condition * (1.0 - sigmoid_cond))
    )
    att_updates = update_all(stored, attention_shards(att_totals), means, squares, (1, 2))
    return grad_condition, [updates[:3]] + att_updates + feed_updates + [updates[3:]]


def tail_in_turn(
    where, copy, stages, condition, ffn_halves, att_parts, small_rows, stored, means, squares
):
    rank, core = where[0], where[1]
    slot_count, model_width = condition.shape
    modulation, cond_low = stored[0], jax.nn.silu(condition).astype(jnp.bfloat16)
    (ffn_stay, ffn_in), (att_send, att_keep) = ffn_halves, att_parts
    ffn_stay, ffn_go = run_split(ffn_stay, ffn_in)
    ffn_totals = reduce_replicas(
        wide_sum([ffn_stay[0], swap_pair(ffn_go[0], 1)]).astype(LOW), copy, stages
    )
    att_stay, att_go = run_split(att_keep, swap_replica(att_send, 1))
    att_stay, att_go = run_split(att_stay, swap_pair(att_go, 0))
    att_totals = reduce_replicas(
        wide_sum([att_stay[0], swap_pair(att_go[0], 1)]).astype(LOW), copy, stages
    )
    row_total = small_rows.shape[0]
    gathered = small_rows[None]
    for low_bit, radix in stages[1:]:
        digit = (copy >> low_bit) % radix
        gathered = in_order(
            [swap_replica(gathered, k << low_bit) for k in range(radix)], digit
        ).reshape(-1, row_total, model_width)
    gathered = in_order([swap_group(gathered, k) for k in range(4)], rank)
    own_plane = lax.dynamic_index_in_dim(gathered, copy >> 1, axis=1, keepdims=False)
    group_mod = own_plane[:, : 6 * slot_count].reshape(4 * slot_count, 6 * model_width)
    grad_cond_columns = dot_last(group_mod, modulation).reshape(4, slot_count, model_width // 4)
    cond_back = in_order(
        [swap_group(pick(grad_cond_columns, rank ^ k), k) for k in range(4)], rank
    )
    sigmoid_cond = jax.nn.sigmoid(condition)
    grad_condition = (
        jnp.swapaxes(cond_back, 0, 1).reshape(slot_count, model_width)
        * sigmoid_cond
        * (1.0 + condition * (1.0 - sigmoid_cond))
    )
    everyone = in_order([swap_replica(gathered, k) for k in range(2)], core).reshape(
        -1, row_total, model_width
    )
    all_mod = everyone[:, : 6 * slot_count].reshape(-1, 6 * model_width)
    all_cond = everyone[:, 6 * slot_count : 7 * slot_count].reshape(-1, model_width)
    cond_own = lax.dynamic_slice_in_dim(all_cond, rank * (model_width // 4), model_width // 4, 1)
    grad_mod = dot_first(cond_own, all_mod)
    mod_bias_grad = jnp.sum(all_mod, axis=0, dtype=jnp.float32).reshape(6, model_width)
    rest_bias_grad = jnp.sum(everyone[:, 7 * slot_count : 22], axis=0, dtype=jnp.float32)
    bias_grad = lax.dynamic_slice_in_dim(
        jnp.concatenate([mod_bias_grad, rest_bias_grad], axis=0),
        rank * (model_width // 4),
        model_width // 4,
        1,
    )
    grad_att_own = jnp.concatenate(
        [att_totals[0][:QUARTER], att_totals[0][QUARTER:], att_totals[1][:QUARTER]], axis=1
    )
    totals = (
        grad_mod,
        grad_att_own,
        att_totals[1][QUARTER:],
        ffn_totals[0],
        ffn_totals[1],
        bias_grad,
    )
    return grad_condition, update_all(stored, totals, means, squares, range(6))


def shards(
    latents,
    condition,
    cotangent,
    live_counts,
    modulation,
    attending,
    projection,
    expand,
    contract,
    biases,
    modulation_mean,
    attending_mean,
    projection_mean,
    expand_mean,
    contract_mean,
    biases_mean,
    modulation_square,
    attending_square,
    projection_square,
    expand_square,
    contract_square,
    biases_square,
):
    slot_count, length, model_width = latents.shape
    rank = lax.axis_index("group")
    copy = lax.axis_index("replica")
    core = copy % 2
    stages = replica_stages(lax.axis_size("replica"))
    where = jnp.stack([rank, core, copy >> 1, live_counts[0]]).astype(jnp.int32)

    cond_low = jax.nn.silu(condition).astype(LOW)
    payload, feed_part = small_call(
        payload_kernel, "own_payload",
        [((2 * QUARTER + 16, model_width), LOW), ((model_width, model_width), LOW)],
        where, condition, attending, projection, biases, expand, contract,
        params=pltpu.CompilerParams(vmem_limit_bytes=60 * 1024 * 1024),
    )
    first, second = swap_pair(payload, 0), swap_pair(payload, 1)
    last, first_far = swap_pair(first, 1), swap_replica(first, 1)
    feed_part = run_gate(
        feed_part, first_far, second, space=pl.BlockSpec(memory_space=pltpu.HBM)
    )
    nears = (first, second, last)
    fars = [first_far, swap_replica(second, 1), swap_replica(last, 1)]
    feed_first, feed_second = swap_pair(feed_part, 0), swap_pair(feed_part, 1)
    stay, go, bias = run_modulation(where, condition, biases, nears, modulation)
    stay, go, feed_first = run_relay(where, stay, swap_pair(go, 0), feed_first)
    arrived = swap_pair(go, 1)
    feed_last = swap_pair(feed_first, 1)
    joined, soft, mixed, mod, att, proj = run_attention_forward(
        where, latents, stay, arrived, bias, attending, projection, nears, fars
    )
    feed_nears = (feed_first, feed_second, run_gate(feed_last, mod))
    feed_fars = [swap_replica(item, 1) for item in feed_nears]
    out_latents, grad_middle, ffn_send, ffn_keep, feed_rows = run_feed(
        where, mixed, latents, cotangent, mod, bias, proj, expand, contract, feed_nears, feed_fars
    )
    cond_wide = cond_low.astype(WIDE)
    two_blocks = (2, model_width, model_width)
    ffn_stay, ffn_go = small_call(
        turn_split_kernel, "sum_and_split", [(two_blocks, WIDE), (two_blocks, LOW)],
        where, ffn_keep, swap_replica(ffn_send, 1),
    )
    earlier = run_attention_backward(
        0, where, latents, grad_middle, joined, soft, mixed, mod, feed_rows, cond_wide, att, proj
    )
    ffn_in = swap_pair(ffn_go, 0)
    grad_latents, att_send, att_keep, small_rows = run_attention_backward(
        1, where, latents, grad_middle, joined, soft, mixed, mod, feed_rows, cond_wide, att, proj,
        (*earlier[1:], earlier[0], ffn_go),
    )
    tail = tail_in_step if lax.axis_size("replica") == 8 else tail_in_turn
    grad_condition, results = tail(
        where, copy, stages, condition, (ffn_stay, ffn_in), (att_send, att_keep), small_rows,
        (modulation, attending, projection, expand, contract, biases),
        (
            modulation_mean, attending_mean, projection_mean,
            expand_mean, contract_mean, biases_mean,
        ),
        (
            modulation_square, attending_square, projection_square,
            expand_square, contract_square, biases_square,
        ),
    )
    return (
        out_latents,
        grad_latents,
        grad_condition,
        results[0][0],
        results[1][0],
        results[2][0],
        results[3][0],
        results[4][0],
        results[5][0],
        results[0][1],
        results[1][1],
        results[2][1],
        results[3][1],
        results[4][1],
        results[5][1],
        results[0][2],
        results[1][2],
        results[2][2],
        results[3][2],
        results[4][2],
        results[5][2],
    )


def solution(mesh):
    return jax.shard_map(
        shards,
        mesh=mesh,
        in_specs=(
            P(("group", "replica"), None, None),
            P(("group", "replica"), None),
            P(("group", "replica"), None, None),
            P(("group", "replica")),
            P("group", None),
            P("group", None),
            P("group", None),
            P(None, "group"),
            P("group", None),
            P(None, "group"),
            P("group", None),
            P("group", None),
            P("group", None),
            P(None, "group"),
            P("group", None),
            P(None, "group"),
            P("group", None),
            P("group", None),
            P("group", None),
            P(None, "group"),
            P("group", None),
            P(None, "group"),
        ),
        out_specs=(
            P(("group", "replica"), None, None),
            P(("group", "replica"), None, None),
            P(("group", "replica"), None),
            P("group", None),
            P("group", None),
            P("group", None),
            P(None, "group"),
            P("group", None),
            P(None, "group"),
            P("group", None),
            P("group", None),
            P("group", None),
            P(None, "group"),
            P("group", None),
            P(None, "group"),
            P("group", None),
            P("group", None),
            P("group", None),
            P(None, "group"),
            P("group", None),
            P(None, "group"),
        ),
        check_vma=False,
    )
```

```python
import functools

import jax
import jax.numpy as jnp
from jax import lax
from jax.experimental import pallas as pl
from jax.experimental.pallas import tpu as pltpu
from jax.sharding import PartitionSpec as P

HEADS = 6
HEAD_DIM = 64
FF = 1536
STEP = 10


NORM_EPS = 1e-06
ADAM_EPS = 1e-08
BETA_FIRST = 0.9
BETA_SECOND = 0.999
DECAY_RATE = 0.1
LEARN_RATES = (0.05, 0.05, 0.2, 0.05, 0.025, 0.1)
DECAY_FLAGS = (1.0, 1.0, 1.0, 1.0, 1.0, 0.0)
GELU_COEF = 0.7978845608028654
BIAS_ROWS = 14
D = 384
SEQ = 256
QUARTER = D // 4
VMEM_BYTES = 48 * 1024 * 1024
LOW = jnp.bfloat16
SMALL = 32
BLOCK = 16
WIDE = jnp.float32


def dot_plain(left_side, right_side):
    return jnp.dot(left_side, right_side, preferred_element_type=WIDE)


def dot_first(left_side, right_side):
    return lax.dot_general(
        left_side, right_side, (((0,), (0,)), ((), ())), preferred_element_type=WIDE
    )


def dot_last(left_side, right_side):
    return lax.dot_general(
        left_side, right_side, (((1,), (1,)), ((), ())), preferred_element_type=WIDE
    )


def adam_update(weight, gradient, mean_old, square_old, step_rate, decay_flag):
    momentum = BETA_FIRST * mean_old + (1.0 - BETA_FIRST) * gradient
    variance = BETA_SECOND * square_old + ((1.0 - BETA_SECOND) * gradient) * gradient
    root = variance * lax.rsqrt(variance)
    bottom = root * (1.0 - BETA_SECOND**STEP) ** (-0.5) + ADAM_EPS
    change = momentum * (step_rate / (1.0 - BETA_FIRST**STEP)) / bottom
    updated = weight * (1.0 - step_rate * decay_flag * DECAY_RATE) - change
    return (updated, momentum, variance)


def replica_stages(count):
    stages, low_bit = [(0, 2)], 1
    while (1 << low_bit) < count:
        radix = min(4, count >> low_bit)
        stages.append((low_bit, radix))
        low_bit += radix.bit_length() - 1
    return stages


def swap_group(value, k):
    if k == 0:
        return value
    return lax.ppermute(value, "group", [(i, i ^ k) for i in range(lax.axis_size("group"))])


def swap_replica(value, k):
    if k == 0:
        return value
    return lax.ppermute(value, "replica", [(i, i ^ k) for i in range(lax.axis_size("replica"))])


def pick(blocks, index):
    return lax.dynamic_index_in_dim(blocks, index, axis=0, keepdims=False)


def in_order(blocks, digit):
    ordered = []
    for place in range(len(blocks)):
        chosen = blocks[0]
        for k in range(1, len(blocks)):
            chosen = jnp.where((digit ^ k) == place, blocks[k], chosen)
        ordered.append(chosen)
    return jnp.stack(ordered)


def wide_sum(blocks):
    total = blocks[0].astype(jnp.float32)
    for block in blocks[1:]:
        total = total + block.astype(jnp.float32)
    return total


def scatter_stage(value, digit, low_bit, radix):
    rows = value.shape[-2] // radix
    parts = [
        lax.dynamic_slice_in_dim(value, (digit ^ k) * rows, rows, value.ndim - 2)
        for k in range(radix)
    ]
    received = [swap_replica(parts[k], k << low_bit) for k in range(radix)]
    return wide_sum(received).astype(jnp.bfloat16)


def reduce_replicas(value, copy, stages):
    core = copy % 2
    for low_bit, radix in stages[1:]:
        value = scatter_stage(value, (copy >> low_bit) % radix, low_bit, radix)
    for low_bit, radix in reversed(stages[1:]):
        blocks = [swap_replica(value, k << low_bit) for k in range(radix)]
        value = in_order(blocks, (copy >> low_bit) % radix)
        value = value.reshape(-1, value.shape[-1])
    other = swap_replica(value, 1)
    return (
        jnp.where(core == 0, value, other).astype(jnp.float32),
        jnp.where(core == 0, other, value).astype(jnp.float32),
    )


def layer_norm_parts(values):
    centred = values - jnp.mean(values, axis=-1, keepdims=True)
    inverse = lax.rsqrt(jnp.mean(centred * centred, axis=-1, keepdims=True) + NORM_EPS)
    return (centred * inverse, inverse)


def norm_backward(grad_normed, normed, inverse):
    mean_grad = jnp.mean(grad_normed, axis=-1, keepdims=True)
    mean_cross = jnp.mean(grad_normed * normed, axis=-1, keepdims=True)
    return inverse * (grad_normed - mean_grad - normed * mean_cross)


def column_sum(values):
    return jnp.sum(values, axis=0, keepdims=True)


def head_mask(shape, which):
    lane = lax.broadcasted_iota(jnp.int32, shape, 1)
    return (lane < HEAD_DIM) if which == 0 else (lane >= HEAD_DIM)


def place_rows(target, lanes, block, owner):
    start = pl.multiple_of(owner * QUARTER, 32)
    target[pl.ds(start, QUARTER), lanes] = block


def neighbours(where):
    rank, core = where[0], where[1]
    return (rank ^ (1 + core), rank ^ (2 - core), rank ^ 3)


def own_message(condition, biases):
    cond = condition[...]
    active = cond / (1.0 + jnp.exp(-cond))
    padded = jnp.concatenate(
        [biases[...].astype(WIDE), jnp.zeros((BIAS_ROWS, D - QUARTER), WIDE)], axis=1
    )
    return jnp.concatenate([active, padded], axis=0)


def payload_kernel(where, condition, attending, projection, biases, expand, contract, out, part):
    @pl.when(where[1] == 0)
    def _():
        part[...] = expand[...]
        out[0:QUARTER, :] = attending[:, 0:D]
        out[QUARTER : 2 * QUARTER, :] = attending[:, D : 2 * D]

    @pl.when(where[1] != 0)
    def _():
        part[...] = contract[...]
        out[0:QUARTER, :] = attending[:, 2 * D : 3 * D]
        out[QUARTER : 2 * QUARTER, :] = projection[...]

    out[2 * QUARTER :, :] = own_message(condition, biases).astype(LOW)


def modulation_kernel(
    where, condition, biases, first, second, last, weight, stay, go, bias_out
):
    rank = where[0]
    owners = (rank,) + neighbours(where)
    rows = [own_message(condition, biases)]
    rows += [block[...].astype(WIDE) for block in (first, second, last)]
    conds = jnp.concatenate([rows[0][0:2], rows[2][0:2], rows[1][0:2], rows[3][0:2]], axis=0)
    columns = conds[:, :QUARTER]
    for place in range(1, 4):
        lanes = slice(place * QUARTER, (place + 1) * QUARTER)
        columns = jnp.where(rank == place, conds[:, lanes], columns)
    partial = dot_plain(columns.astype(LOW), weight[...])
    stay[...] = partial[:4]
    go[...] = partial[4:]
    lanes = []
    for place in range(4):
        chosen = rows[0][:, :QUARTER]
        for k in range(1, 4):
            chosen = jnp.where(owners[k] == place, rows[k][:, :QUARTER], chosen)
        lanes.append(chosen)
    bias_out[...] = jnp.concatenate(lanes, axis=1)


def relay_kernel(where, keep, arrived, _, stay, go, __):
    stay[...] = keep[0:2, :] + arrived[0:2, :]
    go[...] = keep[2:4, :] + arrived[2:4, :]


def gate_kernel(*refs):
    pass


def attention_forward_kernel(
    where, tokens, stay, arrived, bias, own_att, own_proj, n1, n2, n3, f1, f2, f3,
    joined_out, soft_out, mixed_out, mod_out, att, proj,
):
    slot = pl.program_id(0)
    rank = where[0]

    core = where[1]

    def assemble(lows, highs):
        for k, block in zip((1, 2, 3), lows):
            place_rows(att, slice(0, D), block[0:QUARTER, :], rank ^ k)
            place_rows(att, slice(D, 2 * D), block[QUARTER : 2 * QUARTER, :], rank ^ k)
        for k, block in zip((2, 1, 3), highs):
            place_rows(att, slice(2 * D, 3 * D), block[0:QUARTER, :], rank ^ k)
            place_rows(proj, slice(0, D), block[QUARTER : 2 * QUARTER, :], rank ^ k)

    @pl.when(slot == 0)
    def _():
        place_rows(att, slice(0, 3 * D), own_att[...], rank)
        place_rows(proj, slice(0, D), own_proj[...], rank)

        @pl.when(core == 0)
        def _():
            assemble((n1, n2, n3), (f1, f2, f3))

        @pl.when(core != 0)
        def _():
            assemble((f1, f2, f3), (n1, n2, n3))

    summed = stay[...] + arrived[...]
    row = jnp.where(slot == 0, summed[0:1], summed[1:2])
    pieces = [row[:, j * D : (j + 1) * D] + bias[2 + j : 3 + j, :] for j in range(6)]
    mod_out[0] = jnp.concatenate(pieces, axis=0)
    normed, _ = layer_norm_parts(tokens[0].astype(WIDE))
    first_in = (normed * (1.0 + pieces[1]) + pieces[0]).astype(LOW)
    thirds = []
    for third in range(3):
        part = dot_plain(first_in, att[:, third * D : (third + 1) * D])
        if third == 0:
            part = part + bias[8:9, :]
        if third == 2:
            part = part + bias[9:10, :]
        part = part.astype(LOW)
        joined_out[0, :, third * D : (third + 1) * D] = part
        thirds.append(part)
    first_half = head_mask((SEQ, 128), 0)
    scale = jnp.asarray(HEAD_DIM ** (-0.5), LOW)
    zero = jnp.zeros((SEQ, 128), LOW)
    for pair in range(HEADS // 2):
        lanes = slice(pair * 128, (pair + 1) * 128)
        query, key, value = (part[:, lanes] for part in thirds)
        query = query * scale
        outs = []
        for half in range(2):
            masked = (
                jnp.where(first_half, query, zero)
                if half == 0
                else jnp.where(first_half, zero, query)
            )
            scores = dot_last(masked, key)
            weights = jnp.exp(scores - jnp.max(scores, axis=-1, keepdims=True))
            total = jnp.sum(weights, axis=-1, keepdims=True)
            soft = (weights * (1.0 / total)).astype(LOW)
            soft_out[0, 2 * pair + half] = soft
            outs.append(dot_plain(soft, value))
        mixed_out[0, :, lanes] = jnp.where(first_half, outs[0], outs[1]).astype(LOW)


def feed_kernel(
    where, mixed, tokens, cotangent, mod, bias, proj, own_expand, own_contract, n1, n2, n3, f1, f2, f3,
    out, grad_middle_out, send_out, keep_out, rows_out,
    expands, contracts, branch, middle, second, normed, inverse, grad_feed, feed, grad_second,
):
    step = pl.program_id(0)
    rank, core, live = where[0], where[1], where[3]

    def assemble(lows, highs):
        for k, block in zip((1, 2, 3), lows):
            expands[k // 2, :, (k % 2) * D : (k % 2 + 1) * D] = block[...]
        for k, block in zip((2, 1, 3), highs):
            contracts[k // 2, (k % 2) * D : (k % 2 + 1) * D, :] = block[...]

    slots = [slice(s * SEQ, (s + 1) * SEQ) for s in range(2)]

    @pl.when(step == 0)
    def _():
        expands[0, :, 0:D] = own_expand[...]
        contracts[0, 0:D, :] = own_contract[...]

        @pl.when(core == 0)
        def _():
            assemble((n1, n2, n3), (f1, f2, f3))

        @pl.when(core != 0)
        def _():
            assemble((f1, f2, f3), (n1, n2, n3))

        for s, rows in enumerate(slots):
            pieces = mod[s]
            value = dot_plain(mixed[s], proj[...]) + bias[10:11, :]
            branch[rows, :] = value
            centre = tokens[s].astype(WIDE) + pieces[2:3] * value
            middle[rows, :] = centre
            unit, spread = layer_norm_parts(centre)
            normed[rows, :] = unit
            inverse[rows, :] = jnp.broadcast_to(spread, (SEQ, 128))
            second[rows, :] = (unit * (1.0 + pieces[4:5]) + pieces[3:4]).astype(LOW)
            alive = jnp.where(s < live, 1.0, 0.0)
            grad_feed[rows, :] = (
                pieces[5:6] * (cotangent[s].astype(WIDE) * alive)
            ).astype(LOW)
        rows_out[...] = jnp.zeros_like(rows_out)
        rows_out[12:13, :] = column_sum(grad_feed[...].astype(WIDE))

    owners = (rank ^ (2 * step), rank ^ (2 * step + 1))
    hidden_bias = jnp.concatenate([bias[pl.ds(11 + owner, 1), :] for owner in owners], axis=1)
    expand, contract = expands[step], contracts[step]
    before = dot_plain(second[...], expand) + hidden_bias
    square = before * before
    tangent = jnp.tanh(before * (GELU_COEF + (GELU_COEF * 0.044715) * square))
    half_up = 0.5 + 0.5 * tangent
    activated = (before * half_up).astype(LOW)
    slope = half_up + (0.5 * before) * (1.0 - tangent * tangent) * (
        GELU_COEF + (GELU_COEF * 3.0 * 0.044715) * square
    )
    grad_before_wide = dot_last(grad_feed[...], contract) * slope
    grad_before = grad_before_wide.astype(LOW)
    feed_term = dot_plain(activated, contract)
    second_term = dot_last(grad_before, expand)
    grad_expand = dot_first(second[...], grad_before).astype(LOW)
    grad_contract = dot_first(activated, grad_feed[...]).astype(LOW)
    sums = column_sum(grad_before.astype(WIDE))
    for k, owner in enumerate(owners):
        rows_out[pl.ds(8 + owner, 1), :] = sums[:, k * D : (k + 1) * D]

    @pl.when(core == 0)
    def _():
        for k in range(2):
            send_out[k] = grad_contract[k * D : (k + 1) * D, :]
            keep_out[k] = grad_expand[:, k * D : (k + 1) * D]

    @pl.when(core != 0)
    def _():
        for k in range(2):
            send_out[k] = grad_expand[:, k * D : (k + 1) * D]
            keep_out[k] = grad_contract[k * D : (k + 1) * D, :]

    @pl.when(step == 0)
    def _():
        feed[...] = feed_term
        grad_second[...] = second_term

    @pl.when(step > 0)
    def _():
        feed[...] += feed_term
        grad_second[...] += second_term

    @pl.when(step == 1)
    def _():
        for s, rows in enumerate(slots):
            pieces = mod[s]
            alive = jnp.where(s < live, 1.0, 0.0)
            feed_out = feed[rows, :] + bias[15:16, :]
            grad_out = cotangent[s].astype(WIDE) * alive
            out[s] = ((middle[rows, :] + pieces[5:6] * feed_out) * alive).astype(LOW)
            grad = grad_second[rows, :]
            unit = normed[rows, :]
            grad_middle = grad_out + norm_backward(
                grad * (1.0 + pieces[4:5]), unit, inverse[rows, 0:1]
            )
            grad_middle_out[s] = grad_middle
            rows_out[4 * s : 4 * s + 1, :] = column_sum(grad_middle * branch[rows, :])
            rows_out[4 * s + 1 : 4 * s + 2, :] = column_sum(grad)
            rows_out[4 * s + 2 : 4 * s + 3, :] = column_sum(grad * unit)
            rows_out[4 * s + 3 : 4 * s + 4, :] = column_sum(grad_out * feed_out)


def attention_backward_kernel(
    slot, where, tokens, grad_middle_in, joined, soft_in, mixed, mod, feed_rows, cond, att, proj, *refs
):
    rank, core = where[0], where[1]
    if slot == 0:
        grad_tokens_out, grad_joined, first_out, branch_out, rows = refs
    else:
        before_joined, before_first, before_branch, before_rows, _, _ = refs[:6]
        grad_tokens_out, send_out, keep_out, rows_out = refs[6:10]
        grad_joined, grad_att, grad_proj, rows = refs[10:]

    if slot == 0:
        rows[...] = jnp.zeros_like(rows)
        rows[12:14, :] = cond[...]
        rows[19:24, :] = feed_rows[8:13, :]
    else:
        rows[...] = before_rows[...]

    pieces = mod[0]
    grad_middle = grad_middle_in[0]
    grad_branch = (pieces[2:3] * grad_middle).astype(LOW)
    rows[18:19, :] += column_sum(grad_branch.astype(WIDE))
    if slot == 0:
        branch_out[...] = grad_branch
    else:
        grad_proj[...] = (
            dot_first(mixed[0], before_branch[...]) + dot_first(mixed[1], grad_branch)
        ).astype(LOW)
    grad_mixed = dot_last(grad_branch, proj[...]).astype(LOW)
    first_half = head_mask((SEQ, 128), 0)
    zero = jnp.zeros((SEQ, 128), LOW)
    scale = HEAD_DIM ** (-0.5)
    for pair in range(HEADS // 2):
        lanes = slice(pair * 128, (pair + 1) * 128)
        query = joined[0, :, pair * 128 : (pair + 1) * 128]
        key = joined[0, :, D + pair * 128 : D + (pair + 1) * 128]
        value = joined[0, :, 2 * D + pair * 128 : 2 * D + (pair + 1) * 128]
        grads = grad_mixed[:, lanes]
        results = []
        for half in range(2):
            soft = soft_in[0, 2 * pair + half]
            masked = (
                jnp.where(first_half, grads, zero)
                if half == 0
                else jnp.where(first_half, zero, grads)
            )
            grad_soft = dot_last(masked, value)
            grad_values = dot_first(soft, grads)
            soft_wide = soft.astype(WIDE)
            weighted = soft_wide * grad_soft
            inner = jnp.sum(weighted, axis=-1, keepdims=True)
            grad_scores = (weighted - soft_wide * inner).astype(LOW)
            results.append(
                (dot_plain(grad_scores, key), dot_first(grad_scores, query), grad_values)
            )
        for third in range(3):
            merged = jnp.where(first_half, results[0][third], results[1][third])
            if third < 2:
                merged = merged * scale
            grad_joined[:, third * D + pair * 128 : third * D + (pair + 1) * 128] = merged.astype(LOW)
    grads = grad_joined[...]
    sums = column_sum(grads.astype(WIDE))
    rows[16:17, :] += sums[:, :D]
    rows[17:18, :] += sums[:, 2 * D :]
    normed, inverse = layer_norm_parts(tokens[0].astype(WIDE))
    first_in = (normed * (1.0 + pieces[1:2]) + pieces[0:1]).astype(LOW)
    if slot == 0:
        first_out[...] = first_in
    else:
        for third in range(3):
            lanes = slice(third * D, (third + 1) * D)
            grad_att[:, lanes] = (
                dot_first(before_first[...], before_joined[:, lanes])
                + dot_first(first_in, grad_joined[:, lanes])
            ).astype(LOW)
    grad_first = dot_last(grads, att[...])
    grad_tokens_out[0] = (
        grad_middle + norm_backward(grad_first * (1.0 + pieces[1:2]), normed, inverse)
    ).astype(LOW)
    own_rows = jnp.concatenate(
        [
            column_sum(grad_first),
            column_sum(grad_first * normed),
        ],
        axis=0,
    )

    rows[6 * slot : 6 * slot + 2, :] = own_rows
    rows[6 * slot + 2 : 6 * slot + 6, :] = feed_rows[4 * slot : 4 * slot + 4, :]
    if slot == 0:
        return
    rows_out[...] = rows[...].astype(LOW)
    for k in range(4):
        start = pl.multiple_of((rank ^ k) * QUARTER, 32)
        block = grad_att[pl.ds(start, QUARTER), :]
        low_part = (block[:, :D], block[:, D : 2 * D])
        high_part = (block[:, 2 * D :], grad_proj[pl.ds(start, QUARTER), :])
        turned = (0, 2, 1, 3)[k]

        @pl.when(core == 0)
        def _():
            for j in range(2):
                keep_out[turned, j * QUARTER : (j + 1) * QUARTER, :] = low_part[j]
                send_out[k, j * QUARTER : (j + 1) * QUARTER, :] = high_part[j]

        @pl.when(core != 0)
        def _():
            for j in range(2):
                keep_out[k, j * QUARTER : (j + 1) * QUARTER, :] = high_part[j]
                send_out[turned, j * QUARTER : (j + 1) * QUARTER, :] = low_part[j]


def half_of(where, which):
    return (where[2] >> (where[1] ^ which)) & 1


def rows_at(index, count):
    return pl.ds(pl.multiple_of(index * count, 16), count)


def merge_small(out, own, arrived):
    count = own.shape[0] - BLOCK
    out[0:count, :] = own[0:count, :]
    out[count : 2 * count, :] = arrived[0:count, :]
    out[2 * count :, :] = (
        own[count:, :].astype(WIDE) + arrived[count:, :].astype(WIDE)
    ).astype(LOW)


def step1_kernel(
    where, att_keep, att_in, feed_keep, feed_in, small, small_in,
    att_stay, att_go, feed_stay, feed_go, small_out, total,
):
    half = half_of(where, 0)
    count = D // 2
    att_stay[...] = att_keep[0] + att_in[0].astype(WIDE)
    att_go[...] = (att_keep[1] + att_in[1].astype(WIDE)).astype(LOW)
    total[...] = feed_keep[...] + feed_in[...].astype(WIDE)
    feed_stay[...] = total[rows_at(half, count), :]
    feed_go[...] = total[rows_at(1 - half, count), :].astype(LOW)
    merge_small(small_out, small, small_in)


def step2_kernel(where, att_keep, att_in, feed_keep, feed_in, small, small_in, message, small_out):
    count = D // 2
    message[0:count, :] = (feed_keep[...] + feed_in[...].astype(WIDE)).astype(LOW)
    message[count:, :] = (att_keep[...] + att_in[...].astype(WIDE)).astype(LOW)
    merge_small(small_out, small, small_in)


def step3_kernel(where, own, arrived, small, small_in, message, small_out):
    message[...] = (own[...].astype(WIDE) + arrived[...].astype(WIDE)).astype(LOW)
    merge_small(small_out, small, small_in)


def step4_kernel(
    where, own, arrived, small, small_in, weight, att_part, feed_part, small_out, cond_keep, cond_go
):
    half = half_of(where, 0)
    count = D // 2
    feed_part[rows_at(half, count), :] = own[0:count, :]
    feed_part[rows_at(1 - half, count), :] = arrived[0:count, :]
    att_part[...] = (own[count:, :].astype(WIDE) + arrived[count:, :].astype(WIDE)).astype(LOW)
    merge_small(small_out, small, small_in)
    rows = [
        block[start : start + BLOCK, :].astype(WIDE)
        for block in (small, small_in)
        for start in (0, 4 * BLOCK)
    ]
    total = None
    for j in range(6):
        lines = [row[6 * slot + j : 6 * slot + j + 1] for row in rows for slot in range(2)]
        term = dot_last(
            jnp.concatenate(lines, axis=0).astype(LOW), weight[:, j * D : (j + 1) * D]
        )
        total = term if total is None else total + term
    padded = jnp.concatenate([total, jnp.zeros((8, 128 - QUARTER), WIDE)], axis=1)
    blank = jnp.zeros((4, 128), WIDE)
    cond_keep[...] = jnp.concatenate([padded[0:4], blank], axis=0)
    cond_go[...] = jnp.concatenate([padded[4:8], blank], axis=0)


def step5_kernel(where, cond_keep, cond_in, _, cond_go):
    blank = jnp.zeros((4, 128), WIDE)
    cond_go[...] = jnp.concatenate([cond_keep[2:4], cond_in[2:4], blank], axis=0)


def modulation_update_kernel(
    where, near, far, weight, mean, square, bias, bias_mean, bias_square,
    weight_out, mean_out, square_out, bias_out, bias_mean_out, bias_square_out, mark, everyone,
):
    rank, core, plane = where[0], where[1], where[2]
    for side, source in enumerate((near, far)):
        here = core ^ side
        first, second = 1 + here, 2 - here
        for index in range(16):
            a, b, c, d = (index & 1, (index >> 1) & 1, (index >> 2) & 1, index >> 3)
            z_at = plane ^ (a * first) ^ (b * second)
            g_at = rank ^ (c * second) ^ (d * first)
            place = (g_at * 4 + z_at) * 2 + here
            block = source[index * BLOCK : (index + 1) * BLOCK, :].astype(WIDE)
            for third in range(3):
                everyone[third, rows_at(place, BLOCK), :] = block[
                    :, third * 128 : (third + 1) * 128
                ]

    def line(at):
        parts = [everyone[third, pl.ds(at, 32, stride=BLOCK), :] for third in range(3)]
        return jnp.concatenate(parts, axis=1)

    def both(at, other):
        return jnp.concatenate([line(at), line(other)], axis=0)

    def own_lanes(values):
        chosen = values[:, :QUARTER]
        for place in range(1, 4):
            lanes = slice(place * QUARTER, (place + 1) * QUARTER)
            chosen = jnp.where(rank == place, values[:, lanes], chosen)
        return chosen

    cond = own_lanes(both(12, 13)).astype(LOW)
    sums = []
    for j in range(6):
        lanes = slice(j * D, (j + 1) * D)
        grads = both(j, 6 + j)
        sums.append(column_sum(grads))
        gradient = dot_first(cond, grads.astype(LOW))
        updated, momentum, variance = adam_update(
            weight[:, lanes].astype(WIDE),
            gradient,
            mean[:, lanes].astype(WIDE),
            square[:, lanes].astype(WIDE),
            LEARN_RATES[0],
            DECAY_FLAGS[0],
        )
        weight_out[:, lanes] = updated
        mean_out[:, lanes] = momentum
        square_out[:, lanes] = variance
    sums.append(near[16 * BLOCK :, :].astype(WIDE)[0:8] + far[16 * BLOCK :, :].astype(WIDE)[0:8])
    gradient = own_lanes(jnp.concatenate(sums, axis=0))
    updated, momentum, variance = adam_update(
        bias[...].astype(WIDE),
        gradient,
        bias_mean[...].astype(WIDE),
        bias_square[...].astype(WIDE),
        LEARN_RATES[5],
        DECAY_FLAGS[5],
    )
    bias_out[...] = updated
    bias_mean_out[...] = momentum
    bias_square_out[...] = variance
    mark[...] = jnp.zeros_like(mark)


def split_kernel(keep, arrived, stay, go):
    half = stay.shape[0]
    stay[...] = keep[:half].astype(WIDE) + arrived[:half].astype(WIDE)
    go[...] = (keep[half:].astype(WIDE) + arrived[half:].astype(WIDE)).astype(LOW)


def whole(shape):
    return pl.BlockSpec(shape, lambda *grid: (0,) * len(shape))


def by_slot(shape):
    return pl.BlockSpec((1,) + shape, lambda s: (s,) + (0,) * len(shape))


def shape_of(shape, dtype):
    return jax.ShapeDtypeStruct(shape, dtype)


SMEM_SPEC = pl.BlockSpec(memory_space=pltpu.SMEM)
PARAMS = pltpu.CompilerParams(vmem_limit_bytes=VMEM_BYTES)


ANY_SPEC = pl.BlockSpec(memory_space=pl.ANY)


def small_call(kernel, name, outs, where, *operands, scratch=(), after=(), params=PARAMS):
    return pl.pallas_call(
        kernel,
        grid=(1,),
        in_specs=[SMEM_SPEC]
        + [whole(item.shape) for item in operands]
        + [ANY_SPEC] * len(after),
        out_specs=[whole(shape) for shape, _ in outs],
        out_shape=[shape_of(*item) for item in outs],
        scratch_shapes=[pltpu.VMEM(*item) for item in scratch],
        compiler_params=params,
        name=name,
    )(where, *operands, *after)


def run_gate(value, *after, space=ANY_SPEC):
    return pl.pallas_call(
        gate_kernel,
        in_specs=[space] + [ANY_SPEC] * len(after),
        out_specs=space,
        out_shape=shape_of(value.shape, value.dtype),
        input_output_aliases={0: 0},
        compiler_params=pltpu.CompilerParams(vmem_limit_bytes=1024 * 1024),
        name="in_order",
    )(value, *after)


def run_relay(where, keep, arrived, passing):
    two = (2, keep.shape[1])
    return pl.pallas_call(
        relay_kernel,
        grid=(1,),
        in_specs=[SMEM_SPEC, whole(keep.shape), whole(arrived.shape), ANY_SPEC],
        out_specs=[whole(two), whole(two), ANY_SPEC],
        out_shape=[shape_of(two, WIDE)] * 2 + [shape_of(passing.shape, passing.dtype)],
        input_output_aliases={3: 2},
        compiler_params=PARAMS,
        name="relay",
    )(where, keep, arrived, passing)


def run_modulation(where, condition, biases, blocks, weight):
    message = pl.BlockSpec((16, D), lambda s: (2 * QUARTER // 16, 0))
    return pl.pallas_call(
        modulation_kernel,
        grid=(1,),
        in_specs=[SMEM_SPEC, whole((2, D)), whole((BIAS_ROWS, QUARTER))]
        + [message] * 3
        + [whole((QUARTER, 6 * D))],
        out_specs=[whole((4, 6 * D))] * 2 + [whole((16, D))],
        out_shape=[shape_of((4, 6 * D), WIDE)] * 2 + [shape_of((16, D), WIDE)],
        compiler_params=PARAMS,
        cost_estimate=pl.CostEstimate(flops=10**7, bytes_accessed=10**6, transcendentals=0),
        name="modulation_partials",
    )(where, condition, biases, *blocks, weight)


def run_attention_forward(where, tokens, stay, arrived, bias, own_att, own_proj, nears, fars):
    part = whole((2 * QUARTER + 16, D))
    return pl.pallas_call(
        attention_forward_kernel,
        grid=(2,),
        in_specs=[
            SMEM_SPEC,
            by_slot((SEQ, D)),
            whole((2, 6 * D)),
            whole((2, 6 * D)),
            whole((16, D)),
            whole((QUARTER, 3 * D)),
            whole((QUARTER, D)),
        ]
        + [part] * 6,
        out_specs=[
            by_slot((SEQ, 3 * D)),
            by_slot((HEADS, SEQ, SEQ)),
            by_slot((SEQ, D)),
            by_slot((6, D)),
            whole((D, 3 * D)),
            whole((D, D)),
        ],
        out_shape=[
            shape_of((2, SEQ, 3 * D), LOW),
            shape_of((2, HEADS, SEQ, SEQ), LOW),
            shape_of((2, SEQ, D), LOW),
            shape_of((2, 6, D), WIDE),
            shape_of((D, 3 * D), LOW),
            shape_of((D, D), LOW),
        ],
        compiler_params=PARAMS,
        cost_estimate=pl.CostEstimate(
            flops=3 * 10**9, bytes_accessed=6 * 10**6, transcendentals=10**6
        ),
        name="attention_forward",
    )(where, tokens, stay, arrived, bias, own_att, own_proj, *nears, *fars)


def run_feed(where, mixed, tokens, cotangent, mod, bias, proj, own_expand, own_contract, nears, fars):
    rows = 2 * SEQ

    return pl.pallas_call(
        feed_kernel,
        grid=(2,),
        in_specs=[SMEM_SPEC]
        + [whole((2, SEQ, D))] * 3
        + [whole((2, 6, D)), whole((16, D))]
        + [whole((D, D))] * 9,
        out_specs=[
            whole((2, SEQ, D)),
            whole((2, SEQ, D)),
            pl.BlockSpec((2, D, D), lambda i: (i, 0, 0)),
            pl.BlockSpec((2, D, D), lambda i: (i, 0, 0)),
            whole((16, D)),
        ],
        scratch_shapes=[
            pltpu.VMEM((2, D, 2 * D), LOW),
            pltpu.VMEM((2, 2 * D, D), LOW),
            pltpu.VMEM((rows, D), WIDE),
            pltpu.VMEM((rows, D), WIDE),
            pltpu.VMEM((rows, D), LOW),
            pltpu.VMEM((rows, D), WIDE),
            pltpu.VMEM((rows, 128), WIDE),
            pltpu.VMEM((rows, D), LOW),
            pltpu.VMEM((rows, D), WIDE),
            pltpu.VMEM((rows, D), WIDE),
        ],
        out_shape=[
            shape_of((2, SEQ, D), LOW),
            shape_of((2, SEQ, D), WIDE),
            shape_of((4, D, D), LOW),
            shape_of((4, D, D), LOW),
            shape_of((16, D), WIDE),
        ],
        compiler_params=PARAMS,
        cost_estimate=pl.CostEstimate(
            flops=8 * 10**9, bytes_accessed=10**7, transcendentals=10**6
        ),
        name="feed_forward_and_back",
    )(where, mixed, tokens, cotangent, mod, bias, proj, own_expand, own_contract, *nears, *fars)


def run_attention_backward(
    slot, where, tokens, grad_middle, joined, soft, mixed, mod, feed_rows, cond, att, proj, earlier=()
):
    def at_slot(shape):
        return pl.BlockSpec((1,) + shape, lambda i: (slot,) + (0,) * len(shape))

    passed = [((SEQ, 3 * D), LOW), ((SEQ, D), LOW), ((SEQ, D), LOW), ((SMALL, D), WIDE)]
    in_specs = [
        SMEM_SPEC,
        at_slot((SEQ, D)),
        at_slot((SEQ, D)),
        at_slot((SEQ, 3 * D)),
        at_slot((HEADS, SEQ, SEQ)),
        whole((2, SEQ, D)),
        at_slot((6, D)),
        whole((16, D)),
        whole((2, D)),
        whole((D, 3 * D)),
        whole((D, D)),
    ]
    out_specs = [at_slot((SEQ, D))]
    out_shape = [shape_of((2, SEQ, D), LOW)]
    scratch = []
    aliases = {}
    if slot == 0:
        out_specs += [whole(shape) for shape, _ in passed]
        out_shape += [shape_of(*item) for item in passed]
    else:
        in_specs += [whole(shape) for shape, _ in passed] + [ANY_SPEC, ANY_SPEC]
        aliases = {15: 0}
        out_specs += [whole((4, 2 * QUARTER, D))] * 2 + [whole((SMALL, D))]
        out_shape += [shape_of((4, 2 * QUARTER, D), LOW)] * 2 + [shape_of((SMALL, D), LOW)]
        sums = [((D, 3 * D), LOW), ((D, D), LOW)]
        scratch = [pltpu.VMEM(*item) for item in (passed[0], *sums, passed[3])]
    return pl.pallas_call(
        functools.partial(attention_backward_kernel, slot),
        grid=(1,),
        in_specs=in_specs,
        out_specs=out_specs,
        out_shape=out_shape,
        scratch_shapes=scratch,
        input_output_aliases=aliases,
        compiler_params=PARAMS,
        cost_estimate=pl.CostEstimate(
            flops=4 * 10**9, bytes_accessed=8 * 10**6, transcendentals=0
        ),
        name="attention_backward",
    )(where, tokens, grad_middle, joined, soft, mixed, mod, feed_rows, cond, att, proj, *earlier)


def turn_split_kernel(where, keep, arrived, stay, go):
    core = where[1]
    for place, block in enumerate((0, 2 - core)):
        stay[place] = keep[block].astype(WIDE) + arrived[block].astype(WIDE)
    for place, block in enumerate((1 + core, 3)):
        go[place] = (keep[block].astype(WIDE) + arrived[block].astype(WIDE)).astype(LOW)


def run_split(keep, arrived):
    count, rest = keep.shape[0], keep.shape[1:]
    half = (count // 2,) + rest
    return pl.pallas_call(
        split_kernel,
        grid=(1,),
        in_specs=[whole(keep.shape)] * 2,
        out_specs=[whole(half)] * 2,
        out_shape=[shape_of(half, WIDE), shape_of(half, LOW)],
        compiler_params=PARAMS,
        name="sum_and_split",
    )(keep, arrived)


def swap_plane(value, which):
    pairs = [(r, r ^ ((1 + ((r + which) & 1)) << 1)) for r in range(lax.axis_size("replica"))]
    return lax.ppermute(value, "replica", pairs)


def swap_pair(value, which):
    groups, copies = lax.axis_size("group"), lax.axis_size("replica")
    pairs = []
    for g in range(groups):
        for r in range(copies):
            other = g ^ (1 if (r + which) % 2 == 0 else 2)
            pairs.append((g * copies + r, other * copies + r))
    return lax.ppermute(value, ("group", "replica"), pairs)


def gather_pair(value):
    first = swap_pair(value, 0)
    second = swap_pair(value, 1)
    return (first, second, swap_pair(first, 1))


def update_all(stored, gradients, means, squares, kinds):
    return [
        adam_update(
            stored[kind].astype(jnp.float32),
            gradient,
            means[kind].astype(jnp.float32),
            squares[kind].astype(jnp.float32),
            LEARN_RATES[kind],
            DECAY_FLAGS[kind],
        )
        for kind, gradient in zip(kinds, gradients)
    ]


def by_core(core, own, other):
    return (
        jnp.where(core == 0, own, other).astype(jnp.float32),
        jnp.where(core == 0, other, own).astype(jnp.float32),
    )


def attention_shards(totals):
    joined = jnp.concatenate(
        [totals[0][:QUARTER], totals[0][QUARTER:], totals[1][:QUARTER]], axis=1
    )
    return (joined, totals[1][QUARTER:])


def tail_in_step(
    where, copy, stages, condition, ffn_halves, att_parts, small_rows, stored, means, squares
):
    core = where[1]
    (feed_stay, feed_in), (att_send, att_keep) = ffn_halves, att_parts
    half, third = (D // 2, D), (2 * QUARTER, D)
    att_stay, att_go = run_split(att_keep, swap_replica(att_send, 1))
    feed_stay, feed_go = run_split(feed_stay, feed_in)
    feed_stay, feed_go = feed_stay[0], feed_go[0]
    att_stay, att_go, feed_stay, feed_go, small = small_call(
        step1_kernel, "step_1",
        [(third, WIDE), (third, LOW), (half, WIDE), (half, LOW), ((3 * BLOCK, D), LOW)],
        where, att_stay, swap_pair(att_go, 0), feed_stay, swap_pair(feed_go, 1),
        small_rows, swap_plane(small_rows, 0),
        scratch=[((D, D), WIDE)],
    )
    message, small = small_call(
        step2_kernel, "step_2",
        [((D, D), LOW), ((5 * BLOCK, D), LOW)],
        where, att_stay, swap_pair(att_go, 1), feed_stay, swap_plane(feed_go, 0),
        small, swap_plane(small, 1),
    )
    message, small = small_call(
        step3_kernel, "step_3",
        [((D, D), LOW), ((9 * BLOCK, D), LOW)],
        where, message, swap_plane(message, 1), small, swap_pair(small, 1),
    )
    att_part, feed_part, small, cond_keep, cond_go = small_call(
        step4_kernel, "step_4",
        [(third, LOW), ((D, D), LOW), ((17 * BLOCK, D), LOW), ((8, 128), WIDE), ((8, 128), WIDE)],
        where, message, swap_plane(message, 0), small, swap_pair(small, 0), stored[0],
    )
    shard = [((QUARTER, 6 * D), WIDE)] * 3 + [((BIAS_ROWS, QUARTER), WIDE)] * 3
    *updates, mark = small_call(
        modulation_update_kernel, "modulation_update", shard + [((8, 128), WIDE)],
        where, small, swap_replica(small, 1), stored[0], means[0], squares[0],
        stored[5], means[5], squares[5],
        scratch=[((3, 32 * BLOCK, 128), WIDE)],
    )
    feed_totals = by_core(core, feed_part, swap_replica(feed_part, 1))
    feed_updates = update_all(stored, feed_totals, means, squares, (3, 4))
    cond_in = swap_pair(cond_go, 0)
    cond_go = small_call(
        step5_kernel, "step_5", [((8, 128), WIDE)], where, cond_keep, cond_in, after=(mark,)
    )[0]
    cond_last = swap_pair(cond_go, 1)
    att_totals = by_core(core, att_part, swap_replica(att_part, 1))
    blocks = [
        block[:, :QUARTER] for block in (cond_keep[:2], cond_in[:2], cond_last[:2], cond_last[2:4])
    ]
    owners = (where[0],) + neighbours(where)
    lanes = []
    for place in range(4):
        chosen = blocks[0]
        for k in range(1, 4):
            chosen = jnp.where(owners[k] == place, blocks[k], chosen)
        lanes.append(chosen)
    sigmoid_cond = jax.nn.sigmoid(condition)
    grad_condition = (
        jnp.concatenate(lanes, axis=1) * sigmoid_cond * (1.0 + condition * (1.0 - sigmoid_cond))
    )
    att_updates = update_all(stored, attention_shards(att_totals), means, squares, (1, 2))
    return grad_condition, [updates[:3]] + att_updates + feed_updates + [updates[3:]]


def tail_in_turn(
    where, copy, stages, condition, ffn_halves, att_parts, small_rows, stored, means, squares
):
    rank, core = where[0], where[1]
    slot_count, model_width = condition.shape
    modulation, cond_low = stored[0], jax.nn.silu(condition).astype(jnp.bfloat16)
    (ffn_stay, ffn_in), (att_send, att_keep) = ffn_halves, att_parts
    ffn_stay, ffn_go = run_split(ffn_stay, ffn_in)
    ffn_totals = reduce_replicas(
        wide_sum([ffn_stay[0], swap_pair(ffn_go[0], 1)]).astype(LOW), copy, stages
    )
    att_stay, att_go = run_split(att_keep, swap_replica(att_send, 1))
    att_stay, att_go = run_split(att_stay, swap_pair(att_go, 0))
    att_totals = reduce_replicas(
        wide_sum([att_stay[0], swap_pair(att_go[0], 1)]).astype(LOW), copy, stages
    )
    row_total = small_rows.shape[0]
    gathered = small_rows[None]
    for low_bit, radix in stages[1:]:
        digit = (copy >> low_bit) % radix
        gathered = in_order(
            [swap_replica(gathered, k << low_bit) for k in range(radix)], digit
        ).reshape(-1, row_total, model_width)
    gathered = in_order([swap_group(gathered, k) for k in range(4)], rank)
    own_plane = lax.dynamic_index_in_dim(gathered, copy >> 1, axis=1, keepdims=False)
    group_mod = own_plane[:, : 6 * slot_count].reshape(4 * slot_count, 6 * model_width)
    grad_cond_columns = dot_last(group_mod, modulation).reshape(4, slot_count, model_width // 4)
    cond_back = in_order(
        [swap_group(pick(grad_cond_columns, rank ^ k), k) for k in range(4)], rank
    )
    sigmoid_cond = jax.nn.sigmoid(condition)
    grad_condition = (
        jnp.swapaxes(cond_back, 0, 1).reshape(slot_count, model_width)
        * sigmoid_cond
        * (1.0 + condition * (1.0 - sigmoid_cond))
    )
    everyone = in_order([swap_replica(gathered, k) for k in range(2)], core).reshape(
        -1, row_total, model_width
    )
    all_mod = everyone[:, : 6 * slot_count].reshape(-1, 6 * model_width)
    all_cond = everyone[:, 6 * slot_count : 7 * slot_count].reshape(-1, model_width)
    cond_own = lax.dynamic_slice_in_dim(all_cond, rank * (model_width // 4), model_width // 4, 1)
    grad_mod = dot_first(cond_own, all_mod)
    mod_bias_grad = jnp.sum(all_mod, axis=0, dtype=jnp.float32).reshape(6, model_width)
    rest_bias_grad = jnp.sum(everyone[:, BLOCK : BLOCK + 8], axis=0, dtype=jnp.float32)
    bias_grad = lax.dynamic_slice_in_dim(
        jnp.concatenate([mod_bias_grad, rest_bias_grad], axis=0),
        rank * (model_width // 4),
        model_width // 4,
        1,
    )
    grad_att_own = jnp.concatenate(
        [att_totals[0][:QUARTER], att_totals[0][QUARTER:], att_totals[1][:QUARTER]], axis=1
    )
    totals = (
        grad_mod,
        grad_att_own,
        att_totals[1][QUARTER:],
        ffn_totals[0],
        ffn_totals[1],
        bias_grad,
    )
    return grad_condition, update_all(stored, totals, means, squares, range(6))


def shards(
    latents,
    condition,
    cotangent,
    live_counts,
    modulation,
    attending,
    projection,
    expand,
    contract,
    biases,
    modulation_mean,
    attending_mean,
    projection_mean,
    expand_mean,
    contract_mean,
    biases_mean,
    modulation_square,
    attending_square,
    projection_square,
    expand_square,
    contract_square,
    biases_square,
):
    slot_count, length, model_width = latents.shape
    rank = lax.axis_index("group")
    copy = lax.axis_index("replica")
    core = copy % 2
    stages = replica_stages(lax.axis_size("replica"))
    where = jnp.stack([rank, core, copy >> 1, live_counts[0]]).astype(jnp.int32)

    cond_low = jax.nn.silu(condition).astype(LOW)
    payload, feed_part = small_call(
        payload_kernel, "own_payload",
        [((2 * QUARTER + 16, model_width), LOW), ((model_width, model_width), LOW)],
        where, condition, attending, projection, biases, expand, contract,
        params=pltpu.CompilerParams(vmem_limit_bytes=60 * 1024 * 1024),
    )
    first, second = swap_pair(payload, 0), swap_pair(payload, 1)
    last, first_far = swap_pair(first, 1), swap_replica(first, 1)
    feed_part = run_gate(
        feed_part, first_far, second, space=pl.BlockSpec(memory_space=pltpu.HBM)
    )
    nears = (first, second, last)
    fars = [first_far, swap_replica(second, 1), swap_replica(last, 1)]
    feed_first, feed_second = swap_pair(feed_part, 0), swap_pair(feed_part, 1)
    stay, go, bias = run_modulation(where, condition, biases, nears, modulation)
    stay, go, feed_first = run_relay(where, stay, swap_pair(go, 0), feed_first)
    arrived = swap_pair(go, 1)
    feed_last = swap_pair(feed_first, 1)
    joined, soft, mixed, mod, att, proj = run_attention_forward(
        where, latents, stay, arrived, bias, attending, projection, nears, fars
    )
    feed_nears = (feed_first, feed_second, run_gate(feed_last, mod))
    feed_fars = [swap_replica(item, 1) for item in feed_nears]
    out_latents, grad_middle, ffn_send, ffn_keep, feed_rows = run_feed(
        where, mixed, latents, cotangent, mod, bias, proj, expand, contract, feed_nears, feed_fars
    )
    cond_wide = cond_low.astype(WIDE)
    two_blocks = (2, model_width, model_width)
    ffn_stay, ffn_go = small_call(
        turn_split_kernel, "sum_and_split", [(two_blocks, WIDE), (two_blocks, LOW)],
        where, ffn_keep, swap_replica(ffn_send, 1),
    )
    earlier = run_attention_backward(
        0, where, latents, grad_middle, joined, soft, mixed, mod, feed_rows, cond_wide, att, proj
    )
    ffn_in = swap_pair(ffn_go, 0)
    grad_latents, att_send, att_keep, small_rows = run_attention_backward(
        1, where, latents, grad_middle, joined, soft, mixed, mod, feed_rows, cond_wide, att, proj,
        (*earlier[1:], earlier[0], ffn_go),
    )
    tail = tail_in_step if lax.axis_size("replica") == 8 else tail_in_turn
    grad_condition, results = tail(
        where, copy, stages, condition, (ffn_stay, ffn_in), (att_send, att_keep), small_rows,
        (modulation, attending, projection, expand, contract, biases),
        (
            modulation_mean, attending_mean, projection_mean,
            expand_mean, contract_mean, biases_mean,
        ),
        (
            modulation_square, attending_square, projection_square,
            expand_square, contract_square, biases_square,
        ),
    )
    return (
        out_latents,
        grad_latents,
        grad_condition,
        results[0][0],
        results[1][0],
        results[2][0],
        results[3][0],
        results[4][0],
        results[5][0],
        results[0][1],
        results[1][1],
        results[2][1],
        results[3][1],
        results[4][1],
        results[5][1],
        results[0][2],
        results[1][2],
        results[2][2],
        results[3][2],
        results[4][2],
        results[5][2],
    )


def solution(mesh):
    return jax.shard_map(
        shards,
        mesh=mesh,
        in_specs=(
            P(("group", "replica"), None, None),
            P(("group", "replica"), None),
            P(("group", "replica"), None, None),
            P(("group", "replica")),
            P("group", None),
            P("group", None),
            P("group", None),
            P(None, "group"),
            P("group", None),
            P(None, "group"),
            P("group", None),
            P("group", None),
            P("group", None),
            P(None, "group"),
            P("group", None),
            P(None, "group"),
            P("group", None),
            P("group", None),
            P("group", None),
            P(None, "group"),
            P("group", None),
            P(None, "group"),
        ),
        out_specs=(
            P(("group", "replica"), None, None),
            P(("group", "replica"), None, None),
            P(("group", "replica"), None),
            P("group", None),
            P("group", None),
            P("group", None),
            P(None, "group"),
            P("group", None),
            P(None, "group"),
            P("group", None),
            P("group", None),
            P("group", None),
            P(None, "group"),
            P("group", None),
            P(None, "group"),
            P("group", None),
            P("group", None),
            P("group", None),
            P(None, "group"),
            P("group", None),
            P(None, "group"),
        ),
        check_vma=False,
    )
```

```python
import functools

import jax
import jax.numpy as jnp
from jax import lax
from jax.experimental import pallas as pl
from jax.experimental.pallas import tpu as pltpu
from jax.sharding import PartitionSpec as P

HEADS = 6
HEAD_DIM = 64
FF = 1536
STEP = 10


NORM_EPS = 1e-06
ADAM_EPS = 1e-08
BETA_FIRST = 0.9
BETA_SECOND = 0.999
DECAY_RATE = 0.1
LEARN_RATES = (0.05, 0.05, 0.2, 0.05, 0.025, 0.1)
DECAY_FLAGS = (1.0, 1.0, 1.0, 1.0, 1.0, 0.0)
GELU_COEF = 0.7978845608028654
BIAS_ROWS = 14
D = 384
SEQ = 256
QUARTER = D // 4
VMEM_BYTES = 34 * 1024 * 1024
LOW = jnp.bfloat16
SMALL = 32
BLOCK = 16
WIDE = jnp.float32


def dot_plain(left_side, right_side):
    return jnp.dot(left_side, right_side, preferred_element_type=WIDE)


def dot_first(left_side, right_side):
    return lax.dot_general(
        left_side, right_side, (((0,), (0,)), ((), ())), preferred_element_type=WIDE
    )


def dot_last(left_side, right_side):
    return lax.dot_general(
        left_side, right_side, (((1,), (1,)), ((), ())), preferred_element_type=WIDE
    )


def adam_update(weight, gradient, mean_old, square_old, step_rate, decay_flag):
    momentum = BETA_FIRST * mean_old + (1.0 - BETA_FIRST) * gradient
    variance = BETA_SECOND * square_old + ((1.0 - BETA_SECOND) * gradient) * gradient
    root = variance * lax.rsqrt(variance)
    bottom = root * (1.0 - BETA_SECOND**STEP) ** (-0.5) + ADAM_EPS
    change = momentum * (step_rate / (1.0 - BETA_FIRST**STEP)) / bottom
    updated = weight * (1.0 - step_rate * decay_flag * DECAY_RATE) - change
    return (updated, momentum, variance)


def replica_stages(count):
    stages, low_bit = [(0, 2)], 1
    while (1 << low_bit) < count:
        radix = min(4, count >> low_bit)
        stages.append((low_bit, radix))
        low_bit += radix.bit_length() - 1
    return stages


def swap_group(value, k):
    if k == 0:
        return value
    return lax.ppermute(value, "group", [(i, i ^ k) for i in range(lax.axis_size("group"))])


def swap_replica(value, k):
    if k == 0:
        return value
    return lax.ppermute(value, "replica", [(i, i ^ k) for i in range(lax.axis_size("replica"))])


def pick(blocks, index):
    return lax.dynamic_index_in_dim(blocks, index, axis=0, keepdims=False)


def in_order(blocks, digit):
    ordered = []
    for place in range(len(blocks)):
        chosen = blocks[0]
        for k in range(1, len(blocks)):
            chosen = jnp.where((digit ^ k) == place, blocks[k], chosen)
        ordered.append(chosen)
    return jnp.stack(ordered)


def wide_sum(blocks):
    total = blocks[0].astype(jnp.float32)
    for block in blocks[1:]:
        total = total + block.astype(jnp.float32)
    return total


def scatter_stage(value, digit, low_bit, radix):
    rows = value.shape[-2] // radix
    parts = [
        lax.dynamic_slice_in_dim(value, (digit ^ k) * rows, rows, value.ndim - 2)
        for k in range(radix)
    ]
    received = [swap_replica(parts[k], k << low_bit) for k in range(radix)]
    return wide_sum(received).astype(jnp.bfloat16)


def reduce_replicas(value, copy, stages):
    core = copy % 2
    for low_bit, radix in stages[1:]:
        value = scatter_stage(value, (copy >> low_bit) % radix, low_bit, radix)
    for low_bit, radix in reversed(stages[1:]):
        blocks = [swap_replica(value, k << low_bit) for k in range(radix)]
        value = in_order(blocks, (copy >> low_bit) % radix)
        value = value.reshape(-1, value.shape[-1])
    other = swap_replica(value, 1)
    return (
        jnp.where(core == 0, value, other).astype(jnp.float32),
        jnp.where(core == 0, other, value).astype(jnp.float32),
    )


def layer_norm_parts(values):
    centred = values - jnp.mean(values, axis=-1, keepdims=True)
    inverse = lax.rsqrt(jnp.mean(centred * centred, axis=-1, keepdims=True) + NORM_EPS)
    return (centred * inverse, inverse)


def norm_backward(grad_normed, normed, inverse):
    mean_grad = jnp.mean(grad_normed, axis=-1, keepdims=True)
    mean_cross = jnp.mean(grad_normed * normed, axis=-1, keepdims=True)
    return inverse * (grad_normed - mean_grad - normed * mean_cross)


def column_sum(values):
    return jnp.sum(values, axis=0, keepdims=True)


def head_mask(shape, which):
    lane = lax.broadcasted_iota(jnp.int32, shape, 1)
    return (lane < HEAD_DIM) if which == 0 else (lane >= HEAD_DIM)


def place_rows(target, lanes, block, owner):
    start = pl.multiple_of(owner * QUARTER, 32)
    target[pl.ds(start, QUARTER), lanes] = block


def neighbours(where):
    rank, core = where[0], where[1]
    return (rank ^ (1 + core), rank ^ (2 - core), rank ^ 3)


def own_message(condition, biases):
    cond = condition[...]
    active = cond / (1.0 + jnp.exp(-cond))
    padded = jnp.concatenate(
        [biases[...].astype(WIDE), jnp.zeros((BIAS_ROWS, D - QUARTER), WIDE)], axis=1
    )
    return jnp.concatenate([active, padded], axis=0)


def payload_kernel(where, condition, attending, projection, biases, expand, contract, out, part):
    @pl.when(where[1] == 0)
    def _():
        part[...] = expand[...]
        out[0:QUARTER, :] = attending[:, 0:D]
        out[QUARTER : 2 * QUARTER, :] = attending[:, D : 2 * D]

    @pl.when(where[1] != 0)
    def _():
        part[...] = contract[...]
        out[0:QUARTER, :] = attending[:, 2 * D : 3 * D]
        out[QUARTER : 2 * QUARTER, :] = projection[...]

    out[2 * QUARTER :, :] = own_message(condition, biases).astype(LOW)


def modulation_kernel(
    where, condition, biases, first, second, last, weight, stay, go, bias_out
):
    rank = where[0]
    owners = (rank,) + neighbours(where)
    rows = [own_message(condition, biases)]
    rows += [block[...].astype(WIDE) for block in (first, second, last)]
    conds = jnp.concatenate([rows[0][0:2], rows[2][0:2], rows[1][0:2], rows[3][0:2]], axis=0)
    columns = conds[:, :QUARTER]
    for place in range(1, 4):
        lanes = slice(place * QUARTER, (place + 1) * QUARTER)
        columns = jnp.where(rank == place, conds[:, lanes], columns)
    partial = dot_plain(columns.astype(LOW), weight[...])
    stay[...] = partial[:4]
    go[...] = partial[4:]
    lanes = []
    for place in range(4):
        chosen = rows[0][:, :QUARTER]
        for k in range(1, 4):
            chosen = jnp.where(owners[k] == place, rows[k][:, :QUARTER], chosen)
        lanes.append(chosen)
    bias_out[...] = jnp.concatenate(lanes, axis=1)


def relay_kernel(where, keep, arrived, _, stay, go, __):
    stay[...] = keep[0:2, :] + arrived[0:2, :]
    go[...] = keep[2:4, :] + arrived[2:4, :]


def gate_kernel(*refs):
    pass


def attention_forward_kernel(
    where, tokens, stay, arrived, bias, own_att, own_proj, n1, n2, n3, f1, f2, f3,
    joined_out, soft_out, mixed_out, mod_out, att, proj,
):
    slot = pl.program_id(0)
    rank = where[0]

    core = where[1]

    def assemble(lows, highs):
        for k, block in zip((1, 2, 3), lows):
            place_rows(att, slice(0, D), block[0:QUARTER, :], rank ^ k)
            place_rows(att, slice(D, 2 * D), block[QUARTER : 2 * QUARTER, :], rank ^ k)
        for k, block in zip((2, 1, 3), highs):
            place_rows(att, slice(2 * D, 3 * D), block[0:QUARTER, :], rank ^ k)
            place_rows(proj, slice(0, D), block[QUARTER : 2 * QUARTER, :], rank ^ k)

    @pl.when(slot == 0)
    def _():
        place_rows(att, slice(0, 3 * D), own_att[...], rank)
        place_rows(proj, slice(0, D), own_proj[...], rank)

        @pl.when(core == 0)
        def _():
            assemble((n1, n2, n3), (f1, f2, f3))

        @pl.when(core != 0)
        def _():
            assemble((f1, f2, f3), (n1, n2, n3))

    summed = stay[...] + arrived[...]
    row = jnp.where(slot == 0, summed[0:1], summed[1:2])
    pieces = [row[:, j * D : (j + 1) * D] + bias[2 + j : 3 + j, :] for j in range(6)]
    mod_out[0] = jnp.concatenate(pieces, axis=0)
    normed, _ = layer_norm_parts(tokens[0].astype(WIDE))
    first_in = (normed * (1.0 + pieces[1]) + pieces[0]).astype(LOW)
    thirds = []
    for third in range(3):
        part = dot_plain(first_in, att[:, third * D : (third + 1) * D])
        if third == 0:
            part = part + bias[8:9, :]
        if third == 2:
            part = part + bias[9:10, :]
        part = part.astype(LOW)
        joined_out[0, :, third * D : (third + 1) * D] = part
        thirds.append(part)
    first_half = head_mask((SEQ, 128), 0)
    scale = jnp.asarray(HEAD_DIM ** (-0.5), LOW)
    zero = jnp.zeros((SEQ, 128), LOW)
    for pair in range(HEADS // 2):
        lanes = slice(pair * 128, (pair + 1) * 128)
        query, key, value = (part[:, lanes] for part in thirds)
        query = query * scale
        outs = []
        for half in range(2):
            masked = (
                jnp.where(first_half, query, zero)
                if half == 0
                else jnp.where(first_half, zero, query)
            )
            scores = dot_last(masked, key)
            weights = jnp.exp(scores - jnp.max(scores, axis=-1, keepdims=True))
            total = jnp.sum(weights, axis=-1, keepdims=True)
            soft = (weights * (1.0 / total)).astype(LOW)
            soft_out[0, 2 * pair + half] = soft
            outs.append(dot_plain(soft, value))
        mixed_out[0, :, lanes] = jnp.where(first_half, outs[0], outs[1]).astype(LOW)


def feed_kernel(
    where, mixed, tokens, cotangent, mod, bias, proj, own_expand, own_contract, n1, n2, n3, f1, f2, f3,
    out, grad_middle_out, send_out, keep_out, rows_out,
    expands, contracts, branch, middle, second, normed, inverse, grad_feed, feed, grad_second,
):
    step = pl.program_id(0)
    rank, core, live = where[0], where[1], where[3]

    def assemble(lows, highs):
        for k, block in zip((1, 2, 3), lows):
            expands[k // 2, :, (k % 2) * D : (k % 2 + 1) * D] = block[...]
        for k, block in zip((2, 1, 3), highs):
            contracts[k // 2, (k % 2) * D : (k % 2 + 1) * D, :] = block[...]

    slots = [slice(s * SEQ, (s + 1) * SEQ) for s in range(2)]

    @pl.when(step == 0)
    def _():
        expands[0, :, 0:D] = own_expand[...]
        contracts[0, 0:D, :] = own_contract[...]

        @pl.when(core == 0)
        def _():
            assemble((n1, n2, n3), (f1, f2, f3))

        @pl.when(core != 0)
        def _():
            assemble((f1, f2, f3), (n1, n2, n3))

        for s, rows in enumerate(slots):
            pieces = mod[s]
            value = dot_plain(mixed[s], proj[...]) + bias[10:11, :]
            branch[rows, :] = value
            centre = tokens[s].astype(WIDE) + pieces[2:3] * value
            middle[rows, :] = centre
            unit, spread = layer_norm_parts(centre)
            normed[rows, :] = unit
            inverse[rows, :] = jnp.broadcast_to(spread, (SEQ, 128))
            second[rows, :] = (unit * (1.0 + pieces[4:5]) + pieces[3:4]).astype(LOW)
            alive = jnp.where(s < live, 1.0, 0.0)
            grad_feed[rows, :] = (
                pieces[5:6] * (cotangent[s].astype(WIDE) * alive)
            ).astype(LOW)
        rows_out[...] = jnp.zeros_like(rows_out)
        rows_out[12:13, :] = column_sum(grad_feed[...].astype(WIDE))

    owners = (rank ^ (2 * step), rank ^ (2 * step + 1))
    hidden_bias = jnp.concatenate([bias[pl.ds(11 + owner, 1), :] for owner in owners], axis=1)
    expand, contract = expands[step], contracts[step]
    before = dot_plain(second[...], expand) + hidden_bias
    square = before * before
    tangent = jnp.tanh(before * (GELU_COEF + (GELU_COEF * 0.044715) * square))
    half_up = 0.5 + 0.5 * tangent
    activated = (before * half_up).astype(LOW)
    slope = half_up + (0.5 * before) * (1.0 - tangent * tangent) * (
        GELU_COEF + (GELU_COEF * 3.0 * 0.044715) * square
    )
    grad_before_wide = dot_last(grad_feed[...], contract) * slope
    grad_before = grad_before_wide.astype(LOW)
    feed_term = dot_plain(activated, contract)
    second_term = dot_last(grad_before, expand)
    grad_expand = dot_first(second[...], grad_before).astype(LOW)
    grad_contract = dot_first(activated, grad_feed[...]).astype(LOW)
    sums = column_sum(grad_before.astype(WIDE))
    for k, owner in enumerate(owners):
        rows_out[pl.ds(8 + owner, 1), :] = sums[:, k * D : (k + 1) * D]

    @pl.when(core == 0)
    def _():
        for k in range(2):
            send_out[k] = grad_contract[k * D : (k + 1) * D, :]
            keep_out[k] = grad_expand[:, k * D : (k + 1) * D]

    @pl.when(core != 0)
    def _():
        for k in range(2):
            send_out[k] = grad_expand[:, k * D : (k + 1) * D]
            keep_out[k] = grad_contract[k * D : (k + 1) * D, :]

    @pl.when(step == 0)
    def _():
        feed[...] = feed_term
        grad_second[...] = second_term

    @pl.when(step > 0)
    def _():
        feed[...] += feed_term
        grad_second[...] += second_term

    @pl.when(step == 1)
    def _():
        for s, rows in enumerate(slots):
            pieces = mod[s]
            alive = jnp.where(s < live, 1.0, 0.0)
            feed_out = feed[rows, :] + bias[15:16, :]
            grad_out = cotangent[s].astype(WIDE) * alive
            out[s] = ((middle[rows, :] + pieces[5:6] * feed_out) * alive).astype(LOW)
            grad = grad_second[rows, :]
            unit = normed[rows, :]
            grad_middle = grad_out + norm_backward(
                grad * (1.0 + pieces[4:5]), unit, inverse[rows, 0:1]
            )
            grad_middle_out[s] = grad_middle
            rows_out[4 * s : 4 * s + 1, :] = column_sum(grad_middle * branch[rows, :])
            rows_out[4 * s + 1 : 4 * s + 2, :] = column_sum(grad)
            rows_out[4 * s + 2 : 4 * s + 3, :] = column_sum(grad * unit)
            rows_out[4 * s + 3 : 4 * s + 4, :] = column_sum(grad_out * feed_out)


def attention_backward_kernel(
    slot, where, tokens, grad_middle_in, joined, soft_in, mixed, mod, feed_rows, cond, att, proj, *refs
):
    rank, core = where[0], where[1]
    if slot == 0:
        grad_tokens_out, grad_joined, first_out, branch_out, rows = refs
    else:
        before_joined, before_first, before_branch, before_rows, _, _ = refs[:6]
        grad_tokens_out, send_out, keep_out, rows_out = refs[6:10]
        grad_joined, grad_att, grad_proj, rows = refs[10:]

    if slot == 0:
        rows[...] = jnp.zeros_like(rows)
        rows[12:14, :] = cond[...]
        rows[19:24, :] = feed_rows[8:13, :]
    else:
        rows[...] = before_rows[...]

    pieces = mod[0]
    grad_middle = grad_middle_in[0]
    grad_branch = (pieces[2:3] * grad_middle).astype(LOW)
    rows[18:19, :] += column_sum(grad_branch.astype(WIDE))
    if slot == 0:
        branch_out[...] = grad_branch
    else:
        grad_proj[...] = (
            dot_first(mixed[0], before_branch[...]) + dot_first(mixed[1], grad_branch)
        ).astype(LOW)
    grad_mixed = dot_last(grad_branch, proj[...]).astype(LOW)
    first_half = head_mask((SEQ, 128), 0)
    zero = jnp.zeros((SEQ, 128), LOW)
    scale = HEAD_DIM ** (-0.5)
    for pair in range(HEADS // 2):
        lanes = slice(pair * 128, (pair + 1) * 128)
        query = joined[0, :, pair * 128 : (pair + 1) * 128]
        key = joined[0, :, D + pair * 128 : D + (pair + 1) * 128]
        value = joined[0, :, 2 * D + pair * 128 : 2 * D + (pair + 1) * 128]
        grads = grad_mixed[:, lanes]
        results = []
        for half in range(2):
            soft = soft_in[0, 2 * pair + half]
            masked = (
                jnp.where(first_half, grads, zero)
                if half == 0
                else jnp.where(first_half, zero, grads)
            )
            grad_soft = dot_last(masked, value)
            grad_values = dot_first(soft, grads)
            soft_wide = soft.astype(WIDE)
            weighted = soft_wide * grad_soft
            inner = jnp.sum(weighted, axis=-1, keepdims=True)
            grad_scores = (weighted - soft_wide * inner).astype(LOW)
            results.append(
                (dot_plain(grad_scores, key), dot_first(grad_scores, query), grad_values)
            )
        for third in range(3):
            merged = jnp.where(first_half, results[0][third], results[1][third])
            if third < 2:
                merged = merged * scale
            grad_joined[:, third * D + pair * 128 : third * D + (pair + 1) * 128] = merged.astype(LOW)
    grads = grad_joined[...]
    sums = column_sum(grads.astype(WIDE))
    rows[16:17, :] += sums[:, :D]
    rows[17:18, :] += sums[:, 2 * D :]
    normed, inverse = layer_norm_parts(tokens[0].astype(WIDE))
    first_in = (normed * (1.0 + pieces[1:2]) + pieces[0:1]).astype(LOW)
    if slot == 0:
        first_out[...] = first_in
    else:
        for third in range(3):
            lanes = slice(third * D, (third + 1) * D)
            grad_att[:, lanes] = (
                dot_first(before_first[...], before_joined[:, lanes])
                + dot_first(first_in, grad_joined[:, lanes])
            ).astype(LOW)
    grad_first = dot_last(grads, att[...])
    grad_tokens_out[0] = (
        grad_middle + norm_backward(grad_first * (1.0 + pieces[1:2]), normed, inverse)
    ).astype(LOW)
    own_rows = jnp.concatenate(
        [
            column_sum(grad_first),
            column_sum(grad_first * normed),
        ],
        axis=0,
    )

    rows[6 * slot : 6 * slot + 2, :] = own_rows
    rows[6 * slot + 2 : 6 * slot + 6, :] = feed_rows[4 * slot : 4 * slot + 4, :]
    if slot == 0:
        return
    rows_out[...] = rows[...].astype(LOW)
    for k in range(4):
        start = pl.multiple_of((rank ^ k) * QUARTER, 32)
        block = grad_att[pl.ds(start, QUARTER), :]
        low_part = (block[:, :D], block[:, D : 2 * D])
        high_part = (block[:, 2 * D :], grad_proj[pl.ds(start, QUARTER), :])
        turned = (0, 2, 1, 3)[k]

        @pl.when(core == 0)
        def _():
            for j in range(2):
                keep_out[turned, j * QUARTER : (j + 1) * QUARTER, :] = low_part[j]
                send_out[k, j * QUARTER : (j + 1) * QUARTER, :] = high_part[j]

        @pl.when(core != 0)
        def _():
            for j in range(2):
                keep_out[k, j * QUARTER : (j + 1) * QUARTER, :] = high_part[j]
                send_out[turned, j * QUARTER : (j + 1) * QUARTER, :] = low_part[j]


def half_of(where, which):
    return (where[2] >> (where[1] ^ which)) & 1


def rows_at(index, count):
    return pl.ds(pl.multiple_of(index * count, 16), count)


def merge_small(out, own, arrived):
    count = own.shape[0] - BLOCK
    out[0:count, :] = own[0:count, :]
    out[count : 2 * count, :] = arrived[0:count, :]
    out[2 * count :, :] = (
        own[count:, :].astype(WIDE) + arrived[count:, :].astype(WIDE)
    ).astype(LOW)


def step1_kernel(
    where, att_keep, att_in, feed_keep, feed_in, small, small_in,
    att_stay, att_go, feed_stay, feed_go, small_out, total,
):
    half = half_of(where, 0)
    count = D // 2
    att_stay[...] = att_keep[0] + att_in[0].astype(WIDE)
    att_go[...] = (att_keep[1] + att_in[1].astype(WIDE)).astype(LOW)
    total[...] = feed_keep[...] + feed_in[...].astype(WIDE)
    feed_stay[...] = total[rows_at(half, count), :]
    feed_go[...] = total[rows_at(1 - half, count), :].astype(LOW)
    merge_small(small_out, small, small_in)


def step2_kernel(where, att_keep, att_in, feed_keep, feed_in, small, small_in, message, small_out):
    count = D // 2
    message[0:count, :] = (feed_keep[...] + feed_in[...].astype(WIDE)).astype(LOW)
    message[count:, :] = (att_keep[...] + att_in[...].astype(WIDE)).astype(LOW)
    merge_small(small_out, small, small_in)


def step3_kernel(where, own, arrived, small, small_in, message, small_out):
    message[...] = (own[...].astype(WIDE) + arrived[...].astype(WIDE)).astype(LOW)
    merge_small(small_out, small, small_in)


def step4_kernel(
    where, own, arrived, small, small_in, weight, att_part, feed_part, small_out, cond_keep, cond_go
):
    half = half_of(where, 0)
    count = D // 2
    feed_part[rows_at(half, count), :] = own[0:count, :]
    feed_part[rows_at(1 - half, count), :] = arrived[0:count, :]
    att_part[...] = (own[count:, :].astype(WIDE) + arrived[count:, :].astype(WIDE)).astype(LOW)
    merge_small(small_out, small, small_in)
    rows = [
        block[start : start + BLOCK, :].astype(WIDE)
        for block in (small, small_in)
        for start in (0, 4 * BLOCK)
    ]
    total = None
    for j in range(6):
        lines = [row[6 * slot + j : 6 * slot + j + 1] for row in rows for slot in range(2)]
        term = dot_last(
            jnp.concatenate(lines, axis=0).astype(LOW), weight[:, j * D : (j + 1) * D]
        )
        total = term if total is None else total + term
    padded = jnp.concatenate([total, jnp.zeros((8, 128 - QUARTER), WIDE)], axis=1)
    blank = jnp.zeros((4, 128), WIDE)
    cond_keep[...] = jnp.concatenate([padded[0:4], blank], axis=0)
    cond_go[...] = jnp.concatenate([padded[4:8], blank], axis=0)


def step5_kernel(where, cond_keep, cond_in, _, cond_go):
    blank = jnp.zeros((4, 128), WIDE)
    cond_go[...] = jnp.concatenate([cond_keep[2:4], cond_in[2:4], blank], axis=0)


def modulation_update_kernel(
    where, near, far, weight, mean, square, bias, bias_mean, bias_square,
    weight_out, mean_out, square_out, bias_out, bias_mean_out, bias_square_out, mark, everyone,
):
    rank, core, plane = where[0], where[1], where[2]
    for side, source in enumerate((near, far)):
        here = core ^ side
        first, second = 1 + here, 2 - here
        for index in range(16):
            a, b, c, d = (index & 1, (index >> 1) & 1, (index >> 2) & 1, index >> 3)
            z_at = plane ^ (a * first) ^ (b * second)
            g_at = rank ^ (c * second) ^ (d * first)
            place = (g_at * 4 + z_at) * 2 + here
            block = source[index * BLOCK : (index + 1) * BLOCK, :].astype(WIDE)
            for third in range(3):
                everyone[third, rows_at(place, BLOCK), :] = block[
                    :, third * 128 : (third + 1) * 128
                ]

    def line(at):
        parts = [everyone[third, pl.ds(at, 32, stride=BLOCK), :] for third in range(3)]
        return jnp.concatenate(parts, axis=1)

    def both(at, other):
        return jnp.concatenate([line(at), line(other)], axis=0)

    def own_lanes(values):
        chosen = values[:, :QUARTER]
        for place in range(1, 4):
            lanes = slice(place * QUARTER, (place + 1) * QUARTER)
            chosen = jnp.where(rank == place, values[:, lanes], chosen)
        return chosen

    cond = own_lanes(both(12, 13)).astype(LOW)
    sums = []
    for j in range(6):
        lanes = slice(j * D, (j + 1) * D)
        grads = both(j, 6 + j)
        sums.append(column_sum(grads))
        gradient = dot_first(cond, grads.astype(LOW))
        updated, momentum, variance = adam_update(
            weight[:, lanes].astype(WIDE),
            gradient,
            mean[:, lanes].astype(WIDE),
            square[:, lanes].astype(WIDE),
            LEARN_RATES[0],
            DECAY_FLAGS[0],
        )
        weight_out[:, lanes] = updated
        mean_out[:, lanes] = momentum
        square_out[:, lanes] = variance
    sums.append(near[16 * BLOCK :, :].astype(WIDE)[0:8] + far[16 * BLOCK :, :].astype(WIDE)[0:8])
    gradient = own_lanes(jnp.concatenate(sums, axis=0))
    updated, momentum, variance = adam_update(
        bias[...].astype(WIDE),
        gradient,
        bias_mean[...].astype(WIDE),
        bias_square[...].astype(WIDE),
        LEARN_RATES[5],
        DECAY_FLAGS[5],
    )
    bias_out[...] = updated
    bias_mean_out[...] = momentum
    bias_square_out[...] = variance
    mark[...] = jnp.zeros_like(mark)


def split_kernel(keep, arrived, stay, go):
    half = stay.shape[0]
    stay[...] = keep[:half].astype(WIDE) + arrived[:half].astype(WIDE)
    go[...] = (keep[half:].astype(WIDE) + arrived[half:].astype(WIDE)).astype(LOW)


def whole(shape):
    return pl.BlockSpec(shape, lambda *grid: (0,) * len(shape))


def by_slot(shape):
    return pl.BlockSpec((1,) + shape, lambda s: (s,) + (0,) * len(shape))


def shape_of(shape, dtype):
    return jax.ShapeDtypeStruct(shape, dtype)


SMEM_SPEC = pl.BlockSpec(memory_space=pltpu.SMEM)
PARAMS = pltpu.CompilerParams(vmem_limit_bytes=VMEM_BYTES)


ANY_SPEC = pl.BlockSpec(memory_space=pl.ANY)


def small_call(kernel, name, outs, where, *operands, scratch=(), after=(), params=PARAMS):
    return pl.pallas_call(
        kernel,
        grid=(1,),
        in_specs=[SMEM_SPEC]
        + [whole(item.shape) for item in operands]
        + [ANY_SPEC] * len(after),
        out_specs=[whole(shape) for shape, _ in outs],
        out_shape=[shape_of(*item) for item in outs],
        scratch_shapes=[pltpu.VMEM(*item) for item in scratch],
        compiler_params=params,
        name=name,
    )(where, *operands, *after)


def run_gate(value, *after, space=ANY_SPEC):
    return pl.pallas_call(
        gate_kernel,
        in_specs=[space] + [ANY_SPEC] * len(after),
        out_specs=space,
        out_shape=shape_of(value.shape, value.dtype),
        input_output_aliases={0: 0},
        compiler_params=pltpu.CompilerParams(vmem_limit_bytes=1024 * 1024),
        name="in_order",
    )(value, *after)


def run_relay(where, keep, arrived, passing):
    two = (2, keep.shape[1])
    return pl.pallas_call(
        relay_kernel,
        grid=(1,),
        in_specs=[SMEM_SPEC, whole(keep.shape), whole(arrived.shape), ANY_SPEC],
        out_specs=[whole(two), whole(two), ANY_SPEC],
        out_shape=[shape_of(two, WIDE)] * 2 + [shape_of(passing.shape, passing.dtype)],
        input_output_aliases={3: 2},
        compiler_params=PARAMS,
        name="relay",
    )(where, keep, arrived, passing)


def run_modulation(where, condition, biases, blocks, weight):
    message = pl.BlockSpec((16, D), lambda s: (2 * QUARTER // 16, 0))
    return pl.pallas_call(
        modulation_kernel,
        grid=(1,),
        in_specs=[SMEM_SPEC, whole((2, D)), whole((BIAS_ROWS, QUARTER))]
        + [message] * 3
        + [whole((QUARTER, 6 * D))],
        out_specs=[whole((4, 6 * D))] * 2 + [whole((16, D))],
        out_shape=[shape_of((4, 6 * D), WIDE)] * 2 + [shape_of((16, D), WIDE)],
        compiler_params=PARAMS,
        cost_estimate=pl.CostEstimate(flops=10**7, bytes_accessed=10**6, transcendentals=0),
        name="modulation_partials",
    )(where, condition, biases, *blocks, weight)


def run_attention_forward(where, tokens, stay, arrived, bias, own_att, own_proj, nears, fars):
    part = whole((2 * QUARTER + 16, D))
    return pl.pallas_call(
        attention_forward_kernel,
        grid=(2,),
        in_specs=[
            SMEM_SPEC,
            by_slot((SEQ, D)),
            whole((2, 6 * D)),
            whole((2, 6 * D)),
            whole((16, D)),
            whole((QUARTER, 3 * D)),
            whole((QUARTER, D)),
        ]
        + [part] * 6,
        out_specs=[
            by_slot((SEQ, 3 * D)),
            by_slot((HEADS, SEQ, SEQ)),
            by_slot((SEQ, D)),
            by_slot((6, D)),
            whole((D, 3 * D)),
            whole((D, D)),
        ],
        out_shape=[
            shape_of((2, SEQ, 3 * D), LOW),
            shape_of((2, HEADS, SEQ, SEQ), LOW),
            shape_of((2, SEQ, D), LOW),
            shape_of((2, 6, D), WIDE),
            shape_of((D, 3 * D), LOW),
            shape_of((D, D), LOW),
        ],
        compiler_params=PARAMS,
        cost_estimate=pl.CostEstimate(
            flops=3 * 10**9, bytes_accessed=6 * 10**6, transcendentals=10**6
        ),
        name="attention_forward",
    )(where, tokens, stay, arrived, bias, own_att, own_proj, *nears, *fars)


def run_feed(where, mixed, tokens, cotangent, mod, bias, proj, own_expand, own_contract, nears, fars):
    rows = 2 * SEQ

    return pl.pallas_call(
        feed_kernel,
        grid=(2,),
        in_specs=[SMEM_SPEC]
        + [whole((2, SEQ, D))] * 3
        + [whole((2, 6, D)), whole((16, D))]
        + [whole((D, D))] * 9,
        out_specs=[
            whole((2, SEQ, D)),
            whole((2, SEQ, D)),
            pl.BlockSpec((2, D, D), lambda i: (i, 0, 0)),
            pl.BlockSpec((2, D, D), lambda i: (i, 0, 0)),
            whole((16, D)),
        ],
        scratch_shapes=[
            pltpu.VMEM((2, D, 2 * D), LOW),
            pltpu.VMEM((2, 2 * D, D), LOW),
            pltpu.VMEM((rows, D), WIDE),
            pltpu.VMEM((rows, D), WIDE),
            pltpu.VMEM((rows, D), LOW),
            pltpu.VMEM((rows, D), WIDE),
            pltpu.VMEM((rows, 128), WIDE),
            pltpu.VMEM((rows, D), LOW),
            pltpu.VMEM((rows, D), WIDE),
            pltpu.VMEM((rows, D), WIDE),
        ],
        out_shape=[
            shape_of((2, SEQ, D), LOW),
            shape_of((2, SEQ, D), WIDE),
            shape_of((4, D, D), LOW),
            shape_of((4, D, D), LOW),
            shape_of((16, D), WIDE),
        ],
        compiler_params=PARAMS,
        cost_estimate=pl.CostEstimate(
            flops=8 * 10**9, bytes_accessed=10**7, transcendentals=10**6
        ),
        name="feed_forward_and_back",
    )(where, mixed, tokens, cotangent, mod, bias, proj, own_expand, own_contract, *nears, *fars)


def run_attention_backward(
    slot, where, tokens, grad_middle, joined, soft, mixed, mod, feed_rows, cond, att, proj, earlier=()
):
    def at_slot(shape):
        return pl.BlockSpec((1,) + shape, lambda i: (slot,) + (0,) * len(shape))

    passed = [((SEQ, 3 * D), LOW), ((SEQ, D), LOW), ((SEQ, D), LOW), ((SMALL, D), WIDE)]
    in_specs = [
        SMEM_SPEC,
        at_slot((SEQ, D)),
        at_slot((SEQ, D)),
        at_slot((SEQ, 3 * D)),
        at_slot((HEADS, SEQ, SEQ)),
        whole((2, SEQ, D)),
        at_slot((6, D)),
        whole((16, D)),
        whole((2, D)),
        whole((D, 3 * D)),
        whole((D, D)),
    ]
    out_specs = [at_slot((SEQ, D))]
    out_shape = [shape_of((2, SEQ, D), LOW)]
    scratch = []
    aliases = {}
    if slot == 0:
        out_specs += [whole(shape) for shape, _ in passed]
        out_shape += [shape_of(*item) for item in passed]
    else:
        in_specs += [whole(shape) for shape, _ in passed] + [ANY_SPEC, ANY_SPEC]
        aliases = {15: 0}
        out_specs += [whole((4, 2 * QUARTER, D))] * 2 + [whole((SMALL, D))]
        out_shape += [shape_of((4, 2 * QUARTER, D), LOW)] * 2 + [shape_of((SMALL, D), LOW)]
        sums = [((D, 3 * D), LOW), ((D, D), LOW)]
        scratch = [pltpu.VMEM(*item) for item in (passed[0], *sums, passed[3])]
    return pl.pallas_call(
        functools.partial(attention_backward_kernel, slot),
        grid=(1,),
        in_specs=in_specs,
        out_specs=out_specs,
        out_shape=out_shape,
        scratch_shapes=scratch,
        input_output_aliases=aliases,
        compiler_params=PARAMS,
        cost_estimate=pl.CostEstimate(
            flops=4 * 10**9, bytes_accessed=8 * 10**6, transcendentals=0
        ),
        name="attention_backward",
    )(where, tokens, grad_middle, joined, soft, mixed, mod, feed_rows, cond, att, proj, *earlier)


def turn_split_kernel(where, keep, arrived, stay, go):
    core = where[1]
    for place, block in enumerate((0, 2 - core)):
        stay[place] = keep[block].astype(WIDE) + arrived[block].astype(WIDE)
    for place, block in enumerate((1 + core, 3)):
        go[place] = (keep[block].astype(WIDE) + arrived[block].astype(WIDE)).astype(LOW)


def run_split(keep, arrived):
    count, rest = keep.shape[0], keep.shape[1:]
    half = (count // 2,) + rest
    return pl.pallas_call(
        split_kernel,
        grid=(1,),
        in_specs=[whole(keep.shape)] * 2,
        out_specs=[whole(half)] * 2,
        out_shape=[shape_of(half, WIDE), shape_of(half, LOW)],
        compiler_params=PARAMS,
        name="sum_and_split",
    )(keep, arrived)


def swap_plane(value, which):
    pairs = [(r, r ^ ((1 + ((r + which) & 1)) << 1)) for r in range(lax.axis_size("replica"))]
    return lax.ppermute(value, "replica", pairs)


def swap_pair(value, which):
    groups, copies = lax.axis_size("group"), lax.axis_size("replica")
    pairs = []
    for g in range(groups):
        for r in range(copies):
            other = g ^ (1 if (r + which) % 2 == 0 else 2)
            pairs.append((g * copies + r, other * copies + r))
    return lax.ppermute(value, ("group", "replica"), pairs)


def gather_pair(value):
    first = swap_pair(value, 0)
    second = swap_pair(value, 1)
    return (first, second, swap_pair(first, 1))


def update_all(stored, gradients, means, squares, kinds):
    return [
        adam_update(
            stored[kind].astype(jnp.float32),
            gradient,
            means[kind].astype(jnp.float32),
            squares[kind].astype(jnp.float32),
            LEARN_RATES[kind],
            DECAY_FLAGS[kind],
        )
        for kind, gradient in zip(kinds, gradients)
    ]


def by_core(core, own, other):
    return (
        jnp.where(core == 0, own, other).astype(jnp.float32),
        jnp.where(core == 0, other, own).astype(jnp.float32),
    )


def attention_shards(totals):
    joined = jnp.concatenate(
        [totals[0][:QUARTER], totals[0][QUARTER:], totals[1][:QUARTER]], axis=1
    )
    return (joined, totals[1][QUARTER:])


def tail_in_step(
    where, copy, stages, condition, ffn_halves, att_parts, small_rows, stored, means, squares
):
    core = where[1]
    (feed_stay, feed_in), (att_send, att_keep) = ffn_halves, att_parts
    half, third = (D // 2, D), (2 * QUARTER, D)
    att_stay, att_go = run_split(att_keep, swap_replica(att_send, 1))
    feed_stay, feed_go = run_split(feed_stay, feed_in)
    feed_stay, feed_go = feed_stay[0], feed_go[0]
    att_stay, att_go, feed_stay, feed_go, small = small_call(
        step1_kernel, "step_1",
        [(third, WIDE), (third, LOW), (half, WIDE), (half, LOW), ((3 * BLOCK, D), LOW)],
        where, att_stay, swap_pair(att_go, 0), feed_stay, swap_pair(feed_go, 1),
        small_rows, swap_plane(small_rows, 0),
        scratch=[((D, D), WIDE)],
    )
    message, small = small_call(
        step2_kernel, "step_2",
        [((D, D), LOW), ((5 * BLOCK, D), LOW)],
        where, att_stay, swap_pair(att_go, 1), feed_stay, swap_plane(feed_go, 0),
        small, swap_plane(small, 1),
    )
    message, small = small_call(
        step3_kernel, "step_3",
        [((D, D), LOW), ((9 * BLOCK, D), LOW)],
        where, message, swap_plane(message, 1), small, swap_pair(small, 1),
    )
    att_part, feed_part, small, cond_keep, cond_go = small_call(
        step4_kernel, "step_4",
        [(third, LOW), ((D, D), LOW), ((17 * BLOCK, D), LOW), ((8, 128), WIDE), ((8, 128), WIDE)],
        where, message, swap_plane(message, 0), small, swap_pair(small, 0), stored[0],
    )
    shard = [((QUARTER, 6 * D), WIDE)] * 3 + [((BIAS_ROWS, QUARTER), WIDE)] * 3
    *updates, mark = small_call(
        modulation_update_kernel, "modulation_update", shard + [((8, 128), WIDE)],
        where, small, swap_replica(small, 1), stored[0], means[0], squares[0],
        stored[5], means[5], squares[5],
        scratch=[((3, 32 * BLOCK, 128), WIDE)],
    )
    feed_totals = by_core(core, feed_part, swap_replica(feed_part, 1))
    feed_updates = update_all(stored, feed_totals, means, squares, (3, 4))
    cond_in = swap_pair(cond_go, 0)
    cond_go = small_call(
        step5_kernel, "step_5", [((8, 128), WIDE)], where, cond_keep, cond_in, after=(mark,)
    )[0]
    cond_last = swap_pair(cond_go, 1)
    att_totals = by_core(core, att_part, swap_replica(att_part, 1))
    blocks = [
        block[:, :QUARTER] for block in (cond_keep[:2], cond_in[:2], cond_last[:2], cond_last[2:4])
    ]
    owners = (where[0],) + neighbours(where)
    lanes = []
    for place in range(4):
        chosen = blocks[0]
        for k in range(1, 4):
            chosen = jnp.where(owners[k] == place, blocks[k], chosen)
        lanes.append(chosen)
    sigmoid_cond = jax.nn.sigmoid(condition)
    grad_condition = (
        jnp.concatenate(lanes, axis=1) * sigmoid_cond * (1.0 + condition * (1.0 - sigmoid_cond))
    )
    att_updates = update_all(stored, attention_shards(att_totals), means, squares, (1, 2))
    return grad_condition, [updates[:3]] + att_updates + feed_updates + [updates[3:]]


def tail_in_turn(
    where, copy, stages, condition, ffn_halves, att_parts, small_rows, stored, means, squares
):
    rank, core = where[0], where[1]
    slot_count, model_width = condition.shape
    modulation, cond_low = stored[0], jax.nn.silu(condition).astype(jnp.bfloat16)
    (ffn_stay, ffn_in), (att_send, att_keep) = ffn_halves, att_parts
    ffn_stay, ffn_go = run_split(ffn_stay, ffn_in)
    ffn_totals = reduce_replicas(
        wide_sum([ffn_stay[0], swap_pair(ffn_go[0], 1)]).astype(LOW), copy, stages
    )
    att_stay, att_go = run_split(att_keep, swap_replica(att_send, 1))
    att_stay, att_go = run_split(att_stay, swap_pair(att_go, 0))
    att_totals = reduce_replicas(
        wide_sum([att_stay[0], swap_pair(att_go[0], 1)]).astype(LOW), copy, stages
    )
    row_total = small_rows.shape[0]
    gathered = small_rows[None]
    for low_bit, radix in stages[1:]:
        digit = (copy >> low_bit) % radix
        gathered = in_order(
            [swap_replica(gathered, k << low_bit) for k in range(radix)], digit
        ).reshape(-1, row_total, model_width)
    gathered = in_order([swap_group(gathered, k) for k in range(4)], rank)
    own_plane = lax.dynamic_index_in_dim(gathered, copy >> 1, axis=1, keepdims=False)
    group_mod = own_plane[:, : 6 * slot_count].reshape(4 * slot_count, 6 * model_width)
    grad_cond_columns = dot_last(group_mod, modulation).reshape(4, slot_count, model_width // 4)
    cond_back = in_order(
        [swap_group(pick(grad_cond_columns, rank ^ k), k) for k in range(4)], rank
    )
    sigmoid_cond = jax.nn.sigmoid(condition)
    grad_condition = (
        jnp.swapaxes(cond_back, 0, 1).reshape(slot_count, model_width)
        * sigmoid_cond
        * (1.0 + condition * (1.0 - sigmoid_cond))
    )
    everyone = in_order([swap_replica(gathered, k) for k in range(2)], core).reshape(
        -1, row_total, model_width
    )
    all_mod = everyone[:, : 6 * slot_count].reshape(-1, 6 * model_width)
    all_cond = everyone[:, 6 * slot_count : 7 * slot_count].reshape(-1, model_width)
    cond_own = lax.dynamic_slice_in_dim(all_cond, rank * (model_width // 4), model_width // 4, 1)
    grad_mod = dot_first(cond_own, all_mod)
    mod_bias_grad = jnp.sum(all_mod, axis=0, dtype=jnp.float32).reshape(6, model_width)
    rest_bias_grad = jnp.sum(everyone[:, BLOCK : BLOCK + 8], axis=0, dtype=jnp.float32)
    bias_grad = lax.dynamic_slice_in_dim(
        jnp.concatenate([mod_bias_grad, rest_bias_grad], axis=0),
        rank * (model_width // 4),
        model_width // 4,
        1,
    )
    grad_att_own = jnp.concatenate(
        [att_totals[0][:QUARTER], att_totals[0][QUARTER:], att_totals[1][:QUARTER]], axis=1
    )
    totals = (
        grad_mod,
        grad_att_own,
        att_totals[1][QUARTER:],
        ffn_totals[0],
        ffn_totals[1],
        bias_grad,
    )
    return grad_condition, update_all(stored, totals, means, squares, range(6))


def shards(
    latents,
    condition,
    cotangent,
    live_counts,
    modulation,
    attending,
    projection,
    expand,
    contract,
    biases,
    modulation_mean,
    attending_mean,
    projection_mean,
    expand_mean,
    contract_mean,
    biases_mean,
    modulation_square,
    attending_square,
    projection_square,
    expand_square,
    contract_square,
    biases_square,
):
    slot_count, length, model_width = latents.shape
    rank = lax.axis_index("group")
    copy = lax.axis_index("replica")
    core = copy % 2
    stages = replica_stages(lax.axis_size("replica"))
    where = jnp.stack([rank, core, copy >> 1, live_counts[0]]).astype(jnp.int32)

    cond_low = jax.nn.silu(condition).astype(LOW)
    payload, feed_part = small_call(
        payload_kernel, "own_payload",
        [((2 * QUARTER + 16, model_width), LOW), ((model_width, model_width), LOW)],
        where, condition, attending, projection, biases, expand, contract,
        params=pltpu.CompilerParams(vmem_limit_bytes=60 * 1024 * 1024),
    )
    first, second = swap_pair(payload, 0), swap_pair(payload, 1)
    last, first_far = swap_pair(first, 1), swap_replica(first, 1)
    feed_part = run_gate(
        feed_part, first_far, second, space=pl.BlockSpec(memory_space=pltpu.HBM)
    )
    nears = (first, second, last)
    fars = [first_far, swap_replica(second, 1), swap_replica(last, 1)]
    feed_first, feed_second = swap_pair(feed_part, 0), swap_pair(feed_part, 1)
    stay, go, bias = run_modulation(where, condition, biases, nears, modulation)
    stay, go, feed_first = run_relay(where, stay, swap_pair(go, 0), feed_first)
    arrived = swap_pair(go, 1)
    feed_last = swap_pair(feed_first, 1)
    joined, soft, mixed, mod, att, proj = run_attention_forward(
        where, latents, stay, arrived, bias, attending, projection, nears, fars
    )
    feed_nears = (feed_first, feed_second, run_gate(feed_last, mod))
    feed_fars = [swap_replica(item, 1) for item in feed_nears]
    out_latents, grad_middle, ffn_send, ffn_keep, feed_rows = run_feed(
        where, mixed, latents, cotangent, mod, bias, proj, expand, contract, feed_nears, feed_fars
    )
    cond_wide = cond_low.astype(WIDE)
    two_blocks = (2, model_width, model_width)
    ffn_stay, ffn_go = small_call(
        turn_split_kernel, "sum_and_split", [(two_blocks, WIDE), (two_blocks, LOW)],
        where, ffn_keep, swap_replica(ffn_send, 1),
    )
    earlier = run_attention_backward(
        0, where, latents, grad_middle, joined, soft, mixed, mod, feed_rows, cond_wide, att, proj
    )
    ffn_in = swap_pair(ffn_go, 0)
    grad_latents, att_send, att_keep, small_rows = run_attention_backward(
        1, where, latents, grad_middle, joined, soft, mixed, mod, feed_rows, cond_wide, att, proj,
        (*earlier[1:], earlier[0], ffn_go),
    )
    tail = tail_in_step if lax.axis_size("replica") == 8 else tail_in_turn
    grad_condition, results = tail(
        where, copy, stages, condition, (ffn_stay, ffn_in), (att_send, att_keep), small_rows,
        (modulation, attending, projection, expand, contract, biases),
        (
            modulation_mean, attending_mean, projection_mean,
            expand_mean, contract_mean, biases_mean,
        ),
        (
            modulation_square, attending_square, projection_square,
            expand_square, contract_square, biases_square,
        ),
    )
    return (
        out_latents,
        grad_latents,
        grad_condition,
        results[0][0],
        results[1][0],
        results[2][0],
        results[3][0],
        results[4][0],
        results[5][0],
        results[0][1],
        results[1][1],
        results[2][1],
        results[3][1],
        results[4][1],
        results[5][1],
        results[0][2],
        results[1][2],
        results[2][2],
        results[3][2],
        results[4][2],
        results[5][2],
    )


def solution(mesh):
    return jax.shard_map(
        shards,
        mesh=mesh,
        in_specs=(
            P(("group", "replica"), None, None),
            P(("group", "replica"), None),
            P(("group", "replica"), None, None),
            P(("group", "replica")),
            P("group", None),
            P("group", None),
            P("group", None),
            P(None, "group"),
            P("group", None),
            P(None, "group"),
            P("group", None),
            P("group", None),
            P("group", None),
            P(None, "group"),
            P("group", None),
            P(None, "group"),
            P("group", None),
            P("group", None),
            P("group", None),
            P(None, "group"),
            P("group", None),
            P(None, "group"),
        ),
        out_specs=(
            P(("group", "replica"), None, None),
            P(("group", "replica"), None, None),
            P(("group", "replica"), None),
            P("group", None),
            P("group", None),
            P("group", None),
            P(None, "group"),
            P("group", None),
            P(None, "group"),
            P("group", None),
            P("group", None),
            P("group", None),
            P(None, "group"),
            P("group", None),
            P(None, "group"),
            P("group", None),
            P("group", None),
            P("group", None),
            P(None, "group"),
            P("group", None),
            P(None, "group"),
        ),
        check_vma=False,
    )
```

```python
import functools

import jax
import jax.numpy as jnp
from jax import lax
from jax.experimental import pallas as pl
from jax.experimental.pallas import tpu as pltpu
from jax.sharding import PartitionSpec as P

HEADS = 6
HEAD_DIM = 64
FF = 1536
STEP = 10


NORM_EPS = 1e-06
ADAM_EPS = 1e-08
BETA_FIRST = 0.9
BETA_SECOND = 0.999
DECAY_RATE = 0.1
LEARN_RATES = (0.05, 0.05, 0.2, 0.05, 0.025, 0.1)
DECAY_FLAGS = (1.0, 1.0, 1.0, 1.0, 1.0, 0.0)
GELU_COEF = 0.7978845608028654
BIAS_ROWS = 14
D = 384
SEQ = 256
QUARTER = D // 4
VMEM_BYTES = 34 * 1024 * 1024
LOW = jnp.bfloat16
SMALL = 32
BLOCK = 16
WIDE = jnp.float32


def dot_plain(left_side, right_side):
    return jnp.dot(left_side, right_side, preferred_element_type=WIDE)


def dot_first(left_side, right_side):
    return lax.dot_general(
        left_side, right_side, (((0,), (0,)), ((), ())), preferred_element_type=WIDE
    )


def dot_last(left_side, right_side):
    return lax.dot_general(
        left_side, right_side, (((1,), (1,)), ((), ())), preferred_element_type=WIDE
    )


def adam_update(weight, gradient, mean_old, square_old, step_rate, decay_flag):
    momentum = BETA_FIRST * mean_old + (1.0 - BETA_FIRST) * gradient
    variance = BETA_SECOND * square_old + ((1.0 - BETA_SECOND) * gradient) * gradient
    root = variance * lax.rsqrt(variance)
    bottom = root * (1.0 - BETA_SECOND**STEP) ** (-0.5) + ADAM_EPS
    change = momentum * (step_rate / (1.0 - BETA_FIRST**STEP)) / bottom
    updated = weight * (1.0 - step_rate * decay_flag * DECAY_RATE) - change
    return (updated, momentum, variance)


def replica_stages(count):
    stages, low_bit = [(0, 2)], 1
    while (1 << low_bit) < count:
        radix = min(4, count >> low_bit)
        stages.append((low_bit, radix))
        low_bit += radix.bit_length() - 1
    return stages


def swap_group(value, k):
    if k == 0:
        return value
    return lax.ppermute(value, "group", [(i, i ^ k) for i in range(lax.axis_size("group"))])


def swap_replica(value, k):
    if k == 0:
        return value
    return lax.ppermute(value, "replica", [(i, i ^ k) for i in range(lax.axis_size("replica"))])


def pick(blocks, index):
    return lax.dynamic_index_in_dim(blocks, index, axis=0, keepdims=False)


def in_order(blocks, digit):
    ordered = []
    for place in range(len(blocks)):
        chosen = blocks[0]
        for k in range(1, len(blocks)):
            chosen = jnp.where((digit ^ k) == place, blocks[k], chosen)
        ordered.append(chosen)
    return jnp.stack(ordered)


def wide_sum(blocks):
    total = blocks[0].astype(jnp.float32)
    for block in blocks[1:]:
        total = total + block.astype(jnp.float32)
    return total


def scatter_stage(value, digit, low_bit, radix):
    rows = value.shape[-2] // radix
    parts = [
        lax.dynamic_slice_in_dim(value, (digit ^ k) * rows, rows, value.ndim - 2)
        for k in range(radix)
    ]
    received = [swap_replica(parts[k], k << low_bit) for k in range(radix)]
    return wide_sum(received).astype(jnp.bfloat16)


def reduce_replicas(value, copy, stages):
    core = copy % 2
    for low_bit, radix in stages[1:]:
        value = scatter_stage(value, (copy >> low_bit) % radix, low_bit, radix)
    for low_bit, radix in reversed(stages[1:]):
        blocks = [swap_replica(value, k << low_bit) for k in range(radix)]
        value = in_order(blocks, (copy >> low_bit) % radix)
        value = value.reshape(-1, value.shape[-1])
    other = swap_replica(value, 1)
    return (
        jnp.where(core == 0, value, other).astype(jnp.float32),
        jnp.where(core == 0, other, value).astype(jnp.float32),
    )


def layer_norm_parts(values):
    centred = values - jnp.mean(values, axis=-1, keepdims=True)
    inverse = lax.rsqrt(jnp.mean(centred * centred, axis=-1, keepdims=True) + NORM_EPS)
    return (centred * inverse, inverse)


def norm_backward(grad_normed, normed, inverse):
    mean_grad = jnp.mean(grad_normed, axis=-1, keepdims=True)
    mean_cross = jnp.mean(grad_normed * normed, axis=-1, keepdims=True)
    return inverse * (grad_normed - mean_grad - normed * mean_cross)


def column_sum(values):
    return jnp.sum(values, axis=0, keepdims=True)


def head_mask(shape, which):
    lane = lax.broadcasted_iota(jnp.int32, shape, 1)
    return (lane < HEAD_DIM) if which == 0 else (lane >= HEAD_DIM)


def place_rows(target, lanes, block, owner):
    start = pl.multiple_of(owner * QUARTER, 32)
    target[pl.ds(start, QUARTER), lanes] = block


def neighbours(where):
    rank, core = where[0], where[1]
    return (rank ^ (1 + core), rank ^ (2 - core), rank ^ 3)


def own_message(condition, biases):
    cond = condition[...]
    active = cond / (1.0 + jnp.exp(-cond))
    padded = jnp.concatenate(
        [biases[...].astype(WIDE), jnp.zeros((BIAS_ROWS, D - QUARTER), WIDE)], axis=1
    )
    return jnp.concatenate([active, padded], axis=0)


def payload_kernel(condition, attending, projection, biases, expand, contract, out, part, sem):
    core = lax.axis_index("replica") % 2

    @pl.when(core == 0)
    def _():
        pltpu.make_async_copy(expand, part, sem).start()
        out[0:QUARTER, :] = attending[:, 0:D]
        out[QUARTER : 2 * QUARTER, :] = attending[:, D : 2 * D]

    @pl.when(core != 0)
    def _():
        pltpu.make_async_copy(contract, part, sem).start()
        out[0:QUARTER, :] = attending[:, 2 * D : 3 * D]
        out[QUARTER : 2 * QUARTER, :] = projection[...]

    out[2 * QUARTER :, :] = own_message(condition, biases).astype(LOW)
    pltpu.make_async_copy(expand, part, sem).wait()


def modulation_kernel(
    where, condition, biases, first, second, last, weight, stay, go, bias_out
):
    rank = where[0]
    owners = (rank,) + neighbours(where)
    rows = [own_message(condition, biases)]
    rows += [block[...].astype(WIDE) for block in (first, second, last)]
    conds = jnp.concatenate([rows[0][0:2], rows[2][0:2], rows[1][0:2], rows[3][0:2]], axis=0)
    columns = conds[:, :QUARTER]
    for place in range(1, 4):
        lanes = slice(place * QUARTER, (place + 1) * QUARTER)
        columns = jnp.where(rank == place, conds[:, lanes], columns)
    partial = dot_plain(columns.astype(LOW), weight[...])
    stay[...] = partial[:4]
    go[...] = partial[4:]
    lanes = []
    for place in range(4):
        chosen = rows[0][:, :QUARTER]
        for k in range(1, 4):
            chosen = jnp.where(owners[k] == place, rows[k][:, :QUARTER], chosen)
        lanes.append(chosen)
    bias_out[...] = jnp.concatenate(lanes, axis=1)


def relay_kernel(where, keep, arrived, _, stay, go, __):
    stay[...] = keep[0:2, :] + arrived[0:2, :]
    go[...] = keep[2:4, :] + arrived[2:4, :]


def gate_kernel(*refs):
    pass


def attention_forward_kernel(
    where, tokens, stay, arrived, bias, own_att, own_proj, n1, n2, n3, f1, f2, f3,
    joined_out, soft_out, mixed_out, mod_out, att, proj,
):
    slot = pl.program_id(0)
    rank = where[0]

    core = where[1]

    def assemble(lows, highs):
        for k, block in zip((1, 2, 3), lows):
            place_rows(att, slice(0, D), block[0:QUARTER, :], rank ^ k)
            place_rows(att, slice(D, 2 * D), block[QUARTER : 2 * QUARTER, :], rank ^ k)
        for k, block in zip((2, 1, 3), highs):
            place_rows(att, slice(2 * D, 3 * D), block[0:QUARTER, :], rank ^ k)
            place_rows(proj, slice(0, D), block[QUARTER : 2 * QUARTER, :], rank ^ k)

    @pl.when(slot == 0)
    def _():
        place_rows(att, slice(0, 3 * D), own_att[...], rank)
        place_rows(proj, slice(0, D), own_proj[...], rank)

        @pl.when(core == 0)
        def _():
            assemble((n1, n2, n3), (f1, f2, f3))

        @pl.when(core != 0)
        def _():
            assemble((f1, f2, f3), (n1, n2, n3))

    summed = stay[...] + arrived[...]
    row = jnp.where(slot == 0, summed[0:1], summed[1:2])
    pieces = [row[:, j * D : (j + 1) * D] + bias[2 + j : 3 + j, :] for j in range(6)]
    mod_out[0] = jnp.concatenate(pieces, axis=0)
    normed, _ = layer_norm_parts(tokens[0].astype(WIDE))
    first_in = (normed * (1.0 + pieces[1]) + pieces[0]).astype(LOW)
    thirds = []
    for third in range(3):
        part = dot_plain(first_in, att[:, third * D : (third + 1) * D])
        if third == 0:
            part = part + bias[8:9, :]
        if third == 2:
            part = part + bias[9:10, :]
        part = part.astype(LOW)
        joined_out[0, :, third * D : (third + 1) * D] = part
        thirds.append(part)
    first_half = head_mask((SEQ, 128), 0)
    scale = jnp.asarray(HEAD_DIM ** (-0.5), LOW)
    zero = jnp.zeros((SEQ, 128), LOW)
    for pair in range(HEADS // 2):
        lanes = slice(pair * 128, (pair + 1) * 128)
        query, key, value = (part[:, lanes] for part in thirds)
        query = query * scale
        outs = []
        for half in range(2):
            masked = (
                jnp.where(first_half, query, zero)
                if half == 0
                else jnp.where(first_half, zero, query)
            )
            scores = dot_last(masked, key)
            weights = jnp.exp(scores - jnp.max(scores, axis=-1, keepdims=True))
            total = jnp.sum(weights, axis=-1, keepdims=True)
            soft = (weights * (1.0 / total)).astype(LOW)
            soft_out[0, 2 * pair + half] = soft
            outs.append(dot_plain(soft, value))
        mixed_out[0, :, lanes] = jnp.where(first_half, outs[0], outs[1]).astype(LOW)


def feed_kernel(
    where, mixed, tokens, cotangent, mod, bias, proj, own_expand, own_contract, n1, n2, n3, f1, f2, f3,
    out, grad_middle_out, send_out, keep_out, rows_out,
    expands, contracts, branch, middle, second, normed, inverse, grad_feed, feed, grad_second,
):
    step = pl.program_id(0)
    rank, core, live = where[0], where[1], where[3]

    def assemble(lows, highs):
        for k, block in zip((1, 2, 3), lows):
            expands[k // 2, :, (k % 2) * D : (k % 2 + 1) * D] = block[...]
        for k, block in zip((2, 1, 3), highs):
            contracts[k // 2, (k % 2) * D : (k % 2 + 1) * D, :] = block[...]

    slots = [slice(s * SEQ, (s + 1) * SEQ) for s in range(2)]

    @pl.when(step == 0)
    def _():
        expands[0, :, 0:D] = own_expand[...]
        contracts[0, 0:D, :] = own_contract[...]

        @pl.when(core == 0)
        def _():
            assemble((n1, n2, n3), (f1, f2, f3))

        @pl.when(core != 0)
        def _():
            assemble((f1, f2, f3), (n1, n2, n3))

        for s, rows in enumerate(slots):
            pieces = mod[s]
            value = dot_plain(mixed[s], proj[...]) + bias[10:11, :]
            branch[rows, :] = value
            centre = tokens[s].astype(WIDE) + pieces[2:3] * value
            middle[rows, :] = centre
            unit, spread = layer_norm_parts(centre)
            normed[rows, :] = unit
            inverse[rows, :] = jnp.broadcast_to(spread, (SEQ, 128))
            second[rows, :] = (unit * (1.0 + pieces[4:5]) + pieces[3:4]).astype(LOW)
            alive = jnp.where(s < live, 1.0, 0.0)
            grad_feed[rows, :] = (
                pieces[5:6] * (cotangent[s].astype(WIDE) * alive)
            ).astype(LOW)
        rows_out[...] = jnp.zeros_like(rows_out)
        rows_out[12:13, :] = column_sum(grad_feed[...].astype(WIDE))

    owners = (rank ^ (2 * step), rank ^ (2 * step + 1))
    hidden_bias = jnp.concatenate([bias[pl.ds(11 + owner, 1), :] for owner in owners], axis=1)
    expand, contract = expands[step], contracts[step]
    before = dot_plain(second[...], expand) + hidden_bias
    square = before * before
    tangent = jnp.tanh(before * (GELU_COEF + (GELU_COEF * 0.044715) * square))
    half_up = 0.5 + 0.5 * tangent
    activated = (before * half_up).astype(LOW)
    slope = half_up + (0.5 * before) * (1.0 - tangent * tangent) * (
        GELU_COEF + (GELU_COEF * 3.0 * 0.044715) * square
    )
    grad_before_wide = dot_last(grad_feed[...], contract) * slope
    grad_before = grad_before_wide.astype(LOW)
    feed_term = dot_plain(activated, contract)
    second_term = dot_last(grad_before, expand)
    grad_expand = dot_first(second[...], grad_before).astype(LOW)
    grad_contract = dot_first(activated, grad_feed[...]).astype(LOW)
    sums = column_sum(grad_before.astype(WIDE))
    for k, owner in enumerate(owners):
        rows_out[pl.ds(8 + owner, 1), :] = sums[:, k * D : (k + 1) * D]

    @pl.when(core == 0)
    def _():
        for k in range(2):
            send_out[k] = grad_contract[k * D : (k + 1) * D, :]
            keep_out[k] = grad_expand[:, k * D : (k + 1) * D]

    @pl.when(core != 0)
    def _():
        for k in range(2):
            send_out[k] = grad_expand[:, k * D : (k + 1) * D]
            keep_out[k] = grad_contract[k * D : (k + 1) * D, :]

    @pl.when(step == 0)
    def _():
        feed[...] = feed_term
        grad_second[...] = second_term

    @pl.when(step > 0)
    def _():
        feed[...] += feed_term
        grad_second[...] += second_term

    @pl.when(step == 1)
    def _():
        for s, rows in enumerate(slots):
            pieces = mod[s]
            alive = jnp.where(s < live, 1.0, 0.0)
            feed_out = feed[rows, :] + bias[15:16, :]
            grad_out = cotangent[s].astype(WIDE) * alive
            out[s] = ((middle[rows, :] + pieces[5:6] * feed_out) * alive).astype(LOW)
            grad = grad_second[rows, :]
            unit = normed[rows, :]
            grad_middle = grad_out + norm_backward(
                grad * (1.0 + pieces[4:5]), unit, inverse[rows, 0:1]
            )
            grad_middle_out[s] = grad_middle
            rows_out[4 * s : 4 * s + 1, :] = column_sum(grad_middle * branch[rows, :])
            rows_out[4 * s + 1 : 4 * s + 2, :] = column_sum(grad)
            rows_out[4 * s + 2 : 4 * s + 3, :] = column_sum(grad * unit)
            rows_out[4 * s + 3 : 4 * s + 4, :] = column_sum(grad_out * feed_out)


def attention_backward_kernel(
    slot, where, tokens, grad_middle_in, joined, soft_in, mixed, mod, feed_rows, cond, att, proj, *refs
):
    rank, core = where[0], where[1]
    if slot == 0:
        grad_tokens_out, grad_joined, first_out, branch_out, rows = refs
    else:
        before_joined, before_first, before_branch, before_rows, _, _ = refs[:6]
        grad_tokens_out, send_out, keep_out, rows_out = refs[6:10]
        grad_joined, grad_att, grad_proj, rows = refs[10:]

    if slot == 0:
        rows[...] = jnp.zeros_like(rows)
        rows[12:14, :] = cond[...]
        rows[19:24, :] = feed_rows[8:13, :]
    else:
        rows[...] = before_rows[...]

    pieces = mod[0]
    grad_middle = grad_middle_in[0]
    grad_branch = (pieces[2:3] * grad_middle).astype(LOW)
    rows[18:19, :] += column_sum(grad_branch.astype(WIDE))
    if slot == 0:
        branch_out[...] = grad_branch
    else:
        grad_proj[...] = (
            dot_first(mixed[0], before_branch[...]) + dot_first(mixed[1], grad_branch)
        ).astype(LOW)
    grad_mixed = dot_last(grad_branch, proj[...]).astype(LOW)
    first_half = head_mask((SEQ, 128), 0)
    zero = jnp.zeros((SEQ, 128), LOW)
    scale = HEAD_DIM ** (-0.5)
    for pair in range(HEADS // 2):
        lanes = slice(pair * 128, (pair + 1) * 128)
        query = joined[0, :, pair * 128 : (pair + 1) * 128]
        key = joined[0, :, D + pair * 128 : D + (pair + 1) * 128]
        value = joined[0, :, 2 * D + pair * 128 : 2 * D + (pair + 1) * 128]
        grads = grad_mixed[:, lanes]
        results = []
        for half in range(2):
            soft = soft_in[0, 2 * pair + half]
            masked = (
                jnp.where(first_half, grads, zero)
                if half == 0
                else jnp.where(first_half, zero, grads)
            )
            grad_soft = dot_last(masked, value)
            grad_values = dot_first(soft, grads)
            soft_wide = soft.astype(WIDE)
            weighted = soft_wide * grad_soft
            inner = jnp.sum(weighted, axis=-1, keepdims=True)
            grad_scores = (weighted - soft_wide * inner).astype(LOW)
            results.append(
                (dot_plain(grad_scores, key), dot_first(grad_scores, query), grad_values)
            )
        for third in range(3):
            merged = jnp.where(first_half, results[0][third], results[1][third])
            if third < 2:
                merged = merged * scale
            grad_joined[:, third * D + pair * 128 : third * D + (pair + 1) * 128] = merged.astype(LOW)
    grads = grad_joined[...]
    sums = column_sum(grads.astype(WIDE))
    rows[16:17, :] += sums[:, :D]
    rows[17:18, :] += sums[:, 2 * D :]
    normed, inverse = layer_norm_parts(tokens[0].astype(WIDE))
    first_in = (normed * (1.0 + pieces[1:2]) + pieces[0:1]).astype(LOW)
    if slot == 0:
        first_out[...] = first_in
    else:
        for third in range(3):
            lanes = slice(third * D, (third + 1) * D)
            grad_att[:, lanes] = (
                dot_first(before_first[...], before_joined[:, lanes])
                + dot_first(first_in, grad_joined[:, lanes])
            ).astype(LOW)
    grad_first = dot_last(grads, att[...])
    grad_tokens_out[0] = (
        grad_middle + norm_backward(grad_first * (1.0 + pieces[1:2]), normed, inverse)
    ).astype(LOW)
    own_rows = jnp.concatenate(
        [
            column_sum(grad_first),
            column_sum(grad_first * normed),
        ],
        axis=0,
    )

    rows[6 * slot : 6 * slot + 2, :] = own_rows
    rows[6 * slot + 2 : 6 * slot + 6, :] = feed_rows[4 * slot : 4 * slot + 4, :]
    if slot == 0:
        return
    rows_out[...] = rows[...].astype(LOW)
    for k in range(4):
        start = pl.multiple_of((rank ^ k) * QUARTER, 32)
        block = grad_att[pl.ds(start, QUARTER), :]
        low_part = (block[:, :D], block[:, D : 2 * D])
        high_part = (block[:, 2 * D :], grad_proj[pl.ds(start, QUARTER), :])
        turned = (0, 2, 1, 3)[k]

        @pl.when(core == 0)
        def _():
            for j in range(2):
                keep_out[turned, j * QUARTER : (j + 1) * QUARTER, :] = low_part[j]
                send_out[k, j * QUARTER : (j + 1) * QUARTER, :] = high_part[j]

        @pl.when(core != 0)
        def _():
            for j in range(2):
                keep_out[k, j * QUARTER : (j + 1) * QUARTER, :] = high_part[j]
                send_out[turned, j * QUARTER : (j + 1) * QUARTER, :] = low_part[j]


def half_of(where, which):
    return (where[2] >> (where[1] ^ which)) & 1


def rows_at(index, count):
    return pl.ds(pl.multiple_of(index * count, 16), count)


def merge_small(out, own, arrived):
    count = own.shape[0] - BLOCK
    out[0:count, :] = own[0:count, :]
    out[count : 2 * count, :] = arrived[0:count, :]
    out[2 * count :, :] = (
        own[count:, :].astype(WIDE) + arrived[count:, :].astype(WIDE)
    ).astype(LOW)


def step1_kernel(
    where, att_keep, att_in, feed_keep, feed_in, small, small_in,
    att_stay, att_go, feed_stay, feed_go, small_out, total,
):
    half = half_of(where, 0)
    count = D // 2
    att_stay[...] = att_keep[0] + att_in[0].astype(WIDE)
    att_go[...] = (att_keep[1] + att_in[1].astype(WIDE)).astype(LOW)
    total[...] = feed_keep[...] + feed_in[...].astype(WIDE)
    feed_stay[...] = total[rows_at(half, count), :]
    feed_go[...] = total[rows_at(1 - half, count), :].astype(LOW)
    merge_small(small_out, small, small_in)


def step2_kernel(where, att_keep, att_in, feed_keep, feed_in, small, small_in, message, small_out):
    count = D // 2
    message[0:count, :] = (feed_keep[...] + feed_in[...].astype(WIDE)).astype(LOW)
    message[count:, :] = (att_keep[...] + att_in[...].astype(WIDE)).astype(LOW)
    merge_small(small_out, small, small_in)


def step3_kernel(where, own, arrived, small, small_in, message, small_out):
    message[...] = (own[...].astype(WIDE) + arrived[...].astype(WIDE)).astype(LOW)
    merge_small(small_out, small, small_in)


def step4_kernel(
    where, own, arrived, small, small_in, weight, att_part, feed_part, small_out, cond_keep, cond_go
):
    half = half_of(where, 0)
    count = D // 2
    feed_part[rows_at(half, count), :] = own[0:count, :]
    feed_part[rows_at(1 - half, count), :] = arrived[0:count, :]
    att_part[...] = (own[count:, :].astype(WIDE) + arrived[count:, :].astype(WIDE)).astype(LOW)
    merge_small(small_out, small, small_in)
    rows = [
        block[start : start + BLOCK, :].astype(WIDE)
        for block in (small, small_in)
        for start in (0, 4 * BLOCK)
    ]
    total = None
    for j in range(6):
        lines = [row[6 * slot + j : 6 * slot + j + 1] for row in rows for slot in range(2)]
        term = dot_last(
            jnp.concatenate(lines, axis=0).astype(LOW), weight[:, j * D : (j + 1) * D]
        )
        total = term if total is None else total + term
    padded = jnp.concatenate([total, jnp.zeros((8, 128 - QUARTER), WIDE)], axis=1)
    blank = jnp.zeros((4, 128), WIDE)
    cond_keep[...] = jnp.concatenate([padded[0:4], blank], axis=0)
    cond_go[...] = jnp.concatenate([padded[4:8], blank], axis=0)


def step5_kernel(where, cond_keep, cond_in, _, cond_go):
    blank = jnp.zeros((4, 128), WIDE)
    cond_go[...] = jnp.concatenate([cond_keep[2:4], cond_in[2:4], blank], axis=0)


def modulation_update_kernel(
    where, near, far, weight, mean, square, bias, bias_mean, bias_square,
    weight_out, mean_out, square_out, bias_out, bias_mean_out, bias_square_out, mark, everyone,
):
    rank, core, plane = where[0], where[1], where[2]
    for side, source in enumerate((near, far)):
        here = core ^ side
        first, second = 1 + here, 2 - here
        for index in range(16):
            a, b, c, d = (index & 1, (index >> 1) & 1, (index >> 2) & 1, index >> 3)
            z_at = plane ^ (a * first) ^ (b * second)
            g_at = rank ^ (c * second) ^ (d * first)
            place = (g_at * 4 + z_at) * 2 + here
            block = source[index * BLOCK : (index + 1) * BLOCK, :].astype(WIDE)
            for third in range(3):
                everyone[third, rows_at(place, BLOCK), :] = block[
                    :, third * 128 : (third + 1) * 128
                ]

    def line(at):
        parts = [everyone[third, pl.ds(at, 32, stride=BLOCK), :] for third in range(3)]
        return jnp.concatenate(parts, axis=1)

    def both(at, other):
        return jnp.concatenate([line(at), line(other)], axis=0)

    def own_lanes(values):
        chosen = values[:, :QUARTER]
        for place in range(1, 4):
            lanes = slice(place * QUARTER, (place + 1) * QUARTER)
            chosen = jnp.where(rank == place, values[:, lanes], chosen)
        return chosen

    cond = own_lanes(both(12, 13)).astype(LOW)
    sums = []
    for j in range(6):
        lanes = slice(j * D, (j + 1) * D)
        grads = both(j, 6 + j)
        sums.append(column_sum(grads))
        gradient = dot_first(cond, grads.astype(LOW))
        updated, momentum, variance = adam_update(
            weight[:, lanes].astype(WIDE),
            gradient,
            mean[:, lanes].astype(WIDE),
            square[:, lanes].astype(WIDE),
            LEARN_RATES[0],
            DECAY_FLAGS[0],
        )
        weight_out[:, lanes] = updated
        mean_out[:, lanes] = momentum
        square_out[:, lanes] = variance
    sums.append(near[16 * BLOCK :, :].astype(WIDE)[0:8] + far[16 * BLOCK :, :].astype(WIDE)[0:8])
    gradient = own_lanes(jnp.concatenate(sums, axis=0))
    updated, momentum, variance = adam_update(
        bias[...].astype(WIDE),
        gradient,
        bias_mean[...].astype(WIDE),
        bias_square[...].astype(WIDE),
        LEARN_RATES[5],
        DECAY_FLAGS[5],
    )
    bias_out[...] = updated
    bias_mean_out[...] = momentum
    bias_square_out[...] = variance
    mark[...] = jnp.zeros_like(mark)


def split_kernel(keep, arrived, stay, go):
    half = stay.shape[0]
    stay[...] = keep[:half].astype(WIDE) + arrived[:half].astype(WIDE)
    go[...] = (keep[half:].astype(WIDE) + arrived[half:].astype(WIDE)).astype(LOW)


def whole(shape):
    return pl.BlockSpec(shape, lambda *grid: (0,) * len(shape))


def by_slot(shape):
    return pl.BlockSpec((1,) + shape, lambda s: (s,) + (0,) * len(shape))


def shape_of(shape, dtype):
    return jax.ShapeDtypeStruct(shape, dtype)


SMEM_SPEC = pl.BlockSpec(memory_space=pltpu.SMEM)
PARAMS = pltpu.CompilerParams(vmem_limit_bytes=VMEM_BYTES)


ANY_SPEC = pl.BlockSpec(memory_space=pl.ANY)


def small_call(kernel, name, outs, where, *operands, scratch=(), after=(), params=PARAMS):
    return pl.pallas_call(
        kernel,
        grid=(1,),
        in_specs=[SMEM_SPEC]
        + [whole(item.shape) for item in operands]
        + [ANY_SPEC] * len(after),
        out_specs=[whole(shape) for shape, _ in outs],
        out_shape=[shape_of(*item) for item in outs],
        scratch_shapes=[pltpu.VMEM(*item) for item in scratch],
        compiler_params=params,
        name=name,
    )(where, *operands, *after)


def run_payload(*operands):
    return pl.pallas_call(
        payload_kernel,
        grid=(1,),
        in_specs=[whole(item.shape) for item in operands[:4]] + [ANY_SPEC] * 2,
        out_specs=[whole((2 * QUARTER + 16, D)), ANY_SPEC],
        out_shape=[shape_of((2 * QUARTER + 16, D), LOW), shape_of((D, D), LOW)],
        scratch_shapes=[pltpu.SemaphoreType.DMA],
        compiler_params=pltpu.CompilerParams(vmem_limit_bytes=60 * 1024 * 1024),
        name="own_payload",
    )(*operands)


def run_gate(value, *after, space=ANY_SPEC):
    return pl.pallas_call(
        gate_kernel,
        in_specs=[space] + [ANY_SPEC] * len(after),
        out_specs=space,
        out_shape=shape_of(value.shape, value.dtype),
        input_output_aliases={0: 0},
        compiler_params=pltpu.CompilerParams(vmem_limit_bytes=1024 * 1024),
        name="in_order",
    )(value, *after)


def run_relay(where, keep, arrived, passing):
    two = (2, keep.shape[1])
    return pl.pallas_call(
        relay_kernel,
        grid=(1,),
        in_specs=[SMEM_SPEC, whole(keep.shape), whole(arrived.shape), ANY_SPEC],
        out_specs=[whole(two), whole(two), ANY_SPEC],
        out_shape=[shape_of(two, WIDE)] * 2 + [shape_of(passing.shape, passing.dtype)],
        input_output_aliases={3: 2},
        compiler_params=PARAMS,
        name="relay",
    )(where, keep, arrived, passing)


def run_modulation(where, condition, biases, blocks, weight):
    message = pl.BlockSpec((16, D), lambda s: (2 * QUARTER // 16, 0))
    return pl.pallas_call(
        modulation_kernel,
        grid=(1,),
        in_specs=[SMEM_SPEC, whole((2, D)), whole((BIAS_ROWS, QUARTER))]
        + [message] * 3
        + [whole((QUARTER, 6 * D))],
        out_specs=[whole((4, 6 * D))] * 2 + [whole((16, D))],
        out_shape=[shape_of((4, 6 * D), WIDE)] * 2 + [shape_of((16, D), WIDE)],
        compiler_params=PARAMS,
        cost_estimate=pl.CostEstimate(flops=10**7, bytes_accessed=10**6, transcendentals=0),
        name="modulation_partials",
    )(where, condition, biases, *blocks, weight)


def run_attention_forward(where, tokens, stay, arrived, bias, own_att, own_proj, nears, fars):
    part = whole((2 * QUARTER + 16, D))
    return pl.pallas_call(
        attention_forward_kernel,
        grid=(2,),
        in_specs=[
            SMEM_SPEC,
            by_slot((SEQ, D)),
            whole((2, 6 * D)),
            whole((2, 6 * D)),
            whole((16, D)),
            whole((QUARTER, 3 * D)),
            whole((QUARTER, D)),
        ]
        + [part] * 6,
        out_specs=[
            by_slot((SEQ, 3 * D)),
            by_slot((HEADS, SEQ, SEQ)),
            by_slot((SEQ, D)),
            by_slot((6, D)),
            whole((D, 3 * D)),
            whole((D, D)),
        ],
        out_shape=[
            shape_of((2, SEQ, 3 * D), LOW),
            shape_of((2, HEADS, SEQ, SEQ), LOW),
            shape_of((2, SEQ, D), LOW),
            shape_of((2, 6, D), WIDE),
            shape_of((D, 3 * D), LOW),
            shape_of((D, D), LOW),
        ],
        compiler_params=PARAMS,
        cost_estimate=pl.CostEstimate(
            flops=3 * 10**9, bytes_accessed=6 * 10**6, transcendentals=10**6
        ),
        name="attention_forward",
    )(where, tokens, stay, arrived, bias, own_att, own_proj, *nears, *fars)


def run_feed(where, mixed, tokens, cotangent, mod, bias, proj, own_expand, own_contract, nears, fars):
    rows = 2 * SEQ

    return pl.pallas_call(
        feed_kernel,
        grid=(2,),
        in_specs=[SMEM_SPEC]
        + [whole((2, SEQ, D))] * 3
        + [whole((2, 6, D)), whole((16, D))]
        + [whole((D, D))] * 9,
        out_specs=[
            whole((2, SEQ, D)),
            whole((2, SEQ, D)),
            pl.BlockSpec((2, D, D), lambda i: (i, 0, 0)),
            pl.BlockSpec((2, D, D), lambda i: (i, 0, 0)),
            whole((16, D)),
        ],
        scratch_shapes=[
            pltpu.VMEM((2, D, 2 * D), LOW),
            pltpu.VMEM((2, 2 * D, D), LOW),
            pltpu.VMEM((rows, D), WIDE),
            pltpu.VMEM((rows, D), WIDE),
            pltpu.VMEM((rows, D), LOW),
            pltpu.VMEM((rows, D), WIDE),
            pltpu.VMEM((rows, 128), WIDE),
            pltpu.VMEM((rows, D), LOW),
            pltpu.VMEM((rows, D), WIDE),
            pltpu.VMEM((rows, D), WIDE),
        ],
        out_shape=[
            shape_of((2, SEQ, D), LOW),
            shape_of((2, SEQ, D), WIDE),
            shape_of((4, D, D), LOW),
            shape_of((4, D, D), LOW),
            shape_of((16, D), WIDE),
        ],
        compiler_params=PARAMS,
        cost_estimate=pl.CostEstimate(
            flops=8 * 10**9, bytes_accessed=10**7, transcendentals=10**6
        ),
        name="feed_forward_and_back",
    )(where, mixed, tokens, cotangent, mod, bias, proj, own_expand, own_contract, *nears, *fars)


def run_attention_backward(
    slot, where, tokens, grad_middle, joined, soft, mixed, mod, feed_rows, cond, att, proj, earlier=()
):
    def at_slot(shape):
        return pl.BlockSpec((1,) + shape, lambda i: (slot,) + (0,) * len(shape))

    passed = [((SEQ, 3 * D), LOW), ((SEQ, D), LOW), ((SEQ, D), LOW), ((SMALL, D), WIDE)]
    in_specs = [
        SMEM_SPEC,
        at_slot((SEQ, D)),
        at_slot((SEQ, D)),
        at_slot((SEQ, 3 * D)),
        at_slot((HEADS, SEQ, SEQ)),
        whole((2, SEQ, D)),
        at_slot((6, D)),
        whole((16, D)),
        whole((2, D)),
        whole((D, 3 * D)),
        whole((D, D)),
    ]
    out_specs = [at_slot((SEQ, D))]
    out_shape = [shape_of((2, SEQ, D), LOW)]
    scratch = []
    aliases = {}
    if slot == 0:
        out_specs += [whole(shape) for shape, _ in passed]
        out_shape += [shape_of(*item) for item in passed]
    else:
        in_specs += [whole(shape) for shape, _ in passed] + [ANY_SPEC, ANY_SPEC]
        aliases = {15: 0}
        out_specs += [whole((4, 2 * QUARTER, D))] * 2 + [whole((SMALL, D))]
        out_shape += [shape_of((4, 2 * QUARTER, D), LOW)] * 2 + [shape_of((SMALL, D), LOW)]
        sums = [((D, 3 * D), LOW), ((D, D), LOW)]
        scratch = [pltpu.VMEM(*item) for item in (passed[0], *sums, passed[3])]
    return pl.pallas_call(
        functools.partial(attention_backward_kernel, slot),
        grid=(1,),
        in_specs=in_specs,
        out_specs=out_specs,
        out_shape=out_shape,
        scratch_shapes=scratch,
        input_output_aliases=aliases,
        compiler_params=PARAMS,
        cost_estimate=pl.CostEstimate(
            flops=4 * 10**9, bytes_accessed=8 * 10**6, transcendentals=0
        ),
        name="attention_backward",
    )(where, tokens, grad_middle, joined, soft, mixed, mod, feed_rows, cond, att, proj, *earlier)


def turn_go_kernel(where, keep, last_keep, arrived, last_arrived, go):
    go[0] = (keep[0].astype(WIDE) + arrived[0].astype(WIDE)).astype(LOW)
    go[1] = (last_keep[0].astype(WIDE) + last_arrived[0].astype(WIDE)).astype(LOW)


def turn_stay_kernel(where, keep, next_keep, swapped, next_swapped, arrived, stay, go):
    stay[...] = keep[0].astype(WIDE) + swapped[0].astype(WIDE) + arrived[0].astype(WIDE)
    go[...] = (
        next_keep[0].astype(WIDE) + next_swapped[0].astype(WIDE) + arrived[1].astype(WIDE)
    ).astype(LOW)


def run_turned(kernel, name, places, outs, where, keep, swapped, *operands):
    def at(number):
        return pl.BlockSpec((1, D, D), lambda i, where: (places(where[1])[number], 0, 0))

    return pl.pallas_call(
        kernel,
        grid_spec=pltpu.PrefetchScalarGridSpec(
            num_scalar_prefetch=1,
            grid=(1,),
            in_specs=[at(0), at(1), at(0), at(1)] + [whole(item.shape) for item in operands],
            out_specs=[whole(shape) for shape, _ in outs],
        ),
        out_shape=[shape_of(*item) for item in outs],
        compiler_params=PARAMS,
        name=name,
    )(where, keep, keep, swapped, swapped, *operands)


def run_split(keep, arrived):
    count, rest = keep.shape[0], keep.shape[1:]
    half = (count // 2,) + rest
    return pl.pallas_call(
        split_kernel,
        grid=(1,),
        in_specs=[whole(keep.shape)] * 2,
        out_specs=[whole(half)] * 2,
        out_shape=[shape_of(half, WIDE), shape_of(half, LOW)],
        compiler_params=PARAMS,
        name="sum_and_split",
    )(keep, arrived)


def swap_plane(value, which):
    pairs = [(r, r ^ ((1 + ((r + which) & 1)) << 1)) for r in range(lax.axis_size("replica"))]
    return lax.ppermute(value, "replica", pairs)


def swap_pair(value, which):
    groups, copies = lax.axis_size("group"), lax.axis_size("replica")
    pairs = []
    for g in range(groups):
        for r in range(copies):
            other = g ^ (1 if (r + which) % 2 == 0 else 2)
            pairs.append((g * copies + r, other * copies + r))
    return lax.ppermute(value, ("group", "replica"), pairs)


def gather_pair(value):
    first = swap_pair(value, 0)
    second = swap_pair(value, 1)
    return (first, second, swap_pair(first, 1))


def update_all(stored, gradients, means, squares, kinds):
    return [
        adam_update(
            stored[kind].astype(jnp.float32),
            gradient,
            means[kind].astype(jnp.float32),
            squares[kind].astype(jnp.float32),
            LEARN_RATES[kind],
            DECAY_FLAGS[kind],
        )
        for kind, gradient in zip(kinds, gradients)
    ]


def by_core(core, own, other):
    return (
        jnp.where(core == 0, own, other).astype(jnp.float32),
        jnp.where(core == 0, other, own).astype(jnp.float32),
    )


def attention_shards(totals):
    joined = jnp.concatenate(
        [totals[0][:QUARTER], totals[0][QUARTER:], totals[1][:QUARTER]], axis=1
    )
    return (joined, totals[1][QUARTER:])


def tail_in_step(
    where, copy, stages, condition, ffn_halves, att_parts, small_rows, stored, means, squares
):
    core = where[1]
    (feed_stay, feed_go), (att_send, att_keep) = ffn_halves, att_parts
    half, third = (D // 2, D), (2 * QUARTER, D)
    att_stay, att_go = run_split(att_keep, swap_replica(att_send, 1))
    att_stay, att_go, feed_stay, feed_go, small = small_call(
        step1_kernel, "step_1",
        [(third, WIDE), (third, LOW), (half, WIDE), (half, LOW), ((3 * BLOCK, D), LOW)],
        where, att_stay, swap_pair(att_go, 0), feed_stay, swap_pair(feed_go, 1),
        small_rows, swap_plane(small_rows, 0),
        scratch=[((D, D), WIDE)],
    )
    message, small = small_call(
        step2_kernel, "step_2",
        [((D, D), LOW), ((5 * BLOCK, D), LOW)],
        where, att_stay, swap_pair(att_go, 1), feed_stay, swap_plane(feed_go, 0),
        small, swap_plane(small, 1),
    )
    message, small = small_call(
        step3_kernel, "step_3",
        [((D, D), LOW), ((9 * BLOCK, D), LOW)],
        where, message, swap_plane(message, 1), small, swap_pair(small, 1),
    )
    att_part, feed_part, small, cond_keep, cond_go = small_call(
        step4_kernel, "step_4",
        [(third, LOW), ((D, D), LOW), ((17 * BLOCK, D), LOW), ((8, 128), WIDE), ((8, 128), WIDE)],
        where, message, swap_plane(message, 0), small, swap_pair(small, 0), stored[0],
    )
    shard = [((QUARTER, 6 * D), WIDE)] * 3 + [((BIAS_ROWS, QUARTER), WIDE)] * 3
    *updates, mark = small_call(
        modulation_update_kernel, "modulation_update", shard + [((8, 128), WIDE)],
        where, small, swap_replica(small, 1), stored[0], means[0], squares[0],
        stored[5], means[5], squares[5],
        scratch=[((3, 32 * BLOCK, 128), WIDE)],
    )
    feed_totals = by_core(core, feed_part, swap_replica(feed_part, 1))
    feed_updates = update_all(stored, feed_totals, means, squares, (3, 4))
    cond_in = swap_pair(cond_go, 0)
    cond_go = small_call(
        step5_kernel, "step_5", [((8, 128), WIDE)], where, cond_keep, cond_in, after=(mark,)
    )[0]
    cond_last = run_gate(swap_pair(cond_go, 1), feed_updates[0][1])
    att_totals = by_core(core, att_part, swap_replica(att_part, 1))
    blocks = [
        block[:, :QUARTER] for block in (cond_keep[:2], cond_in[:2], cond_last[:2], cond_last[2:4])
    ]
    owners = (where[0],) + neighbours(where)
    lanes = []
    for place in range(4):
        chosen = blocks[0]
        for k in range(1, 4):
            chosen = jnp.where(owners[k] == place, blocks[k], chosen)
        lanes.append(chosen)
    sigmoid_cond = jax.nn.sigmoid(condition)
    grad_condition = (
        jnp.concatenate(lanes, axis=1) * sigmoid_cond * (1.0 + condition * (1.0 - sigmoid_cond))
    )
    att_updates = update_all(stored, attention_shards(att_totals), means, squares, (1, 2))
    return grad_condition, [updates[:3]] + att_updates + feed_updates + [updates[3:]]


def tail_in_turn(
    where, copy, stages, condition, ffn_halves, att_parts, small_rows, stored, means, squares
):
    rank, core = where[0], where[1]
    slot_count, model_width = condition.shape
    modulation, cond_low = stored[0], jax.nn.silu(condition).astype(jnp.bfloat16)
    (ffn_stay, ffn_go), (att_send, att_keep) = ffn_halves, att_parts
    ffn_totals = reduce_replicas(
        wide_sum([ffn_stay, swap_pair(ffn_go, 1)]).astype(LOW), copy, stages
    )
    att_stay, att_go = run_split(att_keep, swap_replica(att_send, 1))
    att_stay, att_go = run_split(att_stay, swap_pair(att_go, 0))
    att_totals = reduce_replicas(
        wide_sum([att_stay[0], swap_pair(att_go[0], 1)]).astype(LOW), copy, stages
    )
    row_total = small_rows.shape[0]
    gathered = small_rows[None]
    for low_bit, radix in stages[1:]:
        digit = (copy >> low_bit) % radix
        gathered = in_order(
            [swap_replica(gathered, k << low_bit) for k in range(radix)], digit
        ).reshape(-1, row_total, model_width)
    gathered = in_order([swap_group(gathered, k) for k in range(4)], rank)
    own_plane = lax.dynamic_index_in_dim(gathered, copy >> 1, axis=1, keepdims=False)
    group_mod = own_plane[:, : 6 * slot_count].reshape(4 * slot_count, 6 * model_width)
    grad_cond_columns = dot_last(group_mod, modulation).reshape(4, slot_count, model_width // 4)
    cond_back = in_order(
        [swap_group(pick(grad_cond_columns, rank ^ k), k) for k in range(4)], rank
    )
    sigmoid_cond = jax.nn.sigmoid(condition)
    grad_condition = (
        jnp.swapaxes(cond_back, 0, 1).reshape(slot_count, model_width)
        * sigmoid_cond
        * (1.0 + condition * (1.0 - sigmoid_cond))
    )
    everyone = in_order([swap_replica(gathered, k) for k in range(2)], core).reshape(
        -1, row_total, model_width
    )
    all_mod = everyone[:, : 6 * slot_count].reshape(-1, 6 * model_width)
    all_cond = everyone[:, 6 * slot_count : 7 * slot_count].reshape(-1, model_width)
    cond_own = lax.dynamic_slice_in_dim(all_cond, rank * (model_width // 4), model_width // 4, 1)
    grad_mod = dot_first(cond_own, all_mod)
    mod_bias_grad = jnp.sum(all_mod, axis=0, dtype=jnp.float32).reshape(6, model_width)
    rest_bias_grad = jnp.sum(everyone[:, BLOCK : BLOCK + 8], axis=0, dtype=jnp.float32)
    bias_grad = lax.dynamic_slice_in_dim(
        jnp.concatenate([mod_bias_grad, rest_bias_grad], axis=0),
        rank * (model_width // 4),
        model_width // 4,
        1,
    )
    grad_att_own = jnp.concatenate(
        [att_totals[0][:QUARTER], att_totals[0][QUARTER:], att_totals[1][:QUARTER]], axis=1
    )
    totals = (
        grad_mod,
        grad_att_own,
        att_totals[1][QUARTER:],
        ffn_totals[0],
        ffn_totals[1],
        bias_grad,
    )
    return grad_condition, update_all(stored, totals, means, squares, range(6))


def shards(
    latents,
    condition,
    cotangent,
    live_counts,
    modulation,
    attending,
    projection,
    expand,
    contract,
    biases,
    modulation_mean,
    attending_mean,
    projection_mean,
    expand_mean,
    contract_mean,
    biases_mean,
    modulation_square,
    attending_square,
    projection_square,
    expand_square,
    contract_square,
    biases_square,
):
    slot_count, length, model_width = latents.shape
    rank = lax.axis_index("group")
    copy = lax.axis_index("replica")
    core = copy % 2
    stages = replica_stages(lax.axis_size("replica"))
    where = jnp.stack([rank, core, copy >> 1, live_counts[0]]).astype(jnp.int32)

    cond_low = jax.nn.silu(condition).astype(LOW)
    payload, feed_part = run_payload(
        condition, attending, projection, biases, expand, contract
    )
    first, second = swap_pair(payload, 0), swap_pair(payload, 1)
    last, first_far = swap_pair(first, 1), swap_replica(first, 1)
    feed_part = run_gate(
        feed_part, first_far, second, space=pl.BlockSpec(memory_space=pltpu.HBM)
    )
    nears = (first, second, last)
    fars = [first_far, swap_replica(second, 1), swap_replica(last, 1)]
    feed_first, feed_second = swap_pair(feed_part, 0), swap_pair(feed_part, 1)
    stay, go, bias = run_modulation(where, condition, biases, nears, modulation)
    stay, go, feed_first = run_relay(where, stay, swap_pair(go, 0), feed_first)
    arrived = swap_pair(go, 1)
    feed_last = swap_pair(feed_first, 1)
    joined, soft, mixed, mod, att, proj = run_attention_forward(
        where, latents, stay, arrived, bias, attending, projection, nears, fars
    )
    feed_nears = (feed_first, feed_second, run_gate(feed_last, mod))
    feed_fars = [swap_replica(item, 1) for item in feed_nears]
    out_latents, grad_middle, ffn_send, ffn_keep, feed_rows = run_feed(
        where, mixed, latents, cotangent, mod, bias, proj, expand, contract, feed_nears, feed_fars
    )
    cond_wide = cond_low.astype(WIDE)
    block = (model_width, model_width)
    ffn_other = swap_replica(ffn_send, 1)
    ffn_go = run_turned(
        turn_go_kernel, "sum_to_send", lambda core: (1 + core, 3), [((2,) + block, LOW)],
        where, ffn_keep, ffn_other,
    )[0]
    earlier = run_attention_backward(
        0, where, latents, grad_middle, joined, soft, mixed, mod, feed_rows, cond_wide, att, proj
    )
    ffn_in = swap_pair(ffn_go, 0)
    grad_latents, att_send, att_keep, small_rows = run_attention_backward(
        1, where, latents, grad_middle, joined, soft, mixed, mod, feed_rows, cond_wide, att, proj,
        (*earlier[1:], earlier[0], ffn_go),
    )
    ffn_halves = run_turned(
        turn_stay_kernel, "sum_and_split", lambda core: (0, 2 - core),
        [(block, WIDE), (block, LOW)], where, ffn_keep, ffn_other, ffn_in,
    )
    tail = tail_in_step if lax.axis_size("replica") == 8 else tail_in_turn
    grad_condition, results = tail(
        where, copy, stages, condition, ffn_halves, (att_send, att_keep), small_rows,
        (modulation, attending, projection, expand, contract, biases),
        (
            modulation_mean, attending_mean, projection_mean,
            expand_mean, contract_mean, biases_mean,
        ),
        (
            modulation_square, attending_square, projection_square,
            expand_square, contract_square, biases_square,
        ),
    )
    return (
        out_latents,
        grad_latents,
        grad_condition,
        results[0][0],
        results[1][0],
        results[2][0],
        results[3][0],
        results[4][0],
        results[5][0],
        results[0][1],
        results[1][1],
        results[2][1],
        results[3][1],
        results[4][1],
        results[5][1],
        results[0][2],
        results[1][2],
        results[2][2],
        results[3][2],
        results[4][2],
        results[5][2],
    )


def solution(mesh):
    return jax.shard_map(
        shards,
        mesh=mesh,
        in_specs=(
            P(("group", "replica"), None, None),
            P(("group", "replica"), None),
            P(("group", "replica"), None, None),
            P(("group", "replica")),
            P("group", None),
            P("group", None),
            P("group", None),
            P(None, "group"),
            P("group", None),
            P(None, "group"),
            P("group", None),
            P("group", None),
            P("group", None),
            P(None, "group"),
            P("group", None),
            P(None, "group"),
            P("group", None),
            P("group", None),
            P("group", None),
            P(None, "group"),
            P("group", None),
            P(None, "group"),
        ),
        out_specs=(
            P(("group", "replica"), None, None),
            P(("group", "replica"), None, None),
            P(("group", "replica"), None),
            P("group", None),
            P("group", None),
            P("group", None),
            P(None, "group"),
            P("group", None),
            P(None, "group"),
            P("group", None),
            P("group", None),
            P("group", None),
            P(None, "group"),
            P("group", None),
            P(None, "group"),
            P("group", None),
            P("group", None),
            P("group", None),
            P(None, "group"),
            P("group", None),
            P(None, "group"),
        ),
        check_vma=False,
    )
```

```python
import functools

import jax
import jax.numpy as jnp
from jax import lax
from jax.experimental import pallas as pl
from jax.experimental.pallas import tpu as pltpu
from jax.sharding import PartitionSpec as P

HEADS = 6
HEAD_DIM = 64
FF = 1536
STEP = 10


NORM_EPS = 1e-06
ADAM_EPS = 1e-08
BETA_FIRST = 0.9
BETA_SECOND = 0.999
DECAY_RATE = 0.1
LEARN_RATES = (0.05, 0.05, 0.2, 0.05, 0.025, 0.1)
DECAY_FLAGS = (1.0, 1.0, 1.0, 1.0, 1.0, 0.0)
GELU_COEF = 0.7978845608028654
BIAS_ROWS = 14
D = 384
SEQ = 256
QUARTER = D // 4
VMEM_BYTES = 34 * 1024 * 1024
LOW = jnp.bfloat16
SMALL = 32
BLOCK = 16
WIDE = jnp.float32


def dot_plain(left_side, right_side):
    return jnp.dot(left_side, right_side, preferred_element_type=WIDE)


def dot_first(left_side, right_side):
    return lax.dot_general(
        left_side, right_side, (((0,), (0,)), ((), ())), preferred_element_type=WIDE
    )


def dot_last(left_side, right_side):
    return lax.dot_general(
        left_side, right_side, (((1,), (1,)), ((), ())), preferred_element_type=WIDE
    )


def adam_update(weight, gradient, mean_old, square_old, step_rate, decay_flag):
    momentum = BETA_FIRST * mean_old + (1.0 - BETA_FIRST) * gradient
    variance = BETA_SECOND * square_old + ((1.0 - BETA_SECOND) * gradient) * gradient
    root = variance * lax.rsqrt(variance)
    bottom = root * (1.0 - BETA_SECOND**STEP) ** (-0.5) + ADAM_EPS
    change = momentum * (step_rate / (1.0 - BETA_FIRST**STEP)) / bottom
    updated = weight * (1.0 - step_rate * decay_flag * DECAY_RATE) - change
    return (updated, momentum, variance)


def replica_stages(count):
    stages, low_bit = [(0, 2)], 1
    while (1 << low_bit) < count:
        radix = min(4, count >> low_bit)
        stages.append((low_bit, radix))
        low_bit += radix.bit_length() - 1
    return stages


def swap_group(value, k):
    if k == 0:
        return value
    return lax.ppermute(value, "group", [(i, i ^ k) for i in range(lax.axis_size("group"))])


def swap_replica(value, k):
    if k == 0:
        return value
    return lax.ppermute(value, "replica", [(i, i ^ k) for i in range(lax.axis_size("replica"))])


def pick(blocks, index):
    return lax.dynamic_index_in_dim(blocks, index, axis=0, keepdims=False)


def in_order(blocks, digit):
    ordered = []
    for place in range(len(blocks)):
        chosen = blocks[0]
        for k in range(1, len(blocks)):
            chosen = jnp.where((digit ^ k) == place, blocks[k], chosen)
        ordered.append(chosen)
    return jnp.stack(ordered)


def wide_sum(blocks):
    total = blocks[0].astype(jnp.float32)
    for block in blocks[1:]:
        total = total + block.astype(jnp.float32)
    return total


def scatter_stage(value, digit, low_bit, radix):
    rows = value.shape[-2] // radix
    parts = [
        lax.dynamic_slice_in_dim(value, (digit ^ k) * rows, rows, value.ndim - 2)
        for k in range(radix)
    ]
    received = [swap_replica(parts[k], k << low_bit) for k in range(radix)]
    return wide_sum(received).astype(jnp.bfloat16)


def reduce_replicas(value, copy, stages):
    core = copy % 2
    for low_bit, radix in stages[1:]:
        value = scatter_stage(value, (copy >> low_bit) % radix, low_bit, radix)
    for low_bit, radix in reversed(stages[1:]):
        blocks = [swap_replica(value, k << low_bit) for k in range(radix)]
        value = in_order(blocks, (copy >> low_bit) % radix)
        value = value.reshape(-1, value.shape[-1])
    other = swap_replica(value, 1)
    return (
        jnp.where(core == 0, value, other).astype(jnp.float32),
        jnp.where(core == 0, other, value).astype(jnp.float32),
    )


def layer_norm_parts(values):
    centred = values - jnp.mean(values, axis=-1, keepdims=True)
    inverse = lax.rsqrt(jnp.mean(centred * centred, axis=-1, keepdims=True) + NORM_EPS)
    return (centred * inverse, inverse)


def norm_backward(grad_normed, normed, inverse):
    mean_grad = jnp.mean(grad_normed, axis=-1, keepdims=True)
    mean_cross = jnp.mean(grad_normed * normed, axis=-1, keepdims=True)
    return inverse * (grad_normed - mean_grad - normed * mean_cross)


def column_sum(values):
    return jnp.sum(values, axis=0, keepdims=True)


def head_mask(shape, which):
    lane = lax.broadcasted_iota(jnp.int32, shape, 1)
    return (lane < HEAD_DIM) if which == 0 else (lane >= HEAD_DIM)


def place_rows(target, lanes, block, owner):
    start = pl.multiple_of(owner * QUARTER, 32)
    target[pl.ds(start, QUARTER), lanes] = block


def neighbours(where):
    rank, core = where[0], where[1]
    return (rank ^ (1 + core), rank ^ (2 - core), rank ^ 3)


def own_message(condition, biases):
    cond = condition[...]
    active = cond / (1.0 + jnp.exp(-cond))
    padded = jnp.concatenate(
        [biases[...].astype(WIDE), jnp.zeros((BIAS_ROWS, D - QUARTER), WIDE)], axis=1
    )
    return jnp.concatenate([active, padded], axis=0)


def payload_kernel(condition, attending, projection, biases, expand, contract, out, part, sem):
    core = lax.axis_index("replica") % 2

    @pl.when(core == 0)
    def _():
        pltpu.make_async_copy(expand, part, sem).start()
        out[0:QUARTER, :] = attending[:, 0:D]
        out[QUARTER : 2 * QUARTER, :] = attending[:, D : 2 * D]

    @pl.when(core != 0)
    def _():
        pltpu.make_async_copy(contract, part, sem).start()
        out[0:QUARTER, :] = attending[:, 2 * D : 3 * D]
        out[QUARTER : 2 * QUARTER, :] = projection[...]

    out[2 * QUARTER :, :] = own_message(condition, biases).astype(LOW)
    pltpu.make_async_copy(expand, part, sem).wait()


def modulation_kernel(
    where, condition, biases, first, second, last, weight, stay, go, bias_out
):
    rank = where[0]
    owners = (rank,) + neighbours(where)
    rows = [own_message(condition, biases)]
    rows += [block[...].astype(WIDE) for block in (first, second, last)]
    conds = jnp.concatenate([rows[0][0:2], rows[2][0:2], rows[1][0:2], rows[3][0:2]], axis=0)
    columns = conds[:, :QUARTER]
    for place in range(1, 4):
        lanes = slice(place * QUARTER, (place + 1) * QUARTER)
        columns = jnp.where(rank == place, conds[:, lanes], columns)
    partial = dot_plain(columns.astype(LOW), weight[...])
    stay[...] = partial[:4]
    go[...] = partial[4:]
    lanes = []
    for place in range(4):
        chosen = rows[0][:, :QUARTER]
        for k in range(1, 4):
            chosen = jnp.where(owners[k] == place, rows[k][:, :QUARTER], chosen)
        lanes.append(chosen)
    bias_out[...] = jnp.concatenate(lanes, axis=1)


def relay_kernel(where, keep, arrived, _, stay, go, __):
    stay[...] = keep[0:2, :] + arrived[0:2, :]
    go[...] = keep[2:4, :] + arrived[2:4, :]


def gate_kernel(*refs):
    pass


def attention_forward_kernel(
    where, tokens, stay, arrived, bias, own_att, own_proj, n1, n2, n3, f1, f2, f3,
    joined_out, soft_out, mixed_out, mod_out, att, proj,
):
    slot = pl.program_id(0)
    rank = where[0]

    core = where[1]

    def assemble(lows, highs):
        for k, block in zip((1, 2, 3), lows):
            place_rows(att, slice(0, D), block[0:QUARTER, :], rank ^ k)
            place_rows(att, slice(D, 2 * D), block[QUARTER : 2 * QUARTER, :], rank ^ k)
        for k, block in zip((2, 1, 3), highs):
            place_rows(att, slice(2 * D, 3 * D), block[0:QUARTER, :], rank ^ k)
            place_rows(proj, slice(0, D), block[QUARTER : 2 * QUARTER, :], rank ^ k)

    @pl.when(slot == 0)
    def _():
        place_rows(att, slice(0, 3 * D), own_att[...], rank)
        place_rows(proj, slice(0, D), own_proj[...], rank)

        @pl.when(core == 0)
        def _():
            assemble((n1, n2, n3), (f1, f2, f3))

        @pl.when(core != 0)
        def _():
            assemble((f1, f2, f3), (n1, n2, n3))

    summed = stay[...] + arrived[...]
    row = jnp.where(slot == 0, summed[0:1], summed[1:2])
    pieces = [row[:, j * D : (j + 1) * D] + bias[2 + j : 3 + j, :] for j in range(6)]
    mod_out[0] = jnp.concatenate(pieces, axis=0)
    normed, _ = layer_norm_parts(tokens[0].astype(WIDE))
    first_in = (normed * (1.0 + pieces[1]) + pieces[0]).astype(LOW)
    thirds = []
    for third in range(3):
        part = dot_plain(first_in, att[:, third * D : (third + 1) * D])
        if third == 0:
            part = part + bias[8:9, :]
        if third == 2:
            part = part + bias[9:10, :]
        part = part.astype(LOW)
        joined_out[0, :, third * D : (third + 1) * D] = part
        thirds.append(part)
    first_half = head_mask((SEQ, 128), 0)
    scale = jnp.asarray(HEAD_DIM ** (-0.5), LOW)
    zero = jnp.zeros((SEQ, 128), LOW)
    for pair in range(HEADS // 2):
        lanes = slice(pair * 128, (pair + 1) * 128)
        query, key, value = (part[:, lanes] for part in thirds)
        query = query * scale
        outs = []
        for half in range(2):
            masked = (
                jnp.where(first_half, query, zero)
                if half == 0
                else jnp.where(first_half, zero, query)
            )
            scores = dot_last(masked, key)
            weights = jnp.exp(scores - jnp.max(scores, axis=-1, keepdims=True))
            total = jnp.sum(weights, axis=-1, keepdims=True)
            soft = (weights * (1.0 / total)).astype(LOW)
            soft_out[0, 2 * pair + half] = soft
            outs.append(dot_plain(soft, value))
        mixed_out[0, :, lanes] = jnp.where(first_half, outs[0], outs[1]).astype(LOW)


def feed_kernel(
    where, mixed, tokens, cotangent, mod, bias, proj, own_expand, own_contract, n1, n2, n3, f1, f2, f3,
    out, grad_middle_out, send_out, keep_out, rows_out,
    expands, contracts, branch, middle, second, normed, inverse, grad_feed, feed, grad_second,
):
    step = pl.program_id(0)
    rank, core, live = where[0], where[1], where[3]

    def assemble(lows, highs):
        for k, block in zip((1, 2, 3), lows):
            expands[k // 2, :, (k % 2) * D : (k % 2 + 1) * D] = block[...]
        for k, block in zip((2, 1, 3), highs):
            contracts[k // 2, (k % 2) * D : (k % 2 + 1) * D, :] = block[...]

    slots = [slice(s * SEQ, (s + 1) * SEQ) for s in range(2)]

    @pl.when(step == 0)
    def _():
        expands[0, :, 0:D] = own_expand[...]
        contracts[0, 0:D, :] = own_contract[...]

        @pl.when(core == 0)
        def _():
            assemble((n1, n2, n3), (f1, f2, f3))

        @pl.when(core != 0)
        def _():
            assemble((f1, f2, f3), (n1, n2, n3))

        for s, rows in enumerate(slots):
            pieces = mod[s]
            value = dot_plain(mixed[s], proj[...]) + bias[10:11, :]
            branch[rows, :] = value
            centre = tokens[s].astype(WIDE) + pieces[2:3] * value
            middle[rows, :] = centre
            unit, spread = layer_norm_parts(centre)
            normed[rows, :] = unit
            inverse[rows, :] = jnp.broadcast_to(spread, (SEQ, 128))
            second[rows, :] = (unit * (1.0 + pieces[4:5]) + pieces[3:4]).astype(LOW)
            alive = jnp.where(s < live, 1.0, 0.0)
            grad_feed[rows, :] = (
                pieces[5:6] * (cotangent[s].astype(WIDE) * alive)
            ).astype(LOW)
        rows_out[...] = jnp.zeros_like(rows_out)
        rows_out[12:13, :] = column_sum(grad_feed[...].astype(WIDE))

    owners = (rank ^ (2 * step), rank ^ (2 * step + 1))
    hidden_bias = jnp.concatenate([bias[pl.ds(11 + owner, 1), :] for owner in owners], axis=1)
    expand, contract = expands[step], contracts[step]
    before = dot_plain(second[...], expand) + hidden_bias
    square = before * before
    tangent = jnp.tanh(before * (GELU_COEF + (GELU_COEF * 0.044715) * square))
    half_up = 0.5 + 0.5 * tangent
    activated = (before * half_up).astype(LOW)
    slope = half_up + (0.5 * before) * (1.0 - tangent * tangent) * (
        GELU_COEF + (GELU_COEF * 3.0 * 0.044715) * square
    )
    grad_before_wide = dot_last(grad_feed[...], contract) * slope
    grad_before = grad_before_wide.astype(LOW)
    feed_term = dot_plain(activated, contract)
    second_term = dot_last(grad_before, expand)
    grad_expand = dot_first(second[...], grad_before).astype(LOW)
    grad_contract = dot_first(activated, grad_feed[...]).astype(LOW)
    sums = column_sum(grad_before.astype(WIDE))
    for k, owner in enumerate(owners):
        rows_out[pl.ds(8 + owner, 1), :] = sums[:, k * D : (k + 1) * D]

    @pl.when(core == 0)
    def _():
        for k in range(2):
            send_out[k] = grad_contract[k * D : (k + 1) * D, :]
            keep_out[k] = grad_expand[:, k * D : (k + 1) * D]

    @pl.when(core != 0)
    def _():
        for k in range(2):
            send_out[k] = grad_expand[:, k * D : (k + 1) * D]
            keep_out[k] = grad_contract[k * D : (k + 1) * D, :]

    @pl.when(step == 0)
    def _():
        feed[...] = feed_term
        grad_second[...] = second_term

    @pl.when(step > 0)
    def _():
        feed[...] += feed_term
        grad_second[...] += second_term

    @pl.when(step == 1)
    def _():
        for s, rows in enumerate(slots):
            pieces = mod[s]
            alive = jnp.where(s < live, 1.0, 0.0)
            feed_out = feed[rows, :] + bias[15:16, :]
            grad_out = cotangent[s].astype(WIDE) * alive
            out[s] = ((middle[rows, :] + pieces[5:6] * feed_out) * alive).astype(LOW)
            grad = grad_second[rows, :]
            unit = normed[rows, :]
            grad_middle = grad_out + norm_backward(
                grad * (1.0 + pieces[4:5]), unit, inverse[rows, 0:1]
            )
            grad_middle_out[s] = grad_middle
            rows_out[4 * s : 4 * s + 1, :] = column_sum(grad_middle * branch[rows, :])
            rows_out[4 * s + 1 : 4 * s + 2, :] = column_sum(grad)
            rows_out[4 * s + 2 : 4 * s + 3, :] = column_sum(grad * unit)
            rows_out[4 * s + 3 : 4 * s + 4, :] = column_sum(grad_out * feed_out)


def attention_backward_kernel(
    slot, where, tokens, grad_middle_in, joined, soft_in, mixed, mod, feed_rows, cond, att, proj, *refs
):
    rank, core = where[0], where[1]
    if slot == 0:
        grad_tokens_out, grad_joined, first_out, branch_out, rows = refs
    else:
        before_joined, before_first, before_branch, before_rows, _, _ = refs[:6]
        grad_tokens_out, send_out, keep_out, rows_out = refs[6:10]
        grad_joined, grad_att, grad_proj, rows = refs[10:]

    if slot == 0:
        rows[...] = jnp.zeros_like(rows)
        rows[12:14, :] = cond[...]
        rows[19:24, :] = feed_rows[8:13, :]
    else:
        rows[...] = before_rows[...]

    pieces = mod[0]
    grad_middle = grad_middle_in[0]
    grad_branch = (pieces[2:3] * grad_middle).astype(LOW)
    rows[18:19, :] += column_sum(grad_branch.astype(WIDE))
    if slot == 0:
        branch_out[...] = grad_branch
    else:
        grad_proj[...] = (
            dot_first(mixed[0], before_branch[...]) + dot_first(mixed[1], grad_branch)
        ).astype(LOW)
    grad_mixed = dot_last(grad_branch, proj[...]).astype(LOW)
    first_half = head_mask((SEQ, 128), 0)
    zero = jnp.zeros((SEQ, 128), LOW)
    scale = HEAD_DIM ** (-0.5)
    for pair in range(HEADS // 2):
        lanes = slice(pair * 128, (pair + 1) * 128)
        query = joined[0, :, pair * 128 : (pair + 1) * 128]
        key = joined[0, :, D + pair * 128 : D + (pair + 1) * 128]
        value = joined[0, :, 2 * D + pair * 128 : 2 * D + (pair + 1) * 128]
        grads = grad_mixed[:, lanes]
        results = []
        for half in range(2):
            soft = soft_in[0, 2 * pair + half]
            masked = (
                jnp.where(first_half, grads, zero)
                if half == 0
                else jnp.where(first_half, zero, grads)
            )
            grad_soft = dot_last(masked, value)
            grad_values = dot_first(soft, grads)
            soft_wide = soft.astype(WIDE)
            weighted = soft_wide * grad_soft
            inner = jnp.sum(weighted, axis=-1, keepdims=True)
            grad_scores = (weighted - soft_wide * inner).astype(LOW)
            results.append(
                (dot_plain(grad_scores, key), dot_first(grad_scores, query), grad_values)
            )
        for third in range(3):
            merged = jnp.where(first_half, results[0][third], results[1][third])
            if third < 2:
                merged = merged * scale
            grad_joined[:, third * D + pair * 128 : third * D + (pair + 1) * 128] = merged.astype(LOW)
    grads = grad_joined[...]
    sums = column_sum(grads.astype(WIDE))
    rows[16:17, :] += sums[:, :D]
    rows[17:18, :] += sums[:, 2 * D :]
    normed, inverse = layer_norm_parts(tokens[0].astype(WIDE))
    first_in = (normed * (1.0 + pieces[1:2]) + pieces[0:1]).astype(LOW)
    if slot == 0:
        first_out[...] = first_in
    else:
        for third in range(3):
            lanes = slice(third * D, (third + 1) * D)
            grad_att[:, lanes] = (
                dot_first(before_first[...], before_joined[:, lanes])
                + dot_first(first_in, grad_joined[:, lanes])
            ).astype(LOW)
    grad_first = dot_last(grads, att[...])
    grad_tokens_out[0] = (
        grad_middle + norm_backward(grad_first * (1.0 + pieces[1:2]), normed, inverse)
    ).astype(LOW)
    own_rows = jnp.concatenate(
        [
            column_sum(grad_first),
            column_sum(grad_first * normed),
        ],
        axis=0,
    )

    rows[6 * slot : 6 * slot + 2, :] = own_rows
    rows[6 * slot + 2 : 6 * slot + 6, :] = feed_rows[4 * slot : 4 * slot + 4, :]
    if slot == 0:
        return
    rows_out[...] = rows[...].astype(LOW)
    for k in range(4):
        start = pl.multiple_of((rank ^ k) * QUARTER, 32)
        block = grad_att[pl.ds(start, QUARTER), :]
        low_part = (block[:, :D], block[:, D : 2 * D])
        high_part = (block[:, 2 * D :], grad_proj[pl.ds(start, QUARTER), :])
        turned = (0, 2, 1, 3)[k]

        @pl.when(core == 0)
        def _():
            for j in range(2):
                keep_out[turned, j * QUARTER : (j + 1) * QUARTER, :] = low_part[j]
                send_out[k, j * QUARTER : (j + 1) * QUARTER, :] = high_part[j]

        @pl.when(core != 0)
        def _():
            for j in range(2):
                keep_out[k, j * QUARTER : (j + 1) * QUARTER, :] = high_part[j]
                send_out[turned, j * QUARTER : (j + 1) * QUARTER, :] = low_part[j]


def half_of(where, which):
    return (where[2] >> (where[1] ^ which)) & 1


def rows_at(index, count):
    return pl.ds(pl.multiple_of(index * count, 16), count)


def merge_small(out, own, arrived):
    count = own.shape[0] - BLOCK
    out[0:count, :] = own[0:count, :]
    out[count : 2 * count, :] = arrived[0:count, :]
    out[2 * count :, :] = (
        own[count:, :].astype(WIDE) + arrived[count:, :].astype(WIDE)
    ).astype(LOW)


def step1_kernel(
    where, att_keep, att_in, feed_keep, feed_in, small, small_in,
    att_stay, att_go, feed_stay, feed_go, small_out, total,
):
    half = half_of(where, 0)
    count = D // 2
    att_stay[...] = att_keep[0] + att_in[0].astype(WIDE)
    att_go[...] = (att_keep[1] + att_in[1].astype(WIDE)).astype(LOW)
    total[...] = feed_keep[...] + feed_in[...].astype(WIDE)
    feed_stay[...] = total[rows_at(half, count), :]
    feed_go[...] = total[rows_at(1 - half, count), :].astype(LOW)
    merge_small(small_out, small, small_in)


def step2_kernel(where, att_keep, att_in, feed_keep, feed_in, small, small_in, message, small_out):
    count = D // 2
    message[0:count, :] = (feed_keep[...] + feed_in[...].astype(WIDE)).astype(LOW)
    message[count:, :] = (att_keep[...] + att_in[...].astype(WIDE)).astype(LOW)
    merge_small(small_out, small, small_in)


def step3_kernel(where, own, arrived, small, small_in, message, small_out):
    message[...] = (own[...].astype(WIDE) + arrived[...].astype(WIDE)).astype(LOW)
    merge_small(small_out, small, small_in)


def step4_kernel(
    where, own, arrived, small, small_in, weight, att_part, feed_part, small_out, cond_keep, cond_go
):
    half = half_of(where, 0)
    count = D // 2
    feed_part[rows_at(half, count), :] = own[0:count, :]
    feed_part[rows_at(1 - half, count), :] = arrived[0:count, :]
    att_part[...] = (own[count:, :].astype(WIDE) + arrived[count:, :].astype(WIDE)).astype(LOW)
    merge_small(small_out, small, small_in)
    rows = [
        block[start : start + BLOCK, :].astype(WIDE)
        for block in (small, small_in)
        for start in (0, 4 * BLOCK)
    ]
    total = None
    for j in range(6):
        lines = [row[6 * slot + j : 6 * slot + j + 1] for row in rows for slot in range(2)]
        term = dot_last(
            jnp.concatenate(lines, axis=0).astype(LOW), weight[:, j * D : (j + 1) * D]
        )
        total = term if total is None else total + term
    padded = jnp.concatenate([total, jnp.zeros((8, 128 - QUARTER), WIDE)], axis=1)
    blank = jnp.zeros((4, 128), WIDE)
    cond_keep[...] = jnp.concatenate([padded[0:4], blank], axis=0)
    cond_go[...] = jnp.concatenate([padded[4:8], blank], axis=0)


def step5_kernel(where, cond_keep, cond_in, _, cond_go):
    blank = jnp.zeros((4, 128), WIDE)
    cond_go[...] = jnp.concatenate([cond_keep[2:4], cond_in[2:4], blank], axis=0)


def modulation_update_kernel(
    where, near, far, weight, mean, square, bias, bias_mean, bias_square,
    weight_out, mean_out, square_out, bias_out, bias_mean_out, bias_square_out, mark, everyone,
):
    rank, core, plane = where[0], where[1], where[2]
    for side, source in enumerate((near, far)):
        here = core ^ side
        first, second = 1 + here, 2 - here
        for index in range(16):
            a, b, c, d = (index & 1, (index >> 1) & 1, (index >> 2) & 1, index >> 3)
            z_at = plane ^ (a * first) ^ (b * second)
            g_at = rank ^ (c * second) ^ (d * first)
            place = (g_at * 4 + z_at) * 2 + here
            block = source[index * BLOCK : (index + 1) * BLOCK, :].astype(WIDE)
            for third in range(3):
                everyone[third, rows_at(place, BLOCK), :] = block[
                    :, third * 128 : (third + 1) * 128
                ]

    def line(at):
        parts = [everyone[third, pl.ds(at, 32, stride=BLOCK), :] for third in range(3)]
        return jnp.concatenate(parts, axis=1)

    def both(at, other):
        return jnp.concatenate([line(at), line(other)], axis=0)

    def own_lanes(values):
        chosen = values[:, :QUARTER]
        for place in range(1, 4):
            lanes = slice(place * QUARTER, (place + 1) * QUARTER)
            chosen = jnp.where(rank == place, values[:, lanes], chosen)
        return chosen

    cond = own_lanes(both(12, 13)).astype(LOW)
    sums = []
    for j in range(6):
        lanes = slice(j * D, (j + 1) * D)
        grads = both(j, 6 + j)
        sums.append(column_sum(grads))
        gradient = dot_first(cond, grads.astype(LOW))
        updated, momentum, variance = adam_update(
            weight[:, lanes].astype(WIDE),
            gradient,
            mean[:, lanes].astype(WIDE),
            square[:, lanes].astype(WIDE),
            LEARN_RATES[0],
            DECAY_FLAGS[0],
        )
        weight_out[:, lanes] = updated
        mean_out[:, lanes] = momentum
        square_out[:, lanes] = variance
    sums.append(near[16 * BLOCK :, :].astype(WIDE)[0:8] + far[16 * BLOCK :, :].astype(WIDE)[0:8])
    gradient = own_lanes(jnp.concatenate(sums, axis=0))
    updated, momentum, variance = adam_update(
        bias[...].astype(WIDE),
        gradient,
        bias_mean[...].astype(WIDE),
        bias_square[...].astype(WIDE),
        LEARN_RATES[5],
        DECAY_FLAGS[5],
    )
    bias_out[...] = updated
    bias_mean_out[...] = momentum
    bias_square_out[...] = variance
    mark[...] = jnp.zeros_like(mark)


def split_kernel(keep, arrived, stay, go):
    half = stay.shape[0]
    stay[...] = keep[:half].astype(WIDE) + arrived[:half].astype(WIDE)
    go[...] = (keep[half:].astype(WIDE) + arrived[half:].astype(WIDE)).astype(LOW)


def whole(shape):
    return pl.BlockSpec(shape, lambda *grid: (0,) * len(shape))


def by_slot(shape):
    return pl.BlockSpec((1,) + shape, lambda s: (s,) + (0,) * len(shape))


def shape_of(shape, dtype):
    return jax.ShapeDtypeStruct(shape, dtype)


SMEM_SPEC = pl.BlockSpec(memory_space=pltpu.SMEM)
PARAMS = pltpu.CompilerParams(vmem_limit_bytes=VMEM_BYTES)


ANY_SPEC = pl.BlockSpec(memory_space=pl.ANY)


def small_call(kernel, name, outs, where, *operands, scratch=(), after=(), params=PARAMS):
    return pl.pallas_call(
        kernel,
        grid=(1,),
        in_specs=[SMEM_SPEC]
        + [whole(item.shape) for item in operands]
        + [ANY_SPEC] * len(after),
        out_specs=[whole(shape) for shape, _ in outs],
        out_shape=[shape_of(*item) for item in outs],
        scratch_shapes=[pltpu.VMEM(*item) for item in scratch],
        compiler_params=params,
        name=name,
    )(where, *operands, *after)


def run_payload(*operands):
    outs = [((2 * QUARTER + 16, D), LOW), ((D, D), LOW)]
    return pl.pallas_call(
        payload_kernel,
        grid=(1,),
        in_specs=[whole(item.shape) for item in operands[:4]] + [ANY_SPEC] * 2,
        out_specs=[whole(shape) for shape, _ in outs],
        out_shape=[shape_of(*item) for item in outs],
        scratch_shapes=[pltpu.SemaphoreType.DMA],
        compiler_params=pltpu.CompilerParams(vmem_limit_bytes=60 * 1024 * 1024),
        name="own_payload",
    )(*operands)


def run_gate(value, *after, space=ANY_SPEC):
    return pl.pallas_call(
        gate_kernel,
        in_specs=[space] + [ANY_SPEC] * len(after),
        out_specs=space,
        out_shape=shape_of(value.shape, value.dtype),
        input_output_aliases={0: 0},
        compiler_params=pltpu.CompilerParams(vmem_limit_bytes=1024 * 1024),
        name="in_order",
    )(value, *after)


def run_relay(where, keep, arrived, passing):
    two = (2, keep.shape[1])
    return pl.pallas_call(
        relay_kernel,
        grid=(1,),
        in_specs=[SMEM_SPEC, whole(keep.shape), whole(arrived.shape), ANY_SPEC],
        out_specs=[whole(two), whole(two), ANY_SPEC],
        out_shape=[shape_of(two, WIDE)] * 2 + [shape_of(passing.shape, passing.dtype)],
        input_output_aliases={3: 2},
        compiler_params=PARAMS,
        name="relay",
    )(where, keep, arrived, passing)


def run_modulation(where, condition, biases, blocks, weight):
    message = pl.BlockSpec((16, D), lambda s: (2 * QUARTER // 16, 0))
    return pl.pallas_call(
        modulation_kernel,
        grid=(1,),
        in_specs=[SMEM_SPEC, whole((2, D)), whole((BIAS_ROWS, QUARTER))]
        + [message] * 3
        + [whole((QUARTER, 6 * D))],
        out_specs=[whole((4, 6 * D))] * 2 + [whole((16, D))],
        out_shape=[shape_of((4, 6 * D), WIDE)] * 2 + [shape_of((16, D), WIDE)],
        compiler_params=PARAMS,
        cost_estimate=pl.CostEstimate(flops=10**7, bytes_accessed=10**6, transcendentals=0),
        name="modulation_partials",
    )(where, condition, biases, *blocks, weight)


def run_attention_forward(where, tokens, stay, arrived, bias, own_att, own_proj, nears, fars):
    part = whole((2 * QUARTER + 16, D))
    return pl.pallas_call(
        attention_forward_kernel,
        grid=(2,),
        in_specs=[
            SMEM_SPEC,
            by_slot((SEQ, D)),
            whole((2, 6 * D)),
            whole((2, 6 * D)),
            whole((16, D)),
            whole((QUARTER, 3 * D)),
            whole((QUARTER, D)),
        ]
        + [part] * 6,
        out_specs=[
            by_slot((SEQ, 3 * D)),
            by_slot((HEADS, SEQ, SEQ)),
            by_slot((SEQ, D)),
            by_slot((6, D)),
            whole((D, 3 * D)),
            whole((D, D)),
        ],
        out_shape=[
            shape_of((2, SEQ, 3 * D), LOW),
            shape_of((2, HEADS, SEQ, SEQ), LOW),
            shape_of((2, SEQ, D), LOW),
            shape_of((2, 6, D), WIDE),
            shape_of((D, 3 * D), LOW),
            shape_of((D, D), LOW),
        ],
        compiler_params=PARAMS,
        cost_estimate=pl.CostEstimate(
            flops=3 * 10**9, bytes_accessed=6 * 10**6, transcendentals=10**6
        ),
        name="attention_forward",
    )(where, tokens, stay, arrived, bias, own_att, own_proj, *nears, *fars)


def run_feed(where, mixed, tokens, cotangent, mod, bias, proj, own_expand, own_contract, nears, fars):
    rows = 2 * SEQ

    return pl.pallas_call(
        feed_kernel,
        grid=(2,),
        in_specs=[SMEM_SPEC]
        + [whole((2, SEQ, D))] * 3
        + [whole((2, 6, D)), whole((16, D))]
        + [whole((D, D))] * 9,
        out_specs=[
            whole((2, SEQ, D)),
            whole((2, SEQ, D)),
            pl.BlockSpec((2, D, D), lambda i: (i, 0, 0)),
            pl.BlockSpec((2, D, D), lambda i: (i, 0, 0)),
            whole((16, D)),
        ],
        scratch_shapes=[
            pltpu.VMEM((2, D, 2 * D), LOW),
            pltpu.VMEM((2, 2 * D, D), LOW),
            pltpu.VMEM((rows, D), WIDE),
            pltpu.VMEM((rows, D), WIDE),
            pltpu.VMEM((rows, D), LOW),
            pltpu.VMEM((rows, D), WIDE),
            pltpu.VMEM((rows, 128), WIDE),
            pltpu.VMEM((rows, D), LOW),
            pltpu.VMEM((rows, D), WIDE),
            pltpu.VMEM((rows, D), WIDE),
        ],
        out_shape=[
            shape_of((2, SEQ, D), LOW),
            shape_of((2, SEQ, D), WIDE),
            shape_of((4, D, D), LOW),
            shape_of((4, D, D), LOW),
            shape_of((16, D), WIDE),
        ],
        compiler_params=PARAMS,
        cost_estimate=pl.CostEstimate(
            flops=8 * 10**9, bytes_accessed=10**7, transcendentals=10**6
        ),
        name="feed_forward_and_back",
    )(where, mixed, tokens, cotangent, mod, bias, proj, own_expand, own_contract, *nears, *fars)


def run_attention_backward(
    slot, where, tokens, grad_middle, joined, soft, mixed, mod, feed_rows, cond, att, proj, earlier=()
):
    def at_slot(shape):
        return pl.BlockSpec((1,) + shape, lambda i: (slot,) + (0,) * len(shape))

    passed = [((SEQ, 3 * D), LOW), ((SEQ, D), LOW), ((SEQ, D), LOW), ((SMALL, D), WIDE)]
    in_specs = [
        SMEM_SPEC,
        at_slot((SEQ, D)),
        at_slot((SEQ, D)),
        at_slot((SEQ, 3 * D)),
        at_slot((HEADS, SEQ, SEQ)),
        whole((2, SEQ, D)),
        at_slot((6, D)),
        whole((16, D)),
        whole((2, D)),
        whole((D, 3 * D)),
        whole((D, D)),
    ]
    out_specs = [at_slot((SEQ, D))]
    out_shape = [shape_of((2, SEQ, D), LOW)]
    scratch = []
    aliases = {}
    if slot == 0:
        out_specs += [whole(shape) for shape, _ in passed]
        out_shape += [shape_of(*item) for item in passed]
    else:
        in_specs += [whole(shape) for shape, _ in passed] + [ANY_SPEC, ANY_SPEC]
        aliases = {15: 0}
        out_specs += [whole((4, 2 * QUARTER, D))] * 2 + [whole((SMALL, D))]
        out_shape += [shape_of((4, 2 * QUARTER, D), LOW)] * 2 + [shape_of((SMALL, D), LOW)]
        sums = [((D, 3 * D), LOW), ((D, D), LOW)]
        scratch = [pltpu.VMEM(*item) for item in (passed[0], *sums, passed[3])]
    return pl.pallas_call(
        functools.partial(attention_backward_kernel, slot),
        grid=(1,),
        in_specs=in_specs,
        out_specs=out_specs,
        out_shape=out_shape,
        scratch_shapes=scratch,
        input_output_aliases=aliases,
        compiler_params=PARAMS,
        cost_estimate=pl.CostEstimate(
            flops=4 * 10**9, bytes_accessed=8 * 10**6, transcendentals=0
        ),
        name="attention_backward",
    )(where, tokens, grad_middle, joined, soft, mixed, mod, feed_rows, cond, att, proj, *earlier)


def turned(where):
    core = where[1]
    return (0, 2 - core), (1 + core, 3)


def turn_go_kernel(where, keep, arrived, go):
    for place, block in enumerate(turned(where)[1]):
        go[place] = (keep[block].astype(WIDE) + arrived[block].astype(WIDE)).astype(LOW)


def turn_stay_kernel(where, keep, swapped, arrived, stay, go):
    own, other = turned(where)[0]
    stay[...] = (
        keep[own].astype(WIDE) + swapped[own].astype(WIDE) + arrived[0].astype(WIDE)
    )
    go[...] = (
        keep[other].astype(WIDE) + swapped[other].astype(WIDE) + arrived[1].astype(WIDE)
    ).astype(LOW)


def run_split(keep, arrived):
    count, rest = keep.shape[0], keep.shape[1:]
    half = (count // 2,) + rest
    return pl.pallas_call(
        split_kernel,
        grid=(1,),
        in_specs=[whole(keep.shape)] * 2,
        out_specs=[whole(half)] * 2,
        out_shape=[shape_of(half, WIDE), shape_of(half, LOW)],
        compiler_params=PARAMS,
        name="sum_and_split",
    )(keep, arrived)


def swap_plane(value, which):
    pairs = [(r, r ^ ((1 + ((r + which) & 1)) << 1)) for r in range(lax.axis_size("replica"))]
    return lax.ppermute(value, "replica", pairs)


def swap_pair(value, which):
    groups, copies = lax.axis_size("group"), lax.axis_size("replica")
    pairs = []
    for g in range(groups):
        for r in range(copies):
            other = g ^ (1 if (r + which) % 2 == 0 else 2)
            pairs.append((g * copies + r, other * copies + r))
    return lax.ppermute(value, ("group", "replica"), pairs)


def gather_pair(value):
    first = swap_pair(value, 0)
    second = swap_pair(value, 1)
    return (first, second, swap_pair(first, 1))


def update_all(stored, gradients, means, squares, kinds):
    return [
        adam_update(
            stored[kind].astype(jnp.float32),
            gradient,
            means[kind].astype(jnp.float32),
            squares[kind].astype(jnp.float32),
            LEARN_RATES[kind],
            DECAY_FLAGS[kind],
        )
        for kind, gradient in zip(kinds, gradients)
    ]


def by_core(core, own, other):
    return (
        jnp.where(core == 0, own, other).astype(jnp.float32),
        jnp.where(core == 0, other, own).astype(jnp.float32),
    )


def attention_shards(totals):
    joined = jnp.concatenate(
        [totals[0][:QUARTER], totals[0][QUARTER:], totals[1][:QUARTER]], axis=1
    )
    return (joined, totals[1][QUARTER:])


def tail_in_step(
    where, copy, stages, condition, ffn_halves, att_parts, small_rows, stored, means, squares
):
    core = where[1]
    (feed_stay, feed_go), (att_send, att_keep) = ffn_halves, att_parts
    half, third = (D // 2, D), (2 * QUARTER, D)
    att_stay, att_go = run_split(att_keep, swap_replica(att_send, 1))
    att_stay, att_go, feed_stay, feed_go, small = small_call(
        step1_kernel, "step_1",
        [(third, WIDE), (third, LOW), (half, WIDE), (half, LOW), ((3 * BLOCK, D), LOW)],
        where, att_stay, swap_pair(att_go, 0), feed_stay, swap_pair(feed_go, 1),
        small_rows, swap_plane(small_rows, 0),
        scratch=[((D, D), WIDE)],
    )
    message, small = small_call(
        step2_kernel, "step_2",
        [((D, D), LOW), ((5 * BLOCK, D), LOW)],
        where, att_stay, swap_pair(att_go, 1), feed_stay, swap_plane(feed_go, 0),
        small, swap_plane(small, 1),
    )
    message, small = small_call(
        step3_kernel, "step_3",
        [((D, D), LOW), ((9 * BLOCK, D), LOW)],
        where, message, swap_plane(message, 1), small, swap_pair(small, 1),
    )
    att_part, feed_part, small, cond_keep, cond_go = small_call(
        step4_kernel, "step_4",
        [(third, LOW), ((D, D), LOW), ((17 * BLOCK, D), LOW), ((8, 128), WIDE), ((8, 128), WIDE)],
        where, message, swap_plane(message, 0), small, swap_pair(small, 0), stored[0],
    )
    shard = [((QUARTER, 6 * D), WIDE)] * 3 + [((BIAS_ROWS, QUARTER), WIDE)] * 3
    *updates, mark = small_call(
        modulation_update_kernel, "modulation_update", shard + [((8, 128), WIDE)],
        where, small, swap_replica(small, 1), stored[0], means[0], squares[0],
        stored[5], means[5], squares[5],
        scratch=[((3, 32 * BLOCK, 128), WIDE)],
    )
    feed_totals = by_core(core, feed_part, swap_replica(feed_part, 1))
    feed_updates = update_all(stored, feed_totals, means, squares, (3, 4))
    cond_in = swap_pair(cond_go, 0)
    cond_go = small_call(
        step5_kernel, "step_5", [((8, 128), WIDE)], where, cond_keep, cond_in, after=(mark,)
    )[0]
    cond_last = run_gate(swap_pair(cond_go, 1), feed_updates[0][1])
    att_totals = by_core(core, att_part, swap_replica(att_part, 1))
    blocks = [
        block[:, :QUARTER] for block in (cond_keep[:2], cond_in[:2], cond_last[:2], cond_last[2:4])
    ]
    owners = (where[0],) + neighbours(where)
    lanes = []
    for place in range(4):
        chosen = blocks[0]
        for k in range(1, 4):
            chosen = jnp.where(owners[k] == place, blocks[k], chosen)
        lanes.append(chosen)
    sigmoid_cond = jax.nn.sigmoid(condition)
    grad_condition = (
        jnp.concatenate(lanes, axis=1) * sigmoid_cond * (1.0 + condition * (1.0 - sigmoid_cond))
    )
    att_updates = update_all(stored, attention_shards(att_totals), means, squares, (1, 2))
    return grad_condition, [updates[:3]] + att_updates + feed_updates + [updates[3:]]


def tail_in_turn(
    where, copy, stages, condition, ffn_halves, att_parts, small_rows, stored, means, squares
):
    rank, core = where[0], where[1]
    slot_count, model_width = condition.shape
    modulation, cond_low = stored[0], jax.nn.silu(condition).astype(jnp.bfloat16)
    (ffn_stay, ffn_go), (att_send, att_keep) = ffn_halves, att_parts
    ffn_totals = reduce_replicas(
        wide_sum([ffn_stay, swap_pair(ffn_go, 1)]).astype(LOW), copy, stages
    )
    att_stay, att_go = run_split(att_keep, swap_replica(att_send, 1))
    att_stay, att_go = run_split(att_stay, swap_pair(att_go, 0))
    att_totals = reduce_replicas(
        wide_sum([att_stay[0], swap_pair(att_go[0], 1)]).astype(LOW), copy, stages
    )
    row_total = small_rows.shape[0]
    gathered = small_rows[None]
    for low_bit, radix in stages[1:]:
        digit = (copy >> low_bit) % radix
        gathered = in_order(
            [swap_replica(gathered, k << low_bit) for k in range(radix)], digit
        ).reshape(-1, row_total, model_width)
    gathered = in_order([swap_group(gathered, k) for k in range(4)], rank)
    own_plane = lax.dynamic_index_in_dim(gathered, copy >> 1, axis=1, keepdims=False)
    group_mod = own_plane[:, : 6 * slot_count].reshape(4 * slot_count, 6 * model_width)
    grad_cond_columns = dot_last(group_mod, modulation).reshape(4, slot_count, model_width // 4)
    cond_back = in_order(
        [swap_group(pick(grad_cond_columns, rank ^ k), k) for k in range(4)], rank
    )
    sigmoid_cond = jax.nn.sigmoid(condition)
    grad_condition = (
        jnp.swapaxes(cond_back, 0, 1).reshape(slot_count, model_width)
        * sigmoid_cond
        * (1.0 + condition * (1.0 - sigmoid_cond))
    )
    everyone = in_order([swap_replica(gathered, k) for k in range(2)], core).reshape(
        -1, row_total, model_width
    )
    all_mod = everyone[:, : 6 * slot_count].reshape(-1, 6 * model_width)
    all_cond = everyone[:, 6 * slot_count : 7 * slot_count].reshape(-1, model_width)
    cond_own = lax.dynamic_slice_in_dim(all_cond, rank * (model_width // 4), model_width // 4, 1)
    grad_mod = dot_first(cond_own, all_mod)
    mod_bias_grad = jnp.sum(all_mod, axis=0, dtype=jnp.float32).reshape(6, model_width)
    rest_bias_grad = jnp.sum(everyone[:, BLOCK : BLOCK + 8], axis=0, dtype=jnp.float32)
    bias_grad = lax.dynamic_slice_in_dim(
        jnp.concatenate([mod_bias_grad, rest_bias_grad], axis=0),
        rank * (model_width // 4),
        model_width // 4,
        1,
    )
    grad_att_own = jnp.concatenate(
        [att_totals[0][:QUARTER], att_totals[0][QUARTER:], att_totals[1][:QUARTER]], axis=1
    )
    totals = (
        grad_mod,
        grad_att_own,
        att_totals[1][QUARTER:],
        ffn_totals[0],
        ffn_totals[1],
        bias_grad,
    )
    return grad_condition, update_all(stored, totals, means, squares, range(6))


def shards(
    latents,
    condition,
    cotangent,
    live_counts,
    modulation,
    attending,
    projection,
    expand,
    contract,
    biases,
    modulation_mean,
    attending_mean,
    projection_mean,
    expand_mean,
    contract_mean,
    biases_mean,
    modulation_square,
    attending_square,
    projection_square,
    expand_square,
    contract_square,
    biases_square,
):
    slot_count, length, model_width = latents.shape
    rank = lax.axis_index("group")
    copy = lax.axis_index("replica")
    core = copy % 2
    stages = replica_stages(lax.axis_size("replica"))
    where = jnp.stack([rank, core, copy >> 1, live_counts[0]]).astype(jnp.int32)

    cond_low = jax.nn.silu(condition).astype(LOW)
    payload, feed_part = run_payload(
        condition, attending, projection, biases, expand, contract
    )
    first, second = swap_pair(payload, 0), swap_pair(payload, 1)
    last, first_far = swap_pair(first, 1), swap_replica(first, 1)
    feed_part = run_gate(
        feed_part, first_far, second, space=pl.BlockSpec(memory_space=pltpu.HBM)
    )
    nears = (first, second, last)
    fars = [first_far, swap_replica(second, 1), swap_replica(last, 1)]
    feed_first, feed_second = swap_pair(feed_part, 0), swap_pair(feed_part, 1)
    stay, go, bias = run_modulation(where, condition, biases, nears, modulation)
    stay, go, feed_first = run_relay(where, stay, swap_pair(go, 0), feed_first)
    arrived = swap_pair(go, 1)
    feed_last = swap_pair(feed_first, 1)
    joined, soft, mixed, mod, att, proj = run_attention_forward(
        where, latents, stay, arrived, bias, attending, projection, nears, fars
    )
    feed_nears = (feed_first, feed_second, run_gate(feed_last, mod))
    feed_fars = [swap_replica(item, 1) for item in feed_nears]
    out_latents, grad_middle, ffn_send, ffn_keep, feed_rows = run_feed(
        where, mixed, latents, cotangent, mod, bias, proj, expand, contract, feed_nears, feed_fars
    )
    cond_wide = cond_low.astype(WIDE)
    block = (model_width, model_width)
    ffn_other = swap_replica(ffn_send, 1)
    ffn_go = small_call(
        turn_go_kernel, "sum_to_send", [((2,) + block, LOW)], where, ffn_keep, ffn_other
    )[0]
    earlier = run_attention_backward(
        0, where, latents, grad_middle, joined, soft, mixed, mod, feed_rows, cond_wide, att, proj
    )
    ffn_in = swap_pair(ffn_go, 0)
    grad_latents, att_send, att_keep, small_rows = run_attention_backward(
        1, where, latents, grad_middle, joined, soft, mixed, mod, feed_rows, cond_wide, att, proj,
        (*earlier[1:], earlier[0], ffn_go),
    )
    ffn_halves = small_call(
        turn_stay_kernel, "sum_and_split", [(block, WIDE), (block, LOW)],
        where, ffn_keep, ffn_other, ffn_in,
    )
    tail = tail_in_step if lax.axis_size("replica") == 8 else tail_in_turn
    grad_condition, results = tail(
        where, copy, stages, condition, ffn_halves, (att_send, att_keep), small_rows,
        (modulation, attending, projection, expand, contract, biases),
        (
            modulation_mean, attending_mean, projection_mean,
            expand_mean, contract_mean, biases_mean,
        ),
        (
            modulation_square, attending_square, projection_square,
            expand_square, contract_square, biases_square,
        ),
    )
    return (
        out_latents,
        grad_latents,
        grad_condition,
        results[0][0],
        results[1][0],
        results[2][0],
        results[3][0],
        results[4][0],
        results[5][0],
        results[0][1],
        results[1][1],
        results[2][1],
        results[3][1],
        results[4][1],
        results[5][1],
        results[0][2],
        results[1][2],
        results[2][2],
        results[3][2],
        results[4][2],
        results[5][2],
    )


def solution(mesh):
    return jax.shard_map(
        shards,
        mesh=mesh,
        in_specs=(
            P(("group", "replica"), None, None),
            P(("group", "replica"), None),
            P(("group", "replica"), None, None),
            P(("group", "replica")),
            P("group", None),
            P("group", None),
            P("group", None),
            P(None, "group"),
            P("group", None),
            P(None, "group"),
            P("group", None),
            P("group", None),
            P("group", None),
            P(None, "group"),
            P("group", None),
            P(None, "group"),
            P("group", None),
            P("group", None),
            P("group", None),
            P(None, "group"),
            P("group", None),
            P(None, "group"),
        ),
        out_specs=(
            P(("group", "replica"), None, None),
            P(("group", "replica"), None, None),
            P(("group", "replica"), None),
            P("group", None),
            P("group", None),
            P("group", None),
            P(None, "group"),
            P("group", None),
            P(None, "group"),
            P("group", None),
            P("group", None),
            P("group", None),
            P(None, "group"),
            P("group", None),
            P(None, "group"),
            P("group", None),
            P("group", None),
            P("group", None),
            P(None, "group"),
            P("group", None),
            P(None, "group"),
        ),
        check_vma=False,
    )
```
